256 devices in a mesh: section: 16 (over z, core), seq: 16 (over y, x).
Axes of the slice: x: 4, y: 4, z: 8, core: 2. Of those that a mesh axis runs over, the one named last changes fastest.
Arguments:
- features: bfloat16 [1, 2048, 5120], P(None, 'seq'), may hold values from -6 to 6
- references: bfloat16 [32, 128, 5120], P('section'), may hold values from -6 to 6
- classifier: bfloat16 [32, 5120, 10], P('section', 'seq'), may hold values from -0.078125 to 0.078125
- lengths: int32 [1], replicated, may hold values from 1024 to 2048
- labels: int32 [1], replicated, may hold values from 0 to 9
Outputs:
- logits: float32 [1, 10], replicated
- grad_features: float32 [1, 2048, 5120], P(None, 'seq', 'section')
- grad_references: float32 [32, 128, 5120], P('section', None, 'seq')
The draws below stay inside these ranges and needn't reach their ends.
All inputs are finite; a program needn't handle non-finite values.
Results may differ from the reference program's by a relative error of at most 0.03.
Values may be sent and summed in bfloat16 or wider, within the bound.
No kernel may reach another device: no remote copies, remote signals or barrier semaphores. Data moves between devices by JAX's collectives and lax.ppermute only.
A program may use at most 64 MiB of HBM per device.

```python
import math
import jax
import jax.numpy as jnp
from jax import lax

D = 5120
H = 32
P_SIZE = 128
C = 10
ITERS = 3
B = 1
LEN = 2048


def level_of(key, dims, pieces, low, largest):
    loudness = 1.0
    for position, blocks in pieces:
        draws = jax.random.uniform(jax.random.fold_in(jax.random.fold_in(key, 6), position), (blocks,), jnp.float32, low / len(pieces), largest / len(pieces))
        loudness = loudness * jnp.repeat(jnp.exp(draws), dims[position] // blocks).reshape((-1,) + (1,) * (len(dims) - 1 - position))
    return loudness


def normal_values(key, extent, spread, limit, split=(), held_as=jnp.bfloat16):
    values = spread * jax.random.normal(key, extent, jnp.float32)
    if split:
        values = values * level_of(key, extent, split, -0.22, 0.18)
    return jnp.clip(values, -limit, limit).astype(held_as)


def setup_inputs(seed: int = 0) -> dict:
    arg_keys = jax.random.split(jax.random.key(seed), 6)
    return {
        "features": normal_values(arg_keys[0], (B, LEN, D), 1.0, 6.0, ((1, 16),)),
        "references": normal_values(arg_keys[1], (H, P_SIZE, D), 1.0, 6.0, ((0, 16),)),
        "classifier": normal_values(arg_keys[2], (H, D, C), D ** -0.5, 0.078125, ((0, 16), (1, 16))),
        "lengths": jax.random.randint(arg_keys[3], (B,), LEN // 2, LEN + 1).astype(jnp.int32),
        "labels": jax.random.randint(arg_keys[4], (B,), 0, C).astype(jnp.int32),
    }


temper = 1.5
epsilon = 1e-06
loss_scale = 65536.0
highest = lax.Precision.HIGHEST

def reference(features, references, classifier, lengths, labels):
    float_features = features.astype(jnp.float32)
    float_refs = references.astype(jnp.float32)
    weights = classifier.astype(jnp.float32)
    score_scale = temper / math.sqrt(D)
    scores = jnp.einsum('bnd,hpd->bnhp', float_features, float_refs, precision=highest) * score_scale
    kernel = jnp.exp(scores)
    positions = jnp.arange(LEN, dtype=jnp.int32)
    alive = (positions[None, :] < lengths[:, None]).astype(jnp.float32)
    masses = alive / lengths[:, None].astype(jnp.float32)
    col_scales = [jnp.ones((B, H, P_SIZE), jnp.float32)]
    row_scales = []
    row_totals = []
    for iteration in range(ITERS):
        row_total = jnp.einsum('bnhp,bhp->bnh', kernel, col_scales[-1], precision=highest)
        row_scale = masses[:, :, None] / row_total
        col_total = jnp.einsum('bnhp,bnh->bhp', kernel, row_scale, precision=highest)
        row_totals.append(row_total)
        row_scales.append(row_scale)
        col_scales.append(1.0 / (P_SIZE * col_total))
    row_scale = row_scales[-1]
    col_scale = col_scales[-1]
    plan_low = (row_scale[..., None] * kernel * col_scale[:, None]).astype(jnp.bfloat16)
    plan_float = plan_low.astype(jnp.float32)
    pooled_raw = float(P_SIZE) * jnp.einsum('bnd,bnhp->bhpd', float_features, plan_float, precision=highest)
    inverse_rms = lax.rsqrt(lax.optimization_barrier(jnp.mean(pooled_raw * pooled_raw, axis=3)) + epsilon)
    normed = pooled_raw * inverse_rms[..., None]
    pooled = lax.optimization_barrier(jnp.mean(normed, axis=2))
    logits = jnp.einsum('bhd,hdc->bc', pooled, weights, precision=highest)
    exps = jnp.exp(logits)
    probs = exps / lax.optimization_barrier(jnp.sum(exps, axis=1, keepdims=True))
    onehot = (labels[:, None] == jnp.arange(C, dtype=jnp.int32)[None, :]).astype(jnp.float32)
    grad_logits = loss_scale * (probs - onehot) / B
    grad_normed = jnp.einsum('bc,hdc->bhd', grad_logits, weights, precision=highest) / P_SIZE
    dual = lax.optimization_barrier(jnp.mean(grad_normed[:, :, None, :] * normed, axis=3))
    grad_raw = (inverse_rms[..., None] * (grad_normed[:, :, None, :] - normed * dual[..., None])).astype(jnp.bfloat16)
    grad_float = grad_raw.astype(jnp.float32)
    grad_plan = float(P_SIZE) * jnp.einsum('bnd,bhpd->bnhp', float_features, grad_float, precision=highest)
    grad_direct = float(P_SIZE) * jnp.einsum('bnhp,bhpd->bnd', plan_float, grad_float, precision=highest)
    weighted = grad_plan * kernel
    grad_row = jnp.einsum('bnhp,bhp->bnh', weighted, col_scale, precision=highest)
    grad_col = jnp.einsum('bnhp,bnh->bhp', weighted, row_scale, precision=highest)
    grad_kernel = row_scale[..., None] * col_scale[:, None] * grad_plan
    for iteration in reversed(range(ITERS)):
        grad_total = -float(P_SIZE) * col_scales[iteration + 1] ** 2 * grad_col
        grad_row = grad_row + jnp.einsum('bnhp,bhp->bnh', kernel, grad_total, precision=highest)
        grad_kernel = grad_kernel + row_scales[iteration][..., None] * grad_total[:, None]
        grad_rowsum = -grad_row * row_scales[iteration] / row_totals[iteration]
        grad_kernel = grad_kernel + grad_rowsum[..., None] * col_scales[iteration][:, None]
        if iteration > 0:
            grad_col = jnp.einsum('bnhp,bnh->bhp', kernel, grad_rowsum, precision=highest)
            grad_row = jnp.zeros_like(grad_row)
    grad_scores = (score_scale * grad_kernel * kernel).astype(jnp.bfloat16).astype(jnp.float32)
    grad_features = grad_direct + jnp.einsum('bnhp,hpd->bnd', grad_scores, float_refs, precision=highest)
    grad_references = jnp.einsum('bnhp,bnd->hpd', grad_scores, float_features, precision=highest)
    return (logits, grad_features, grad_references)
```

```python
import functools
import math

import jax
import jax.numpy as jnp
from jax import lax
from jax.experimental import pallas as pl
from jax.experimental.pallas import tpu as pltpu
from jax.sharding import Mesh, PartitionSpec as P

P_SIZE = 128
ITERS = 3
CLASSES = 10
PAD = 16

temper = 1.5
epsilon = 1e-06
loss_scale = 65536.0
f32 = jnp.float32
bf16 = jnp.bfloat16

SIDE = 4
DEPTH = 8
BLOCKS = SIDE * SIDE
ORDER = (0, 1, 3, 2)
VMEM = pl.BlockSpec(memory_space=pltpu.VMEM)
SMEM = pl.BlockSpec(memory_space=pltpu.SMEM)
NT = (((1,), (1,)), ((), ()))
TN = (((0,), (0,)), ((), ()))


def params():
    return pltpu.CompilerParams(vmem_limit_bytes=40 * 1024 * 1024)


def block_of(s):
    y = lax.rem(lax.axis_index("y") + ORDER[s // SIDE], SIDE)
    x = lax.rem(lax.axis_index("x") + ORDER[s % SIDE], SIDE)
    return y * SIDE + x


def shift(value, axis, size, step):
    return lax.ppermute(value, axis, [(i, (i - step) % size) for i in range(size)])


def gather(value):
    row = jnp.stack([value] + [shift(value, "x", SIDE, k) for k in ORDER[1:]])
    return [row] + [shift(row, "y", SIDE, k) for k in ORDER[1:]]


def split_kernel(f_ref, slices_ref, half_ref):
    core = lax.axis_index("core")
    rows, part = slices_ref.shape[1:]
    for j in range(DEPTH):
        pair = f_ref[:, 2 * part * j : 2 * part * (j + 1)]
        slices_ref[2 * j] = pair[:, :part]
        slices_ref[2 * j + 1] = pair[:, part:]
    start = pl.multiple_of(core * (rows // 2), rows // 2)
    for j in range(BLOCKS):
        half_ref[j] = slices_ref[j, pl.ds(start, rows // 2), :]


def scores_kernel(scale, f_ref, r_ref, k_ref):
    scores = lax.dot_general(r_ref[...], f_ref[...], NT, preferred_element_type=f32)
    k_ref[...] = jnp.exp(scores * scale).astype(bf16)


def forward_kernel(
    q0, q1, q2, q3, mine_ref, other_ref, wt_ref, len_ref, r_ref, rs_ref, rt_ref, col_ref, fc_ref, p0_ref, plan_ref
):
    q = (q0, q1, q2, q3)
    core = lax.axis_index("core")
    length = len_ref[0]
    rows = q0.shape[2]
    mass = 1.0 / (jnp.zeros((1, rows), jnp.int32) + length).astype(f32)
    lane = lax.broadcasted_iota(jnp.int32, (1, rows), 1)
    masses = [jnp.where(block_of(s) * rows + lane < length, mass, 0.0) for s in range(BLOCKS)]
    half = rows // 2
    for s in range(BLOCKS):
        where = block_of(s)
        fc_ref[pl.ds(pl.multiple_of(s * rows + core * half, half), half), :] = mine_ref[where]
        fc_ref[pl.ds(pl.multiple_of(s * rows + (1 - core) * half, half), half), :] = other_ref[where]
    for t in range(ITERS):
        for h in range(2):
            here = slice(h * P_SIZE, (h + 1) * P_SIZE)
            acc = jnp.zeros((P_SIZE, rows), f32)
            for s in range(BLOCKS):
                k = q[s // SIDE][s % SIDE, here, :].astype(f32)
                weighted = k if t == 0 else k * col_ref[t - 1, here, :]
                total = jnp.sum(weighted, axis=0, keepdims=True)
                scale = masses[s] / total
                place = (t * 2 + h) * BLOCKS + s
                rt_ref[place : place + 1, :] = total
                rs_ref[place : place + 1, :] = scale
                acc = acc + k * scale
            col = 1.0 / (float(P_SIZE) * jnp.sum(acc, axis=1, keepdims=True))
            col_ref[t, here, :] = jnp.broadcast_to(col, (P_SIZE, rows))
    for h in range(2):
        here = slice(h * P_SIZE, (h + 1) * P_SIZE)
        for s in range(BLOCKS):
            k = q[s // SIDE][s % SIDE, here, :].astype(f32)
            place = ((ITERS - 1) * 2 + h) * BLOCKS + s
            plan = (rs_ref[place : place + 1, :] * k * col_ref[ITERS - 1, here, :]).astype(bf16)
            plan_ref[here, s * rows : (s + 1) * rows] = plan
            if s == 0:
                p0_ref[here, :] = plan
    raw = jnp.dot(plan_ref[...], fc_ref[...], preferred_element_type=f32)
    r_ref[: 2 * P_SIZE, :] = (float(P_SIZE) * raw).astype(bf16)
    r_ref[2 * P_SIZE :, :] = wt_ref[...]


def pooled_kernel(width, r0, r1, r2, r3, f_ref, t_ref, m_ref, inv_ref, logit_ref):
    r = (r0, r1, r2, r3)
    heads = 2 * P_SIZE
    rows = f_ref.shape[1]
    acc = jnp.zeros((r0.shape[1], rows), f32)
    for s in range(BLOCKS):
        acc = acc + lax.dot_general(
            r[s // SIDE][s % SIDE], f_ref[block_of(s)], NT, preferred_element_type=f32
        )
    t_ref[:heads, :] = acc[:heads].astype(bf16)
    high = acc[heads:].astype(bf16)
    t_ref[heads : heads + 2 * PAD, :] = high
    t_ref[heads + 2 * PAD :, :] = (acc[heads:] - high.astype(f32)).astype(bf16)
    logits = jnp.zeros((1, PAD), f32)
    for h in range(2):
        here = slice(h * P_SIZE, (h + 1) * P_SIZE)
        squares = jnp.zeros((P_SIZE, 1), f32)
        m = jnp.zeros((P_SIZE, PAD), f32)
        for s in range(BLOCKS):
            block = r[s // SIDE][s % SIDE, here, :]
            weights = r[s // SIDE][s % SIDE, heads + h * PAD : heads + (h + 1) * PAD, :]
            m = m + lax.dot_general(block, weights, NT, preferred_element_type=f32)
            wide = block.astype(f32)
            squares = squares + jnp.sum(wide * wide, axis=1, keepdims=True)
        inverse = lax.rsqrt(squares / width + epsilon)
        m_ref[here, :] = m
        inv_ref[here, :] = jnp.broadcast_to(inverse, (P_SIZE, inv_ref.shape[1]))
        logits = logits + jnp.sum(inverse * m, axis=0, keepdims=True) / P_SIZE
    logit_ref[...] = logits


def class_grads(logits, label):
    lane = lax.broadcasted_iota(jnp.int32, logits.shape, 1)
    exps = jnp.where(lane < CLASSES, jnp.exp(logits), 0.0)
    probs = exps / jnp.sum(exps, axis=1, keepdims=True)
    grads = loss_scale * (probs - (lane == label).astype(f32))
    square = (PAD, PAD)
    diagonal = lax.broadcasted_iota(jnp.int32, square, 0) == lax.broadcasted_iota(jnp.int32, square, 1)
    column = jnp.sum(jnp.where(diagonal, grads, 0.0), axis=1, keepdims=True)
    return grads, column


def raw_kernel(width, r0, r1, r2, r3, m_ref, inv_ref, logit_ref, label_ref, out_ref):
    r = (r0, r1, r2, r3)
    heads = 2 * P_SIZE
    grads, column = class_grads(logit_ref[...], label_ref[0])
    for h in range(2):
        here = slice(h * P_SIZE, (h + 1) * P_SIZE)
        inverse = inv_ref[here, :1]
        dual = inverse * jnp.sum(grads * m_ref[here, :], axis=1, keepdims=True) / (P_SIZE * width)
        for s in range(BLOCKS):
            block = r[s // SIDE][s % SIDE, here, :].astype(f32)
            weights = r[s // SIDE][s % SIDE, heads + h * PAD : heads + (h + 1) * PAD, :].astype(f32)
            normed = jnp.sum(column * weights, axis=0, keepdims=True) / P_SIZE
            out_ref[block_of(s), here, :] = (inverse * (normed - block * (inverse * dual))).astype(bf16)


def backward_kernel(
    width, score_scale,
    q0, q1, q2, q3, t0, t1, t2, t3, rs_ref, rt_ref, col_ref, m_ref, inv_ref, logit_ref, label_ref,
    gs_ref, gs0_ref, gt_ref, grs_ref, u_ref,
):
    q = (q0, q1, q2, q3)
    tt = (t0, t1, t2, t3)
    heads = 2 * P_SIZE
    rows = q0.shape[2]
    size = float(P_SIZE)
    grads, column = class_grads(logit_ref[...], label_ref[0])
    for h in range(2):
        here = slice(h * P_SIZE, (h + 1) * P_SIZE)
        inverse = inv_ref[here, :]
        dual = inverse * (jnp.sum(grads * m_ref[here, :], axis=1, keepdims=True) / (size * width))
        first = size * inverse
        second = first * inverse * dual

        def load(s):
            return q[s // SIDE][s % SIDE, here, :].astype(f32)

        def grad_plan(s, u):
            return first * u - second * tt[s // SIDE][s % SIDE, here, :].astype(f32)

        def row(ref, t, s):
            place = (t * 2 + h) * BLOCKS + s
            return ref[place : place + 1, :]

        def put(ref, t, s, value):
            place = (t * 2 + h) * BLOCKS + s
            ref[place : place + 1, :] = value

        acc = jnp.zeros((P_SIZE, rows), f32)
        for s in range(BLOCKS):
            low = heads + h * PAD
            v = tt[s // SIDE][s % SIDE, low : low + PAD, :].astype(f32)
            v = v + tt[s // SIDE][s % SIDE, low + 2 * PAD : low + 3 * PAD, :].astype(f32)
            u = jnp.sum(column * v, axis=0, keepdims=True) / size
            put(u_ref, 0, s, u)
            weighted = grad_plan(s, u) * load(s)
            put(grs_ref, ITERS - 1, s, jnp.sum(weighted * col_ref[ITERS - 1, here, :], axis=0, keepdims=True))
            acc = acc + weighted * row(rs_ref, ITERS - 1, s)
        for t in reversed(range(ITERS)):
            grad_col = jnp.sum(acc, axis=1, keepdims=True)
            grad_total = -size * col_ref[t, here, :] ** 2 * grad_col
            gt_ref[t] = grad_total
            acc = jnp.zeros((P_SIZE, rows), f32)
            for s in range(BLOCKS):
                k = load(s)
                grad_row = jnp.sum(k * gt_ref[t], axis=0, keepdims=True)
                if t == ITERS - 1:
                    grad_row = grad_row + row(grs_ref, t, s)
                grad_rowsum = -grad_row * row(rs_ref, t, s) / row(rt_ref, t, s)
                put(grs_ref, t, s, grad_rowsum)
                if t > 0:
                    acc = acc + k * grad_rowsum
        for s in range(BLOCKS):
            total = row(rs_ref, ITERS - 1, s) * col_ref[ITERS - 1, here, :] * grad_plan(s, row(u_ref, 0, s))
            for t in range(ITERS):
                total = total + row(rs_ref, t, s) * gt_ref[t]
                if t > 0:
                    total = total + row(grs_ref, t, s) * col_ref[t - 1, here, :]
                else:
                    total = total + row(grs_ref, t, s)
            value = (score_scale * total * load(s)).astype(bf16)
            gs_ref[here, s * rows : (s + 1) * rows] = value
            if s == 0:
                gs0_ref[here, :] = value


def features_kernel(p0_ref, gs_ref, refs_ref, raw_ref, out_ref):
    j = pl.program_id(0)
    core = lax.axis_index("core")
    z = lax.axis_index("z")
    part = raw_ref.shape[2]
    pair = lax.dot_general(gs_ref[...], refs_ref[...], TN, preferred_element_type=f32)
    place = 2 * lax.rem(j // 2 + 4 - z // 2, 4) + lax.rem(j + z, 2)
    for side in range(2):
        direct = lax.dot_general(p0_ref[...], raw_ref[side], TN, preferred_element_type=f32)
        value = pair[:, side * part : (side + 1) * part] + float(P_SIZE) * direct
        out_ref[lax.rem(core + side, 2), place] = value.astype(bf16)


def reduce_sections(parts):
    other = lax.ppermute(parts[1], "core", [(0, 1), (1, 0)])
    both = (parts[0].astype(f32) + other.astype(f32)).astype(bf16)
    total = both[:2].astype(f32)
    for k in (2, 3, 1):
        total = total + shift(both[2 * k : 2 * k + 2], "z", DEPTH, -2 * k).astype(f32)
    away = lax.ppermute(total[1].astype(bf16), "z", [(i, i ^ 1) for i in range(DEPTH)])
    return total[0] + away.astype(f32)


def sum_logits(part):
    total = part + lax.ppermute(part, "core", [(0, 1), (1, 0)])
    for k in (1, 2, 4):
        total = total + lax.ppermute(total, "z", [(i, i ^ k) for i in range(DEPTH)])
    return total


def local(features, references, classifier, lengths, labels):
    batch, rows, width = features.shape
    heads = references.shape[0] * P_SIZE
    part = width // BLOCKS
    score_scale = temper / math.sqrt(width)
    feats = features.reshape(rows, width)
    refs = references.reshape(heads, width)
    kind = jax.ShapeDtypeStruct

    slices, half = pl.pallas_call(
        split_kernel,
        out_shape=[kind((BLOCKS, rows, part), bf16), kind((BLOCKS, rows // 2, part), bf16)],
        in_specs=[VMEM], out_specs=[VMEM, VMEM], compiler_params=params(), name="split",
    )(feats)
    kernel = pl.pallas_call(
        functools.partial(scores_kernel, score_scale),
        out_shape=kind((heads, rows), bf16),
        in_specs=[VMEM, VMEM], out_specs=VMEM, compiler_params=params(), name="scores",
    )(feats, refs)
    mine = lax.all_to_all(half, ("y", "x"), 0, 0)
    other = lax.ppermute(mine, "core", [(0, 1), (1, 0)])
    weights = jnp.pad(jnp.transpose(classifier, (0, 2, 1)), ((0, 0), (0, PAD - CLASSES), (0, 0)))
    weights = weights.reshape(2 * PAD, part)
    q = gather(kernel)
    raw, rs, rt, col, cols, p0 = pl.pallas_call(
        forward_kernel,
        out_shape=[
            kind((heads + 2 * PAD, part), bf16),
            kind((ITERS * 2 * BLOCKS, rows), f32),
            kind((ITERS * 2 * BLOCKS, rows), f32),
            kind((ITERS, heads, rows), f32),
            kind((BLOCKS * rows, part), bf16),
            kind((heads, rows), bf16),
        ],
        in_specs=[VMEM] * 7 + [SMEM], out_specs=[VMEM] * 6,
        scratch_shapes=[pltpu.VMEM((heads, BLOCKS * rows), bf16)],
        compiler_params=params(), name="forward",
    )(*q, mine, other, weights, lengths)
    r = gather(raw)
    t, m, inverse, logit_part = pl.pallas_call(
        functools.partial(pooled_kernel, width),
        out_shape=[
            kind((heads + 4 * PAD, rows), bf16),
            kind((heads, PAD), f32),
            kind((heads, rows), f32),
            kind((1, PAD), f32),
        ],
        in_specs=[VMEM] * 5, out_specs=[VMEM] * 4, compiler_params=params(), name="pooled",
    )(*r, slices)
    logits = sum_logits(logit_part)
    ts = gather(t)
    grad_raw = pl.pallas_call(
        functools.partial(raw_kernel, width),
        out_shape=kind((BLOCKS, heads, part), bf16),
        in_specs=[VMEM] * 7 + [SMEM], out_specs=VMEM, compiler_params=params(), name="grad_raw",
    )(*r, m, inverse, logits, labels)
    grad_scores, gs0 = pl.pallas_call(
        functools.partial(backward_kernel, width, score_scale),
        out_shape=[kind((heads, BLOCKS * rows), bf16), kind((heads, rows), bf16)],
        in_specs=[VMEM] * 14 + [SMEM], out_specs=[VMEM, VMEM],
        scratch_shapes=[
            pltpu.VMEM((ITERS, P_SIZE, rows), f32),
            pltpu.VMEM((ITERS * 2 * BLOCKS, rows), f32),
            pltpu.VMEM((2 * BLOCKS, rows), f32),
        ],
        compiler_params=params(), name="backward",
    )(*q, *ts, rs, rt, col, m, inverse, logits, labels)
    parts = pl.pallas_call(
        features_kernel,
        grid=(DEPTH,),
        out_shape=kind((2, DEPTH, rows, part), bf16),
        in_specs=[
            pl.BlockSpec((heads, rows), lambda j: (0, 0)),
            pl.BlockSpec((heads, rows), lambda j: (0, 0)),
            pl.BlockSpec((heads, 2 * part), lambda j: (0, j)),
            pl.BlockSpec((2, heads, part), lambda j: (j, 0, 0)),
        ],
        out_specs=pl.BlockSpec((2, DEPTH, rows, part), lambda j: (0, 0, 0, 0)),
        compiler_params=params(), name="features",
    )(p0, gs0, refs, grad_raw)
    grad_features = reduce_sections(parts)
    grad_references = jnp.dot(grad_scores, cols, preferred_element_type=f32)
    return (
        logits[:, :CLASSES],
        grad_features.reshape(batch, rows, part),
        grad_references.reshape(references.shape[0], P_SIZE, part),
    )


def solution(mesh):
    grid = Mesh(mesh.devices.reshape(DEPTH, 2, SIDE, SIDE), ("z", "core", "y", "x"))
    section, seq = ("z", "core"), ("y", "x")
    in_specs = (P(None, seq, None), P(section, None, None), P(section, seq, None), P(), P())
    out_specs = (P(), P(None, seq, section), P(section, None, seq))
    return jax.shard_map(local, mesh=grid, in_specs=in_specs, out_specs=out_specs, check_vma=False)
```

```python
import functools
import math

import jax
import jax.numpy as jnp
from jax import lax
from jax.experimental import pallas as pl
from jax.experimental.pallas import tpu as pltpu
from jax.sharding import Mesh, PartitionSpec as P

P_SIZE = 128
ITERS = 3
CLASSES = 10
PAD = 16
HEADS = 2
REFS = HEADS * P_SIZE

temper = 1.5
epsilon = 1e-06
loss_scale = 65536.0
f32 = jnp.float32
bf16 = jnp.bfloat16

SIDE = 4
DEPTH = 8
BLOCKS = SIDE * SIDE
FAR = ((0, 0), (2, 0), (0, 2), (2, 2))
NEAR = ((0, 0), (1, 0), (0, 1), (3, 3))
CHIPS = ((0, 1, 7, 2), (0, 1, 7, 6))
T_ROWS = REFS + HEADS * PAD
M_ROWS = 4 * PAD
VMEM = pl.BlockSpec(memory_space=pltpu.VMEM)
SMEM = pl.BlockSpec(memory_space=pltpu.SMEM)
NT = (((1,), (1,)), ((), ()))
TN = (((0,), (0,)), ((), ()))


def call(kernel, name, shapes, n_vmem, n_smem=0, scratch=(), flops=0):
    many = isinstance(shapes, list)
    return pl.pallas_call(
        kernel,
        out_shape=shapes,
        in_specs=[VMEM] * n_vmem + [SMEM] * n_smem,
        out_specs=[VMEM] * len(shapes) if many else VMEM,
        scratch_shapes=list(scratch),
        compiler_params=pltpu.CompilerParams(vmem_limit_bytes=40 * 1024 * 1024),
        cost_estimate=pl.CostEstimate(flops=flops, bytes_accessed=1 << 20, transcendentals=0) if flops else None,
        name=name,
    )


def moved(first, second):
    y = lax.rem(lax.axis_index("y") + first[0] + second[0], SIDE)
    x = lax.rem(lax.axis_index("x") + first[1] + second[1], SIDE)
    return y * SIDE + x


def block_of(s):
    return moved(NEAR[s // 4], FAR[s % 4])


def lanes(block, rows):
    return pl.ds(pl.multiple_of(block * rows, rows), rows)


def send(value, step, sign=1):
    pairs = []
    for y in range(SIDE):
        for x in range(SIDE):
            to = (y + sign * step[0]) % SIDE * SIDE + (x + sign * step[1]) % SIDE
            pairs.append((y * SIDE + x, to))
    return lax.ppermute(value, ("y", "x"), pairs)


def gather(value):
    row = jnp.stack([value] + [send(value, step, -1) for step in FAR[1:]])
    return [row] + [send(row, step, -1) for step in NEAR[1:]]


def scores_kernel(scale, f_ref, r_ref, k_ref):
    scores = lax.dot_general(r_ref[...], f_ref[...], NT, preferred_element_type=f32)
    k_ref[...] = jnp.exp(scores * scale).astype(bf16)


def split_kernel(f_ref, refs_ref, half_ref, mine_ref, turned_ref):
    part = mine_ref.shape[1]
    half = part // 2
    for j in range(BLOCKS // 2):
        where = slice(2 * part * j, 2 * part * (j + 1))
        turned_ref[where, :] = jnp.transpose(f_ref[:, where])
    core = lax.axis_index("core")
    for j in range(BLOCKS):
        half_ref[j] = turned_ref[pl.ds(pl.multiple_of(part * j + half * core, half), half), :]
    place = moved((0, 0), (0, 0))
    pair = refs_ref[:, pl.ds(pl.multiple_of((place // 2) * (2 * part), 2 * part), 2 * part)]
    mine_ref[...] = jnp.where(lax.rem(place, 2) == 0, pair[:, :part], pair[:, part:])


def diagonal():
    square = (P_SIZE, P_SIZE)
    return lax.broadcasted_iota(jnp.int32, square, 0) == lax.broadcasted_iota(jnp.int32, square, 1)


def to_row(column):
    return jnp.sum(jnp.where(diagonal(), column, 0.0), axis=0, keepdims=True)


def to_column(row):
    return jnp.sum(jnp.where(diagonal(), row, 0.0), axis=1, keepdims=True)


def put_moments(ref, row, moments):
    for h in range(HEADS):
        high = moments[h].astype(bf16)
        ref[row + h * PAD : row + (h + 1) * PAD, :] = high
        low = row + (HEADS + h) * PAD
        ref[low : low + PAD, :] = (moments[h] - high.astype(f32)).astype(bf16)


def add_moments(refs, row):
    moments = []
    for h in range(HEADS):
        total = jnp.zeros((PAD, P_SIZE), f32)
        for ref in refs:
            total = total + ref[row + h * PAD : row + (h + 1) * PAD, :].astype(f32)
            low = row + (HEADS + h) * PAD
            total = total + ref[low : low + PAD, :].astype(f32)
        moments.append(total)
    return moments


def forward_kernel(
    q0, q1, q2, q3, near_ref, other_ref, wt_ref, len_ref,
    a0, a1, a2, a3, raw_ref, rs_ref, rt_ref, col_ref, fc_ref, plan_ref, wide_ref, ext_ref,
):
    q = (q0, q1, q2, q3)
    core = lax.axis_index("core")
    length = len_ref[0]
    rows = q0.shape[2]
    half = near_ref.shape[1]
    mass = 1.0 / (jnp.zeros((1, rows), jnp.int32) + length).astype(f32)
    lane = lax.broadcasted_iota(jnp.int32, (1, rows), 1)
    masses = [jnp.where(block_of(s) * rows + lane < length, mass, 0.0) for s in range(BLOCKS)]
    for s in range(BLOCKS):
        here = slice(s * rows, (s + 1) * rows)
        fc_ref[pl.ds(pl.multiple_of(core * half, half), half), here] = near_ref[s]
        fc_ref[pl.ds(pl.multiple_of((1 - core) * half, half), half), here] = other_ref[s]
    for t in range(ITERS):
        for h in range(HEADS):
            here = slice(h * P_SIZE, (h + 1) * P_SIZE)
            acc = jnp.zeros((P_SIZE, rows), f32)
            for s in range(BLOCKS):
                k = q[s // 4][s % 4, here, :].astype(f32)
                weighted = k if t == 0 else k * col_ref[t - 1, here, :]
                total = jnp.sum(weighted, axis=0, keepdims=True)
                scale = masses[s] / total
                place = (t * HEADS + h) * BLOCKS + s
                rt_ref[place : place + 1, :] = total
                rs_ref[place : place + 1, :] = scale
                acc = acc + k * scale
            col = 1.0 / (float(P_SIZE) * jnp.sum(acc, axis=1, keepdims=True))
            col_ref[t, here, :] = jnp.broadcast_to(col, (P_SIZE, rows))
    for h in range(HEADS):
        here = slice(h * P_SIZE, (h + 1) * P_SIZE)
        for s in range(BLOCKS):
            k = q[s // 4][s % 4, here, :].astype(f32)
            place = ((ITERS - 1) * HEADS + h) * BLOCKS + s
            plan = rs_ref[place : place + 1, :] * k * col_ref[ITERS - 1, here, :]
            plan_ref[here, lanes(block_of(s), rows)] = plan.astype(bf16)
    raw = float(P_SIZE) * lax.dot_general(plan_ref[...], fc_ref[...], NT, preferred_element_type=f32)
    raw_ref[...] = raw
    ext_ref[:REFS, :] = raw.astype(bf16)
    ext_ref[REFS:, :] = wt_ref[...]
    wide_ref[...] = jnp.dot(ext_ref[...], fc_ref[...], preferred_element_type=f32).astype(bf16)
    moments = []
    for h in range(HEADS):
        here = slice(h * P_SIZE, (h + 1) * P_SIZE)
        squares = jnp.sum(raw_ref[here, :] * raw_ref[here, :], axis=1, keepdims=True)
        products = lax.dot_general(
            wt_ref[h * PAD : (h + 1) * PAD, :], ext_ref[here, :], NT, preferred_element_type=f32
        )
        kind = lax.broadcasted_iota(jnp.int32, products.shape, 0)
        moments.append(jnp.where(kind == CLASSES, to_row(squares), products))
    for i, out in enumerate((a0, a1, a2, a3)):
        for k in range(4):
            out[k * T_ROWS : (k + 1) * T_ROWS, :] = wide_ref[:, lanes(moved(NEAR[i], FAR[k]), rows)]
        put_moments(out, 4 * T_ROWS, moments)


def add_blocks(refs, rows):
    total = refs[0][rows, :].astype(f32)
    for ref in refs[1:]:
        total = total + ref[rows, :].astype(f32)
    return total.astype(bf16)


def first_sum_kernel(a0, a1, a2, a3, c0, c1, c2, c3):
    parts = (a0, a1, a2, a3)
    moments = add_moments(parts, 4 * T_ROWS)
    for k, out in enumerate((c0, c1, c2, c3)):
        for low in range(0, T_ROWS, 96):
            out[low : low + 96, :] = add_blocks(parts, slice(k * T_ROWS + low, k * T_ROWS + low + 96))
        put_moments(out, T_ROWS, moments)


def inverse_rms(moments, width):
    return lax.rsqrt(moments[CLASSES : CLASSES + 1, :] / width + epsilon)


def second_sum_kernel(width, c0, c1, c2, c3, t_ref, m_ref, logit_ref):
    parts = (c0, c1, c2, c3)
    moments = add_moments(parts, T_ROWS)
    logits = jnp.zeros((PAD, 1), f32)
    for h in range(HEADS):
        m_ref[h * PAD : (h + 1) * PAD, :] = moments[h]
        part = jnp.sum(inverse_rms(moments[h], width) * moments[h], axis=1, keepdims=True)
        logits = logits + part / P_SIZE
    logit_ref[...] = jnp.broadcast_to(logits, logit_ref.shape)
    for low in range(0, T_ROWS, 96):
        t_ref[low : low + 96, :] = add_blocks(parts, slice(low, low + 96))


def backward_kernel(
    width, score_scale,
    q0, q1, q2, q3, t0, t1, t2, t3, rs_ref, rt_ref, col_ref, m_ref, logit_ref, raw_ref, wt_ref, plan_ref, refs_ref, label_ref,
    gs_ref, p0, p1, p2, p3, other_ref, gt_ref, grs_ref, u_ref, left_ref, right_ref, wide_ref,
):
    q = (q0, q1, q2, q3)
    tt = (t0, t1, t2, t3)
    rows = q0.shape[2]
    size = float(P_SIZE)
    logits = logit_ref[...]
    kind = lax.broadcasted_iota(jnp.int32, logits.shape, 0)
    exps = jnp.where(kind < CLASSES, jnp.exp(logits), 0.0)
    probs = exps / jnp.sum(exps, axis=0, keepdims=True)
    grads = loss_scale * (probs - (kind == label_ref[0]).astype(f32))
    grads = jnp.where(kind < CLASSES, grads, 0.0)
    left_ref[:REFS, :] = refs_ref[...]
    right_ref[REFS:, :] = plan_ref[...]
    for h in range(HEADS):
        here = slice(h * P_SIZE, (h + 1) * P_SIZE)
        moments = m_ref[h * PAD : (h + 1) * PAD, :]
        inverse_row = inverse_rms(moments, width)
        dual_row = inverse_row * jnp.sum(grads * moments, axis=0, keepdims=True) / (size * width)
        inverse = to_column(inverse_row)
        pull = to_column(inverse_row * dual_row)
        normed = jnp.sum(grads[:, :1] * wt_ref[h * PAD : (h + 1) * PAD, :].astype(f32), axis=0, keepdims=True) / size
        grad_raw = (inverse * (normed - raw_ref[here, :] * pull)).astype(bf16)
        left_ref[REFS + h * P_SIZE : REFS + (h + 1) * P_SIZE, :] = (size * grad_raw.astype(f32)).astype(bf16)
        first = jnp.broadcast_to(size * inverse, (P_SIZE, rows))
        second = first * pull

        def load(s):
            return q[s // 4][s % 4, here, :].astype(f32)

        def grad_plan(s, u):
            return first * u - second * tt[s // 4][s % 4, here, :].astype(f32)

        def row(ref, t, s):
            place = (t * HEADS + h) * BLOCKS + s
            return ref[place : place + 1, :]

        def put(ref, t, s, value):
            place = (t * HEADS + h) * BLOCKS + s
            ref[place : place + 1, :] = value

        acc = jnp.zeros((P_SIZE, rows), f32)
        for s in range(BLOCKS):
            low = REFS + h * PAD
            v = tt[s // 4][s % 4, low : low + PAD, :].astype(f32)
            u = jnp.sum(grads * v, axis=0, keepdims=True) / size
            put(u_ref, 0, s, u)
            weighted = grad_plan(s, u) * load(s)
            put(grs_ref, ITERS - 1, s, jnp.sum(weighted * col_ref[ITERS - 1, here, :], axis=0, keepdims=True))
            acc = acc + weighted * row(rs_ref, ITERS - 1, s)
        for t in reversed(range(ITERS)):
            grad_col = jnp.sum(acc, axis=1, keepdims=True)
            gt_ref[t] = -size * col_ref[t, here, :] ** 2 * grad_col
            acc = jnp.zeros((P_SIZE, rows), f32)
            for s in range(BLOCKS):
                k = load(s)
                grad_row = jnp.sum(k * gt_ref[t], axis=0, keepdims=True)
                if t == ITERS - 1:
                    grad_row = grad_row + row(grs_ref, t, s)
                grad_rowsum = -grad_row * row(rs_ref, t, s) / row(rt_ref, t, s)
                put(grs_ref, t, s, grad_rowsum)
                if t > 0:
                    acc = acc + k * grad_rowsum
        for s in range(BLOCKS):
            total = row(rs_ref, ITERS - 1, s) * col_ref[ITERS - 1, here, :] * grad_plan(s, row(u_ref, 0, s))
            for t in range(ITERS):
                total = total + row(rs_ref, t, s) * gt_ref[t]
                if t > 0:
                    total = total + row(grs_ref, t, s) * col_ref[t - 1, here, :]
                else:
                    total = total + row(grs_ref, t, s)
            right_ref[here, lanes(block_of(s), rows)] = (score_scale * total * load(s)).astype(bf16)
    gs_ref[...] = right_ref[:REFS, :]
    wide_ref[...] = lax.dot_general(left_ref[...], right_ref[...], TN, preferred_element_type=f32)
    core, z = lax.axis_index("core"), lax.axis_index("z")
    outs = (p0, p1, p2, p3)

    def take(step, which):
        return wide_ref[:, lanes(2 * lax.rem(z + step, DEPTH) + which, rows)].astype(bf16)

    for k in range(4):
        for b in range(2):
            step = jnp.where(core == 0, CHIPS[0][k], CHIPS[1][k]) + 4 * b
            outs[k][b] = take(step, core)
            step = jnp.where(core == 0, CHIPS[1][k], CHIPS[0][k]) + 4 * b
            other_ref[2 * k + b] = take(step, 1 - core)


def cores_kernel(p0, p1, p2, p3, other_ref, o0, o1, o2, o3):
    for k, (part, out) in enumerate(zip((p0, p1, p2, p3), (o0, o1, o2, o3))):
        for b in range(2):
            out[b] = (part[b].astype(f32) + other_ref[2 * k + b].astype(f32)).astype(bf16)


def chips_kernel(o0, o1, o2, o3, u0, u1):
    for b, out in enumerate((u0, u1)):
        total = o0[b].astype(f32) + o1[b].astype(f32) + o2[b].astype(f32) + o3[b].astype(f32)
        out[...] = total.astype(bf16)


def last_kernel(u0, u1, out_ref):
    eye = diagonal().astype(bf16)
    out_ref[...] = lax.dot_general(eye, u0[...], NT, preferred_element_type=f32) + lax.dot_general(
        eye, u1[...], NT, preferred_element_type=f32
    )


def references_kernel(gs_ref, fc_ref, out_ref):
    out_ref[...] = lax.dot_general(gs_ref[...], fc_ref[...], NT, preferred_element_type=f32)


def along_z(value, k):
    pairs = []
    for z in range(DEPTH):
        for core in range(2):
            pairs.append((2 * z + core, 2 * ((z + CHIPS[core][k]) % DEPTH) + core))
    return lax.ppermute(value, ("z", "core"), pairs)


def to_place(value, b):
    pairs = []
    for z in range(DEPTH):
        for core in range(2):
            for j in range(BLOCKS):
                block = 2 * ((z + 4 * b) % DEPTH) + core
                pairs.append(((2 * z + core) * BLOCKS + j, j * BLOCKS + block))
    return lax.ppermute(value, ("z", "core", "y", "x"), pairs)


def sum_logits(part):
    total = part + lax.ppermute(part, "core", [(0, 1), (1, 0)])
    for k in (1, 2, 4):
        total = total + lax.ppermute(total, "z", [(i, i ^ k) for i in range(DEPTH)])
    return total


def local(features, references, classifier, lengths, labels):
    batch, rows, width = features.shape
    part = width // BLOCKS
    everything = BLOCKS * rows
    score_scale = temper / math.sqrt(width)
    feats = features.reshape(rows, width)
    refs = references.reshape(REFS, width)
    kind = jax.ShapeDtypeStruct

    kernel = call(functools.partial(scores_kernel, score_scale), "scores", kind((REFS, rows), bf16), 2)(feats, refs)
    q = gather(kernel)
    half, refs_part = call(
        split_kernel, "split", [kind((BLOCKS, part // 2, rows), bf16), kind((REFS, part), bf16)], 2,
        scratch=[pltpu.VMEM((width, rows), bf16)],
    )(feats, refs)
    half = lax.optimization_barrier((half, q[0]))[0]
    near = lax.all_to_all(half, ("y", "x"), 0, 0)
    other = lax.ppermute(near, "core", [(0, 1), (1, 0)])
    weights = jnp.pad(jnp.transpose(classifier, (0, 2, 1)), ((0, 0), (0, PAD - CLASSES), (0, 0)))
    weights = weights.reshape(HEADS * PAD, part)

    scales = kind((ITERS * HEADS * BLOCKS, rows), f32)
    *a, raw, rs, rt, col, cols, plan = call(
        forward_kernel, "forward",
        [kind((4 * T_ROWS + M_ROWS, rows), bf16)] * 4
        + [
            kind((REFS, part), f32), scales, scales, kind((ITERS, REFS, rows), f32),
            kind((part, everything), bf16), kind((REFS, everything), bf16),
        ],
        7, 1,
        scratch=[pltpu.VMEM((T_ROWS, everything), bf16), pltpu.VMEM((T_ROWS, part), bf16)],
    )(*q, near, other, weights, lengths)
    a = [a[0]] + [send(value, step) for value, step in zip(a[1:], NEAR[1:])]
    c = call(first_sum_kernel, "first_sum", [kind((T_ROWS + M_ROWS, rows), bf16)] * 4, 4)(*a)
    c = [c[0]] + [send(value, step) for value, step in zip(c[1:], FAR[1:])]
    t, moments, logit_part = call(
        functools.partial(second_sum_kernel, width), "second_sum",
        [kind((T_ROWS, rows), bf16), kind((HEADS * PAD, P_SIZE), f32), kind((PAD, P_SIZE), f32)], 4,
    )(*c)
    logits = sum_logits(logit_part)
    ts = gather(t)
    pair = kind((2, part, rows), bf16)
    grad_scores, *mine, away = call(
        functools.partial(backward_kernel, width, score_scale), "backward",
        [kind((REFS, everything), bf16)] + [pair] * 4 + [kind((DEPTH, part, rows), bf16)],
        17, 1,
        scratch=[
            pltpu.VMEM((ITERS, P_SIZE, rows), f32),
            pltpu.VMEM((ITERS * HEADS * BLOCKS, rows), f32),
            pltpu.VMEM((HEADS * BLOCKS, rows), f32),
            pltpu.VMEM((2 * REFS, part), bf16),
            pltpu.VMEM((2 * REFS, everything), bf16),
            pltpu.VMEM((part, everything), f32),
        ],
    )(*q, *ts, rs, rt, col, moments, logits, raw, weights, plan, refs_part, labels)
    away = lax.ppermute(away, "core", [(0, 1), (1, 0)])
    o = call(cores_kernel, "cores", [pair] * 4, 5)(*mine, away)
    o = [o[0]] + [along_z(o[k], k) for k in (1, 2, 3)]
    u = call(chips_kernel, "chips", [kind((part, rows), bf16)] * 2, 4)(*o)
    u = [to_place(u[b], b) for b in range(2)]
    grad_features = call(last_kernel, "last", kind((rows, part), f32), 2)(*u)
    grad_references = call(references_kernel, "references", kind((REFS, part), f32), 2, flops=2 * REFS * part * everything)(
        grad_scores, cols
    )
    return (
        logits[:CLASSES, 0].reshape(batch, CLASSES),
        grad_features.reshape(batch, rows, part),
        grad_references.reshape(HEADS, P_SIZE, part),
    )


def solution(mesh):
    grid = Mesh(mesh.devices.reshape(DEPTH, 2, SIDE, SIDE), ("z", "core", "y", "x"))
    section, seq = ("z", "core"), ("y", "x")
    in_specs = (P(None, seq, None), P(section, None, None), P(section, seq, None), P(), P())
    out_specs = (P(), P(None, seq, section), P(section, None, seq))
    return jax.shard_map(local, mesh=grid, in_specs=in_specs, out_specs=out_specs, check_vma=False)
```

```python
import functools
import math

import jax
import jax.numpy as jnp
from jax import lax
from jax.experimental import pallas as pl
from jax.experimental.pallas import tpu as pltpu
from jax.sharding import Mesh, PartitionSpec as P

P_SIZE = 128
ITERS = 3
CLASSES = 10
PAD = 16
HEADS = 2
REFS = HEADS * P_SIZE

temper = 1.5
epsilon = 1e-06
loss_scale = 65536.0
f32 = jnp.float32
bf16 = jnp.bfloat16

SIDE = 4
DEPTH = 8
BLOCKS = SIDE * SIDE
FAR = ((0, 0), (2, 0), (0, 2), (2, 2))
NEAR = ((0, 0), (1, 0), (0, 1), (3, 3))
CHIPS = ((0, 1, 7, 2), (0, 1, 7, 6))
T_ROWS = REFS + HEADS * PAD
M_ROWS = 4 * PAD
L_ROWS = 2 * PAD
VMEM = pl.BlockSpec(memory_space=pltpu.VMEM)
SMEM = pl.BlockSpec(memory_space=pltpu.SMEM)
NT = (((1,), (1,)), ((), ()))
TN = (((0,), (0,)), ((), ()))


def call(kernel, name, shapes, n_vmem, n_smem=0, scratch=(), flops=0):
    many = isinstance(shapes, list)
    return pl.pallas_call(
        kernel,
        out_shape=shapes,
        in_specs=[VMEM] * n_vmem + [SMEM] * n_smem,
        out_specs=[VMEM] * len(shapes) if many else VMEM,
        scratch_shapes=list(scratch),
        compiler_params=pltpu.CompilerParams(vmem_limit_bytes=40 * 1024 * 1024),
        cost_estimate=pl.CostEstimate(flops=flops, bytes_accessed=1 << 20, transcendentals=0) if flops else None,
        name=name,
    )


def moved(first, second):
    y = lax.rem(lax.axis_index("y") + (first[0] + second[0]) % SIDE, SIDE)
    x = lax.rem(lax.axis_index("x") + (first[1] + second[1]) % SIDE, SIDE)
    return y * SIDE + x


def back(step):
    return (-step[0], -step[1])


def block_of(s):
    return moved(NEAR[s // 4], FAR[s % 4])


def lanes(block, rows):
    return pl.ds(pl.multiple_of(block * rows, rows), rows)


def send(value, step, sign=1):
    pairs = []
    for y in range(SIDE):
        for x in range(SIDE):
            to = (y + sign * step[0]) % SIDE * SIDE + (x + sign * step[1]) % SIDE
            pairs.append((y * SIDE + x, to))
    return lax.ppermute(value, ("y", "x"), pairs)


def stack_kernel(a, b, c, d, out_ref):
    for k, ref in enumerate((a, b, c, d)):
        out_ref[k] = ref[...]


def stack(values):
    shape = values[0].shape
    return call(stack_kernel, "stack", jax.ShapeDtypeStruct((4,) + shape, bf16), 4)(*values)


def scores_kernel(scale, f_ref, r_ref, k_ref):
    scores = lax.dot_general(r_ref[...], f_ref[...], NT, preferred_element_type=f32)
    k_ref[...] = jnp.exp(scores * scale).astype(bf16)


def split_kernel(f_ref, g0, g1, g2, g3, turned_ref):
    half = g0.shape[1]
    part = 2 * half
    for j in range(BLOCKS // 2):
        where = slice(2 * part * j, 2 * part * (j + 1))
        turned_ref[where, :] = jnp.transpose(f_ref[:, where])
    core = lax.axis_index("core")
    for k, out in enumerate((g0, g1, g2, g3)):
        for i in range(4):
            start = part * moved(FAR[k], NEAR[i]) + half * core
            out[i] = turned_ref[pl.ds(pl.multiple_of(start, half), half), :]


def regroup_kernel(h0, h1, h2, h3, refs_ref, e0, e1, e2, e3, mine_ref):
    part = mine_ref.shape[1]
    for i, out in enumerate((e0, e1, e2, e3)):
        for k, ref in enumerate((h0, h1, h2, h3)):
            out[k] = ref[i]
    place = moved((0, 0), (0, 0))
    pair = refs_ref[:, pl.ds(pl.multiple_of((place // 2) * (2 * part), 2 * part), 2 * part)]
    mine_ref[...] = jnp.where(lax.rem(place, 2) == 0, pair[:, :part], pair[:, part:])


def diagonal():
    square = (P_SIZE, P_SIZE)
    return lax.broadcasted_iota(jnp.int32, square, 0) == lax.broadcasted_iota(jnp.int32, square, 1)


def to_row(column):
    return jnp.sum(jnp.where(diagonal(), column, 0.0), axis=0, keepdims=True)


def to_column(row):
    return jnp.sum(jnp.where(diagonal(), row, 0.0), axis=1, keepdims=True)


def put_moments(ref, row, moments):
    for h in range(HEADS):
        high = moments[h].astype(bf16)
        ref[row + h * PAD : row + (h + 1) * PAD, :] = high
        low = row + (HEADS + h) * PAD
        ref[low : low + PAD, :] = (moments[h] - high.astype(f32)).astype(bf16)


def add_moments(refs, row):
    moments = []
    for h in range(HEADS):
        total = jnp.zeros((PAD, P_SIZE), f32)
        for ref in refs:
            total = total + ref[row + h * PAD : row + (h + 1) * PAD, :].astype(f32)
            low = row + (HEADS + h) * PAD
            total = total + ref[low : low + PAD, :].astype(f32)
        moments.append(total)
    return moments


def sinkhorn_kernel(q0, q1, q2, q3, len_ref, rs_ref, rt_ref, col_ref, plan_ref):
    q = (q0, q1, q2, q3)
    length = len_ref[0]
    rows = q0.shape[2]
    mass = 1.0 / (jnp.zeros((1, rows), jnp.int32) + length).astype(f32)
    lane = lax.broadcasted_iota(jnp.int32, (1, rows), 1)
    masses = [jnp.where(block_of(s) * rows + lane < length, mass, 0.0) for s in range(BLOCKS)]
    for t in range(ITERS):
        for h in range(HEADS):
            here = slice(h * P_SIZE, (h + 1) * P_SIZE)
            acc = jnp.zeros((P_SIZE, rows), f32)
            for s in range(BLOCKS):
                k = q[s // 4][s % 4, here, :].astype(f32)
                weighted = k if t == 0 else k * col_ref[t - 1, here, :]
                total = jnp.sum(weighted, axis=0, keepdims=True)
                scale = masses[s] / total
                place = (t * HEADS + h) * BLOCKS + s
                rt_ref[place : place + 1, :] = total
                rs_ref[place : place + 1, :] = scale
                acc = acc + k * scale
            col = 1.0 / (float(P_SIZE) * jnp.sum(acc, axis=1, keepdims=True))
            col_ref[t, here, :] = jnp.broadcast_to(col, (P_SIZE, rows))
    for h in range(HEADS):
        here = slice(h * P_SIZE, (h + 1) * P_SIZE)
        for s in range(BLOCKS):
            k = q[s // 4][s % 4, here, :].astype(f32)
            place = ((ITERS - 1) * HEADS + h) * BLOCKS + s
            plan = rs_ref[place : place + 1, :] * k * col_ref[ITERS - 1, here, :]
            plan_ref[here, lanes(block_of(s), rows)] = plan.astype(bf16)


def forward_kernel(
    e_ref, other_ref, wt_ref, plan_ref, a0, a1, a2, a3, raw_ref, fc_ref, wide_ref, ext_ref
):
    core = lax.axis_index("core")
    half, rows = e_ref.shape[2:]
    for i in range(4):
        for k in range(4):
            here = lanes(moved(back(NEAR[i]), FAR[k]), rows)
            fc_ref[pl.ds(pl.multiple_of(core * half, half), half), here] = e_ref[i, k]
            fc_ref[pl.ds(pl.multiple_of((1 - core) * half, half), half), here] = other_ref[i, k]
    raw = float(P_SIZE) * lax.dot_general(plan_ref[...], fc_ref[...], NT, preferred_element_type=f32)
    raw_ref[...] = raw
    ext_ref[:REFS, :] = raw.astype(bf16)
    ext_ref[REFS:, :] = wt_ref[...]
    wide_ref[...] = jnp.dot(ext_ref[...], fc_ref[...], preferred_element_type=f32).astype(bf16)
    moments = []
    for h in range(HEADS):
        here = slice(h * P_SIZE, (h + 1) * P_SIZE)
        squares = jnp.sum(raw_ref[here, :] * raw_ref[here, :], axis=1, keepdims=True)
        products = lax.dot_general(
            wt_ref[h * PAD : (h + 1) * PAD, :], ext_ref[here, :], NT, preferred_element_type=f32
        )
        kind = lax.broadcasted_iota(jnp.int32, products.shape, 0)
        moments.append(jnp.where(kind == CLASSES, to_row(squares), products))
    for i, out in enumerate((a0, a1, a2, a3)):
        for k in range(4):
            out[k * T_ROWS : (k + 1) * T_ROWS, :] = wide_ref[:, lanes(moved(NEAR[i], FAR[k]), rows)]
        put_moments(out, 4 * T_ROWS, moments)


def add_blocks(refs, rows):
    total = refs[0][rows, :].astype(f32)
    for ref in refs[1:]:
        total = total + ref[rows, :].astype(f32)
    return total.astype(bf16)


def first_sum_kernel(a0, a1, a2, a3, c0, c1, c2, c3):
    parts = (a0, a1, a2, a3)
    moments = add_moments(parts, 4 * T_ROWS)
    for k, out in enumerate((c0, c1, c2, c3)):
        for low in range(0, T_ROWS, 96):
            out[low : low + 96, :] = add_blocks(parts, slice(k * T_ROWS + low, k * T_ROWS + low + 96))
        put_moments(out, T_ROWS, moments)


def inverse_rms(moments, width):
    return lax.rsqrt(moments[CLASSES : CLASSES + 1, :] / width + epsilon)


def second_sum_kernel(width, c0, c1, c2, c3, t_ref, m_ref, logit_ref):
    parts = (c0, c1, c2, c3)
    moments = add_moments(parts, T_ROWS)
    logits = jnp.zeros((PAD, 1), f32)
    for h in range(HEADS):
        m_ref[h * PAD : (h + 1) * PAD, :] = moments[h]
        part = jnp.sum(inverse_rms(moments[h], width) * moments[h], axis=1, keepdims=True)
        logits = logits + part / P_SIZE
    logit_ref[...] = jnp.broadcast_to(logits, logit_ref.shape)
    for low in range(0, T_ROWS, 96):
        t_ref[low : low + 96, :] = add_blocks(parts, slice(low, low + 96))


def row_kernel(t0, t1, t2, t3, l0, l1, out_ref):
    for k, ref in enumerate((t0, t1, t2, t3)):
        out_ref[k * T_ROWS : (k + 1) * T_ROWS, :] = ref[...]
    logits = l0[...] + l1[...]
    high = logits.astype(bf16)
    low = 4 * T_ROWS
    out_ref[low : low + PAD, :] = high
    out_ref[low + PAD : low + 2 * PAD, :] = (logits - high.astype(f32)).astype(bf16)


def sum_logits(rows):
    y, x, z = lax.axis_index("y"), lax.axis_index("x"), lax.axis_index("z")
    total = jnp.zeros((PAD, P_SIZE), f32)
    parts, starts = [], []
    for ref, step in zip(rows, NEAR):
        low = 4 * T_ROWS
        parts.append(ref[low : low + PAD, :].astype(f32) + ref[low + PAD : low + 2 * PAD, :].astype(f32))
        away = 2 * lax.rem(y + step[0], 2) + lax.rem(x + step[1], 2)
        starts.append(lax.rem(z + away, 4))
    for a in range(4):
        for part, start in zip(parts, starts):
            total = total + jnp.where(start == a, part, 0.0)
    return total


def backward_kernel(
    width, score_scale,
    q0, q1, q2, q3, t0, t1, t2, t3, rs_ref, rt_ref, col_ref, m_ref, raw_ref, wt_ref, plan_ref, refs_ref, label_ref,
    logit_ref, gs_ref, p0, p1, p2, p3, other_ref, gt_ref, grs_ref, u_ref, left_ref, right_ref, wide_ref,
):
    q = (q0, q1, q2, q3)
    tt = (t0, t1, t2, t3)
    rows = q0.shape[2]
    size = float(P_SIZE)
    logits = sum_logits(tt)
    square = lax.broadcasted_iota(jnp.int32, (PAD, PAD), 0) == lax.broadcasted_iota(jnp.int32, (PAD, PAD), 1)
    logit_ref[...] = jnp.sum(jnp.where(square, logits[:, :PAD], 0.0), axis=0, keepdims=True)
    kind = lax.broadcasted_iota(jnp.int32, logits.shape, 0)
    exps = jnp.where(kind < CLASSES, jnp.exp(logits), 0.0)
    probs = exps / jnp.sum(exps, axis=0, keepdims=True)
    grads = loss_scale * (probs - (kind == label_ref[0]).astype(f32))
    grads = jnp.where(kind < CLASSES, grads, 0.0)
    left_ref[:REFS, :] = refs_ref[...]
    right_ref[REFS:, :] = plan_ref[...]
    for h in range(HEADS):
        here = slice(h * P_SIZE, (h + 1) * P_SIZE)
        moments = m_ref[h * PAD : (h + 1) * PAD, :]
        inverse_row = inverse_rms(moments, width)
        dual_row = inverse_row * jnp.sum(grads * moments, axis=0, keepdims=True) / (size * width)
        inverse = to_column(inverse_row)
        pull = to_column(inverse_row * dual_row)
        normed = jnp.sum(grads[:, :1] * wt_ref[h * PAD : (h + 1) * PAD, :].astype(f32), axis=0, keepdims=True) / size
        grad_raw = (inverse * (normed - raw_ref[here, :] * pull)).astype(bf16)
        left_ref[REFS + h * P_SIZE : REFS + (h + 1) * P_SIZE, :] = (size * grad_raw.astype(f32)).astype(bf16)
        first = jnp.broadcast_to(size * inverse, (P_SIZE, rows))
        second = first * pull

        def load(s):
            return q[s // 4][s % 4, here, :].astype(f32)

        def grad_plan(s, u):
            return first * u - second * tt[s // 4][s % 4 * T_ROWS + h * P_SIZE : s % 4 * T_ROWS + (h + 1) * P_SIZE, :].astype(f32)

        def row(ref, t, s):
            place = (t * HEADS + h) * BLOCKS + s
            return ref[place : place + 1, :]

        def put(ref, t, s, value):
            place = (t * HEADS + h) * BLOCKS + s
            ref[place : place + 1, :] = value

        acc = jnp.zeros((P_SIZE, rows), f32)
        for s in range(BLOCKS):
            low = s % 4 * T_ROWS + REFS + h * PAD
            v = tt[s // 4][low : low + PAD, :].astype(f32)
            u = jnp.sum(grads * v, axis=0, keepdims=True) / size
            put(u_ref, 0, s, u)
            weighted = grad_plan(s, u) * load(s)
            put(grs_ref, ITERS - 1, s, jnp.sum(weighted * col_ref[ITERS - 1, here, :], axis=0, keepdims=True))
            acc = acc + weighted * row(rs_ref, ITERS - 1, s)
        for t in reversed(range(ITERS)):
            grad_col = jnp.sum(acc, axis=1, keepdims=True)
            gt_ref[t] = -size * col_ref[t, here, :] ** 2 * grad_col
            acc = jnp.zeros((P_SIZE, rows), f32)
            for s in range(BLOCKS):
                k = load(s)
                grad_row = jnp.sum(k * gt_ref[t], axis=0, keepdims=True)
                if t == ITERS - 1:
                    grad_row = grad_row + row(grs_ref, t, s)
                grad_rowsum = -grad_row * row(rs_ref, t, s) / row(rt_ref, t, s)
                put(grs_ref, t, s, grad_rowsum)
                if t > 0:
                    acc = acc + k * grad_rowsum
        for s in range(BLOCKS):
            total = row(rs_ref, ITERS - 1, s) * col_ref[ITERS - 1, here, :] * grad_plan(s, row(u_ref, 0, s))
            for t in range(ITERS):
                total = total + row(rs_ref, t, s) * gt_ref[t]
                if t > 0:
                    total = total + row(grs_ref, t, s) * col_ref[t - 1, here, :]
                else:
                    total = total + row(grs_ref, t, s)
            right_ref[here, lanes(block_of(s), rows)] = (score_scale * total * load(s)).astype(bf16)
    gs_ref[...] = right_ref[:REFS, :]
    wide_ref[...] = lax.dot_general(left_ref[...], right_ref[...], TN, preferred_element_type=f32)
    core, z = lax.axis_index("core"), lax.axis_index("z")
    outs = (p0, p1, p2, p3)

    def take(step, which):
        return wide_ref[:, lanes(2 * lax.rem(z + step, DEPTH) + which, rows)].astype(bf16)

    for k in range(4):
        for b in range(2):
            step = jnp.where(core == 0, CHIPS[0][k], CHIPS[1][k]) + 4 * b
            outs[k][b] = take(step, core)
            step = jnp.where(core == 0, CHIPS[1][k], CHIPS[0][k]) + 4 * b
            other_ref[2 * k + b] = take(step, 1 - core)


def cores_kernel(p0, p1, p2, p3, other_ref, o0, o1, o2, o3):
    for k, (part, out) in enumerate(zip((p0, p1, p2, p3), (o0, o1, o2, o3))):
        for b in range(2):
            out[b] = (part[b].astype(f32) + other_ref[2 * k + b].astype(f32)).astype(bf16)


def chips_kernel(o0, o1, o2, o3, u0, u1):
    for b, out in enumerate((u0, u1)):
        total = o0[b].astype(f32) + o1[b].astype(f32) + o2[b].astype(f32) + o3[b].astype(f32)
        out[...] = total.astype(bf16)


def last_kernel(u0, u1, out_ref):
    out_ref[...] = u0[...].astype(f32) + u1[...].astype(f32)


def references_kernel(gs_ref, fc_ref, out_ref):
    for h in range(HEADS):
        heads = gs_ref[h * P_SIZE : (h + 1) * P_SIZE, :]
        out_ref[h] = lax.dot_general(fc_ref[...], heads, NT, preferred_element_type=f32)


def along_z(value, k):
    pairs = []
    for z in range(DEPTH):
        for core in range(2):
            pairs.append((2 * z + core, 2 * ((z + CHIPS[core][k]) % DEPTH) + core))
    return lax.ppermute(value, ("z", "core"), pairs)


def to_place(value, b):
    pairs = []
    for z in range(DEPTH):
        for core in range(2):
            for j in range(BLOCKS):
                block = 2 * ((z + 4 * b) % DEPTH) + core
                pairs.append(((2 * z + core) * BLOCKS + j, j * BLOCKS + block))
    return lax.ppermute(value, ("z", "core", "y", "x"), pairs)


def far_logits(value, b):
    pairs = []
    for z in range(DEPTH):
        for y in range(SIDE):
            for x in range(SIDE):
                source = (z + 4 * b + 2 * (y % 2) + x % 2) % DEPTH
                place = y * SIDE + x
                pairs.append((source * BLOCKS + place, z * BLOCKS + place))
    return lax.ppermute(value, ("z", "y", "x"), pairs)


def local(features, references, classifier, lengths, labels):
    batch, rows, width = features.shape
    part = width // BLOCKS
    everything = BLOCKS * rows
    score_scale = temper / math.sqrt(width)
    feats = features.reshape(rows, width)
    refs = references.reshape(REFS, width)
    kind = jax.ShapeDtypeStruct

    blocks = [kind((4, part // 2, rows), bf16)] * 4
    g = call(split_kernel, "split", blocks, 1, scratch=[pltpu.VMEM((width, rows), bf16)])(feats)
    kernel = call(functools.partial(scores_kernel, score_scale), "scores", kind((REFS, rows), bf16), 2)(feats, refs)
    g = [g[0]] + [send(value, step) for value, step in zip(g[1:], FAR[1:])]
    row = stack([kernel] + [send(kernel, step, -1) for step in FAR[1:]])
    *e, refs_part = call(regroup_kernel, "regroup", blocks + [kind((REFS, part), bf16)], 5)(*g, refs)
    e = stack([e[0]] + [send(value, step) for value, step in zip(e[1:], NEAR[1:])])
    q = [row] + [send(row, step, -1) for step in NEAR[1:]]
    other = lax.ppermute(e, "core", [(0, 1), (1, 0)])
    weights = jnp.pad(jnp.transpose(classifier, (0, 2, 1)), ((0, 0), (0, PAD - CLASSES), (0, 0)))
    weights = weights.reshape(HEADS * PAD, part)

    scales = kind((ITERS * HEADS * BLOCKS, rows), f32)
    rs, rt, col, plan = call(
        sinkhorn_kernel, "sinkhorn",
        [scales, scales, kind((ITERS, REFS, rows), f32), kind((REFS, everything), bf16)], 4, 1,
    )(*q, lengths)
    *a, raw, cols = call(
        forward_kernel, "forward",
        [kind((4 * T_ROWS + M_ROWS, rows), bf16)] * 4 + [kind((REFS, part), f32), kind((part, everything), bf16)], 4,
        scratch=[pltpu.VMEM((T_ROWS, everything), bf16), pltpu.VMEM((T_ROWS, part), bf16)],
    )(e, other, weights, plan)
    a = [a[0]] + [send(value, step) for value, step in zip(a[1:], NEAR[1:])]
    c = call(first_sum_kernel, "first_sum", [kind((T_ROWS + M_ROWS, rows), bf16)] * 4, 4)(*a)
    c = [c[0]] + [send(value, step) for value, step in zip(c[1:], FAR[1:])]
    t, moments, logit_part = call(
        functools.partial(second_sum_kernel, width), "second_sum",
        [kind((T_ROWS, rows), bf16), kind((HEADS * PAD, P_SIZE), f32), kind((PAD, P_SIZE), f32)], 4,
    )(*c)
    t = [t] + [send(t, step, -1) for step in FAR[1:]]
    logit_part = logit_part + lax.ppermute(logit_part, "core", [(0, 1), (1, 0)])
    row = call(row_kernel, "row", kind((4 * T_ROWS + L_ROWS, rows), bf16), 6)(
        *t, far_logits(logit_part, 0), far_logits(logit_part, 1)
    )
    ts = [row] + [send(row, step, -1) for step in NEAR[1:]]
    pair = kind((2, part, rows), bf16)
    logits, grad_scores, *mine, away = call(
        functools.partial(backward_kernel, width, score_scale), "backward",
        [kind((1, PAD), f32), kind((REFS, everything), bf16)] + [pair] * 4 + [kind((DEPTH, part, rows), bf16)],
        16, 1,
        scratch=[
            pltpu.VMEM((ITERS, P_SIZE, rows), f32),
            pltpu.VMEM((ITERS * HEADS * BLOCKS, rows), f32),
            pltpu.VMEM((HEADS * BLOCKS, rows), f32),
            pltpu.VMEM((2 * REFS, part), bf16),
            pltpu.VMEM((2 * REFS, everything), bf16),
            pltpu.VMEM((part, everything), f32),
        ],
    )(*q, *ts, rs, rt, col, moments, raw, weights, plan, refs_part, labels)
    away = lax.ppermute(away, "core", [(0, 1), (1, 0)])
    o = call(cores_kernel, "cores", [pair] * 4, 5)(*mine, away)
    o = [o[0]] + [along_z(o[k], k) for k in (1, 2, 3)]
    u = call(chips_kernel, "chips", [kind((part, rows), bf16)] * 2, 4)(*o)
    u = [to_place(u[b], b) for b in range(2)]
    grad_features = call(last_kernel, "last", kind((part, rows), f32), 2)(*u)
    grad_references = call(references_kernel, "references", kind((HEADS, part, rows), f32), 2, flops=2 * REFS * part * everything)(
        grad_scores, cols
    )
    return (
        logits[:, :CLASSES],
        jnp.transpose(grad_features).reshape(batch, rows, part),
        jnp.transpose(grad_references, (0, 2, 1)),
    )


def solution(mesh):
    grid = Mesh(mesh.devices.reshape(DEPTH, 2, SIDE, SIDE), ("z", "core", "y", "x"))
    section, seq = ("z", "core"), ("y", "x")
    in_specs = (P(None, seq, None), P(section, None, None), P(section, seq, None), P(), P())
    out_specs = (P(), P(None, seq, section), P(section, None, seq))
    return jax.shard_map(local, mesh=grid, in_specs=in_specs, out_specs=out_specs, check_vma=False)
```

```python
import functools
import math

import jax
import jax.numpy as jnp
from jax import lax
from jax.experimental import pallas as pl
from jax.experimental.pallas import tpu as pltpu
from jax.sharding import Mesh, PartitionSpec as P

P_SIZE = 128
ITERS = 3
CLASSES = 10
PAD = 16
HEADS = 2
REFS = HEADS * P_SIZE

temper = 1.5
epsilon = 1e-06
loss_scale = 65536.0
f32 = jnp.float32
bf16 = jnp.bfloat16

SIDE = 4
DEPTH = 8
BLOCKS = SIDE * SIDE
FAR = ((0, 0), (2, 0), (0, 2), (2, 2))
NEAR = ((0, 0), (1, 0), (0, 1), (3, 3))
CHIPS = ((0, 1, 7, 2), (0, 1, 7, 6))
T_ROWS = REFS + HEADS * PAD
M_ROWS = 4 * PAD
L_ROWS = 2 * PAD
VMEM = pl.BlockSpec(memory_space=pltpu.VMEM)
SMEM = pl.BlockSpec(memory_space=pltpu.SMEM)
NT = (((1,), (1,)), ((), ()))
TN = (((0,), (0,)), ((), ()))


def call(kernel, name, shapes, n_vmem, n_smem=0, scratch=(), flops=0):
    many = isinstance(shapes, list)
    return pl.pallas_call(
        kernel,
        out_shape=shapes,
        in_specs=[VMEM] * n_vmem + [SMEM] * n_smem,
        out_specs=[VMEM] * len(shapes) if many else VMEM,
        scratch_shapes=list(scratch),
        compiler_params=pltpu.CompilerParams(vmem_limit_bytes=40 * 1024 * 1024),
        cost_estimate=pl.CostEstimate(flops=flops, bytes_accessed=1 << 20, transcendentals=0) if flops else None,
        name=name,
    )


def moved(first, second):
    y = lax.rem(lax.axis_index("y") + (first[0] + second[0]) % SIDE, SIDE)
    x = lax.rem(lax.axis_index("x") + (first[1] + second[1]) % SIDE, SIDE)
    return y * SIDE + x


def back(step):
    return (-step[0], -step[1])


def block_of(s):
    return moved(NEAR[s // 4], FAR[s % 4])


def lanes(block, rows):
    return pl.ds(pl.multiple_of(block * rows, rows), rows)


def send(value, step, sign=1):
    pairs = []
    for y in range(SIDE):
        for x in range(SIDE):
            to = (y + sign * step[0]) % SIDE * SIDE + (x + sign * step[1]) % SIDE
            pairs.append((y * SIDE + x, to))
    return lax.ppermute(value, ("y", "x"), pairs)


def stack_kernel(a, b, c, d, out_ref):
    for k, ref in enumerate((a, b, c, d)):
        out_ref[k] = ref[...]


def stack(values):
    shape = values[0].shape
    return call(stack_kernel, "stack", jax.ShapeDtypeStruct((4,) + shape, bf16), 4)(*values)


def scores_kernel(scale, f_ref, r_ref, k_ref):
    scores = lax.dot_general(r_ref[...], f_ref[...], NT, preferred_element_type=f32)
    k_ref[...] = jnp.exp(scores * scale).astype(bf16)


def split_kernel(f_ref, g0, g1, g2, g3, turned_ref):
    half = g0.shape[1]
    part = 2 * half
    for j in range(BLOCKS // 2):
        where = slice(2 * part * j, 2 * part * (j + 1))
        turned_ref[where, :] = jnp.transpose(f_ref[:, where])
    core = lax.axis_index("core")
    for k, out in enumerate((g0, g1, g2, g3)):
        for i in range(4):
            start = part * moved(FAR[k], NEAR[i]) + half * core
            out[i] = turned_ref[pl.ds(pl.multiple_of(start, half), half), :]


def regroup_kernel(h0, h1, h2, h3, refs_ref, e0, e1, e2, e3, mine_ref):
    part = mine_ref.shape[1]
    for i, out in enumerate((e0, e1, e2, e3)):
        for k, ref in enumerate((h0, h1, h2, h3)):
            out[k] = ref[i]
    place = moved((0, 0), (0, 0))
    pair = refs_ref[:, pl.ds(pl.multiple_of((place // 2) * (2 * part), 2 * part), 2 * part)]
    mine_ref[...] = jnp.where(lax.rem(place, 2) == 0, pair[:, :part], pair[:, part:])


def diagonal():
    square = (P_SIZE, P_SIZE)
    return lax.broadcasted_iota(jnp.int32, square, 0) == lax.broadcasted_iota(jnp.int32, square, 1)


def to_row(column):
    return jnp.sum(jnp.where(diagonal(), column, 0.0), axis=0, keepdims=True)


def to_column(row):
    return jnp.sum(jnp.where(diagonal(), row, 0.0), axis=1, keepdims=True)


def put_moments(ref, row, moments):
    for h in range(HEADS):
        high = moments[h].astype(bf16)
        ref[row + h * PAD : row + (h + 1) * PAD, :] = high
        low = row + (HEADS + h) * PAD
        ref[low : low + PAD, :] = (moments[h] - high.astype(f32)).astype(bf16)


def add_moments(refs, row):
    moments = []
    for h in range(HEADS):
        total = jnp.zeros((PAD, P_SIZE), f32)
        for ref in refs:
            total = total + ref[row + h * PAD : row + (h + 1) * PAD, :].astype(f32)
            low = row + (HEADS + h) * PAD
            total = total + ref[low : low + PAD, :].astype(f32)
        moments.append(total)
    return moments


def sinkhorn_kernel(q0, q1, q2, q3, len_ref, rs_ref, rt_ref, col_ref, plan_ref):
    q = (q0, q1, q2, q3)
    length = len_ref[0]
    rows = q0.shape[2]
    mass = 1.0 / (jnp.zeros((1, rows), jnp.int32) + length).astype(f32)
    lane = lax.broadcasted_iota(jnp.int32, (1, rows), 1)
    masses = [jnp.where(block_of(s) * rows + lane < length, mass, 0.0) for s in range(BLOCKS)]
    for t in range(ITERS):
        for h in range(HEADS):
            here = slice(h * P_SIZE, (h + 1) * P_SIZE)
            acc = jnp.zeros((P_SIZE, rows), f32)
            for s in range(BLOCKS):
                k = q[s // 4][s % 4, here, :].astype(f32)
                weighted = k if t == 0 else k * col_ref[t - 1, here, :]
                total = jnp.sum(weighted, axis=0, keepdims=True)
                scale = masses[s] / total
                place = (t * HEADS + h) * BLOCKS + s
                rt_ref[place : place + 1, :] = total
                rs_ref[place : place + 1, :] = scale
                acc = acc + k * scale
            col = 1.0 / (float(P_SIZE) * jnp.sum(acc, axis=1, keepdims=True))
            col_ref[t, here, :] = jnp.broadcast_to(col, (P_SIZE, rows))
    for h in range(HEADS):
        here = slice(h * P_SIZE, (h + 1) * P_SIZE)
        for s in range(BLOCKS):
            k = q[s // 4][s % 4, here, :].astype(f32)
            place = ((ITERS - 1) * HEADS + h) * BLOCKS + s
            plan = rs_ref[place : place + 1, :] * k * col_ref[ITERS - 1, here, :]
            plan_ref[here, lanes(block_of(s), rows)] = plan.astype(bf16)


def forward_kernel(
    e_ref, other_ref, wt_ref, plan_ref, a0, a1, a2, a3, raw_ref, fc_ref, wide_ref, ext_ref
):
    core = lax.axis_index("core")
    half, rows = e_ref.shape[2:]
    for i in range(4):
        for k in range(4):
            here = lanes(moved(back(NEAR[i]), FAR[k]), rows)
            fc_ref[pl.ds(pl.multiple_of(core * half, half), half), here] = e_ref[i, k]
            fc_ref[pl.ds(pl.multiple_of((1 - core) * half, half), half), here] = other_ref[i, k]
    raw = float(P_SIZE) * lax.dot_general(plan_ref[...], fc_ref[...], NT, preferred_element_type=f32)
    raw_ref[...] = raw
    ext_ref[:REFS, :] = raw.astype(bf16)
    ext_ref[REFS:, :] = wt_ref[...]
    wide_ref[...] = jnp.dot(ext_ref[...], fc_ref[...], preferred_element_type=f32).astype(bf16)
    moments = []
    for h in range(HEADS):
        here = slice(h * P_SIZE, (h + 1) * P_SIZE)
        squares = jnp.sum(raw_ref[here, :] * raw_ref[here, :], axis=1, keepdims=True)
        products = lax.dot_general(
            wt_ref[h * PAD : (h + 1) * PAD, :], ext_ref[here, :], NT, preferred_element_type=f32
        )
        kind = lax.broadcasted_iota(jnp.int32, products.shape, 0)
        moments.append(jnp.where(kind == CLASSES, to_row(squares), products))
    for i, out in enumerate((a0, a1, a2, a3)):
        for k in range(4):
            out[k * T_ROWS : (k + 1) * T_ROWS, :] = wide_ref[:, lanes(moved(NEAR[i], FAR[k]), rows)]
        put_moments(out, 4 * T_ROWS, moments)


def add_blocks(refs, rows):
    total = refs[0][rows, :].astype(f32)
    for ref in refs[1:]:
        total = total + ref[rows, :].astype(f32)
    return total.astype(bf16)


def first_sum_kernel(a0, a1, a2, a3, c0, c1, c2, c3):
    parts = (a0, a1, a2, a3)
    moments = add_moments(parts, 4 * T_ROWS)
    for k, out in enumerate((c0, c1, c2, c3)):
        for low in range(0, T_ROWS, 96):
            out[low : low + 96, :] = add_blocks(parts, slice(k * T_ROWS + low, k * T_ROWS + low + 96))
        put_moments(out, T_ROWS, moments)


def inverse_rms(moments, width):
    return lax.rsqrt(moments[CLASSES : CLASSES + 1, :] / width + epsilon)


def second_sum_kernel(width, c0, c1, c2, c3, t_ref, m_ref, logit_ref):
    parts = (c0, c1, c2, c3)
    moments = add_moments(parts, T_ROWS)
    logits = jnp.zeros((PAD, 1), f32)
    for h in range(HEADS):
        m_ref[h * PAD : (h + 1) * PAD, :] = moments[h]
        part = jnp.sum(inverse_rms(moments[h], width) * moments[h], axis=1, keepdims=True)
        logits = logits + part / P_SIZE
    logit_ref[...] = jnp.broadcast_to(logits, logit_ref.shape)
    for low in range(0, T_ROWS, 96):
        t_ref[low : low + 96, :] = add_blocks(parts, slice(low, low + 96))


def row_kernel(t0, t1, t2, t3, l0, l1, out_ref):
    for k, ref in enumerate((t0, t1, t2, t3)):
        out_ref[k * T_ROWS : (k + 1) * T_ROWS, :] = ref[...]
    logits = l0[...] + l1[...]
    high = logits.astype(bf16)
    low = 4 * T_ROWS
    out_ref[low : low + PAD, :] = high
    out_ref[low + PAD : low + 2 * PAD, :] = (logits - high.astype(f32)).astype(bf16)


def sum_logits(rows):
    y, x, z = lax.axis_index("y"), lax.axis_index("x"), lax.axis_index("z")
    total = jnp.zeros((PAD, P_SIZE), f32)
    parts, starts = [], []
    for ref, step in zip(rows, NEAR):
        low = 4 * T_ROWS
        parts.append(ref[low : low + PAD, :].astype(f32) + ref[low + PAD : low + 2 * PAD, :].astype(f32))
        away = 2 * lax.rem(y + step[0], 2) + lax.rem(x + step[1], 2)
        starts.append(lax.rem(z + away, 4))
    for a in range(4):
        for part, start in zip(parts, starts):
            total = total + jnp.where(start == a, part, 0.0)
    return total


def backward_kernel(
    width, score_scale,
    q0, q1, q2, q3, t0, t1, t2, t3, rs_ref, rt_ref, col_ref, m_ref, raw_ref, wt_ref, plan_ref, refs_ref, label_ref,
    logit_ref, gs_ref, p0, p1, p2, p3, other_ref, gt_ref, grs_ref, u_ref, left_ref, right_ref, wide_ref,
):
    q = (q0, q1, q2, q3)
    tt = (t0, t1, t2, t3)
    rows = q0.shape[2]
    size = float(P_SIZE)
    logits = sum_logits(tt)
    square = lax.broadcasted_iota(jnp.int32, (PAD, PAD), 0) == lax.broadcasted_iota(jnp.int32, (PAD, PAD), 1)
    logit_ref[...] = jnp.sum(jnp.where(square, logits[:, :PAD], 0.0), axis=0, keepdims=True)
    kind = lax.broadcasted_iota(jnp.int32, logits.shape, 0)
    exps = jnp.where(kind < CLASSES, jnp.exp(logits), 0.0)
    probs = exps / jnp.sum(exps, axis=0, keepdims=True)
    grads = loss_scale * (probs - (kind == label_ref[0]).astype(f32))
    grads = jnp.where(kind < CLASSES, grads, 0.0)
    left_ref[:REFS, :] = refs_ref[...]
    right_ref[REFS:, :] = plan_ref[...]
    for h in range(HEADS):
        here = slice(h * P_SIZE, (h + 1) * P_SIZE)
        moments = m_ref[h * PAD : (h + 1) * PAD, :]
        inverse_row = inverse_rms(moments, width)
        dual_row = inverse_row * jnp.sum(grads * moments, axis=0, keepdims=True) / (size * width)
        inverse = to_column(inverse_row)
        pull = to_column(inverse_row * dual_row)
        normed = jnp.sum(grads[:, :1] * wt_ref[h * PAD : (h + 1) * PAD, :].astype(f32), axis=0, keepdims=True) / size
        grad_raw = (inverse * (normed - raw_ref[here, :] * pull)).astype(bf16)
        left_ref[REFS + h * P_SIZE : REFS + (h + 1) * P_SIZE, :] = (size * grad_raw.astype(f32)).astype(bf16)
        first = jnp.broadcast_to(size * inverse, (P_SIZE, rows))
        second = first * pull

        def load(s):
            return q[s // 4][s % 4, here, :].astype(f32)

        def grad_plan(s, u):
            return first * u - second * tt[s // 4][s % 4 * T_ROWS + h * P_SIZE : s % 4 * T_ROWS + (h + 1) * P_SIZE, :].astype(f32)

        def row(ref, t, s):
            place = (t * HEADS + h) * BLOCKS + s
            return ref[place : place + 1, :]

        def put(ref, t, s, value):
            place = (t * HEADS + h) * BLOCKS + s
            ref[place : place + 1, :] = value

        acc = jnp.zeros((P_SIZE, rows), f32)
        for s in range(BLOCKS):
            low = s % 4 * T_ROWS + REFS + h * PAD
            v = tt[s // 4][low : low + PAD, :].astype(f32)
            u = jnp.sum(grads * v, axis=0, keepdims=True) / size
            put(u_ref, 0, s, u)
            weighted = grad_plan(s, u) * load(s)
            put(grs_ref, ITERS - 1, s, jnp.sum(weighted * col_ref[ITERS - 1, here, :], axis=0, keepdims=True))
            acc = acc + weighted * row(rs_ref, ITERS - 1, s)
        for t in reversed(range(ITERS)):
            grad_col = jnp.sum(acc, axis=1, keepdims=True)
            gt_ref[t] = -size * col_ref[t, here, :] ** 2 * grad_col
            acc = jnp.zeros((P_SIZE, rows), f32)
            for s in range(BLOCKS):
                k = load(s)
                grad_row = jnp.sum(k * gt_ref[t], axis=0, keepdims=True)
                if t == ITERS - 1:
                    grad_row = grad_row + row(grs_ref, t, s)
                grad_rowsum = -grad_row * row(rs_ref, t, s) / row(rt_ref, t, s)
                put(grs_ref, t, s, grad_rowsum)
                if t > 0:
                    acc = acc + k * grad_rowsum
        for s in range(BLOCKS):
            total = row(rs_ref, ITERS - 1, s) * col_ref[ITERS - 1, here, :] * grad_plan(s, row(u_ref, 0, s))
            for t in range(ITERS):
                total = total + row(rs_ref, t, s) * gt_ref[t]
                if t > 0:
                    total = total + row(grs_ref, t, s) * col_ref[t - 1, here, :]
                else:
                    total = total + row(grs_ref, t, s)
            right_ref[here, lanes(block_of(s), rows)] = (score_scale * total * load(s)).astype(bf16)
    gs_ref[...] = right_ref[:REFS, :]
    wide_ref[...] = lax.dot_general(left_ref[...], right_ref[...], TN, preferred_element_type=f32)
    core, z = lax.axis_index("core"), lax.axis_index("z")
    outs = (p0, p1, p2, p3)

    def take(step, which):
        return wide_ref[:, lanes(2 * lax.rem(z + step, DEPTH) + which, rows)].astype(bf16)

    for k in range(4):
        for b in range(2):
            step = jnp.where(core == 0, CHIPS[0][k], CHIPS[1][k]) + 4 * b
            outs[k][b] = take(step, core)
            step = jnp.where(core == 0, CHIPS[1][k], CHIPS[0][k]) + 4 * b
            other_ref[2 * k + b] = take(step, 1 - core)


def cores_kernel(p0, p1, p2, p3, other_ref, o0, o1, o2, o3):
    for k, (part, out) in enumerate(zip((p0, p1, p2, p3), (o0, o1, o2, o3))):
        for b in range(2):
            out[b] = (part[b].astype(f32) + other_ref[2 * k + b].astype(f32)).astype(bf16)


def chips_kernel(o0, o1, o2, o3, u0, u1):
    for b, out in enumerate((u0, u1)):
        total = o0[b].astype(f32) + o1[b].astype(f32) + o2[b].astype(f32) + o3[b].astype(f32)
        out[...] = total.astype(bf16)


def last_kernel(u0, u1, out_ref):
    out_ref[...] = u0[...].astype(f32) + u1[...].astype(f32)


def references_kernel(gs_ref, fc_ref, out_ref):
    for h in range(HEADS):
        heads = gs_ref[h * P_SIZE : (h + 1) * P_SIZE, :]
        out_ref[h] = lax.dot_general(fc_ref[...], heads, NT, preferred_element_type=f32)


def along_z(value, k):
    pairs = []
    for z in range(DEPTH):
        for core in range(2):
            pairs.append((2 * z + core, 2 * ((z + CHIPS[core][k]) % DEPTH) + core))
    return lax.ppermute(value, ("z", "core"), pairs)


def to_place(value, b):
    pairs = []
    for z in range(DEPTH):
        for core in range(2):
            for j in range(BLOCKS):
                block = 2 * ((z + 4 * b) % DEPTH) + core
                pairs.append(((2 * z + core) * BLOCKS + j, j * BLOCKS + block))
    return lax.ppermute(value, ("z", "core", "y", "x"), pairs)


def far_logits(value, b):
    pairs = []
    for z in range(DEPTH):
        for y in range(SIDE):
            for x in range(SIDE):
                source = (z + 4 * b + 2 * (y % 2) + x % 2) % DEPTH
                place = y * SIDE + x
                pairs.append((source * BLOCKS + place, z * BLOCKS + place))
    return lax.ppermute(value, ("z", "y", "x"), pairs)


def local(features, references, classifier, lengths, labels):
    batch, rows, width = features.shape
    part = width // BLOCKS
    everything = BLOCKS * rows
    score_scale = temper / math.sqrt(width)
    feats = features.reshape(rows, width)
    refs = references.reshape(REFS, width)
    kind = jax.ShapeDtypeStruct

    blocks = [kind((4, part // 2, rows), bf16)] * 4
    g = call(split_kernel, "split", blocks, 1, scratch=[pltpu.VMEM((width, rows), bf16)])(feats)
    kernel = call(functools.partial(scores_kernel, score_scale), "scores", kind((REFS, rows), bf16), 2)(feats, refs)
    g = [g[0]] + [send(value, step) for value, step in zip(g[1:], FAR[1:])]
    row = [kernel] + [send(kernel, step, -1) for step in FAR[1:]]
    g, row = lax.optimization_barrier((g, row))
    row = stack(row)
    *e, refs_part = call(regroup_kernel, "regroup", blocks + [kind((REFS, part), bf16)], 5)(*g, refs)
    e = [e[0]] + [send(value, step) for value, step in zip(e[1:], NEAR[1:])]
    q = [row] + [send(row, step, -1) for step in NEAR[1:]]
    e, q = lax.optimization_barrier((e, q))
    e = stack(e)
    other = lax.ppermute(e, "core", [(0, 1), (1, 0)])
    weights = jnp.pad(jnp.transpose(classifier, (0, 2, 1)), ((0, 0), (0, PAD - CLASSES), (0, 0)))
    weights = weights.reshape(HEADS * PAD, part)

    scales = kind((ITERS * HEADS * BLOCKS, rows), f32)
    rs, rt, col, plan = call(
        sinkhorn_kernel, "sinkhorn",
        [scales, scales, kind((ITERS, REFS, rows), f32), kind((REFS, everything), bf16)], 4, 1,
    )(*q, lengths)
    *a, raw, cols = call(
        forward_kernel, "forward",
        [kind((4 * T_ROWS + M_ROWS, rows), bf16)] * 4 + [kind((REFS, part), f32), kind((part, everything), bf16)], 4,
        scratch=[pltpu.VMEM((T_ROWS, everything), bf16), pltpu.VMEM((T_ROWS, part), bf16)],
    )(e, other, weights, plan)
    a = [a[0]] + [send(value, step) for value, step in zip(a[1:], NEAR[1:])]
    c = call(first_sum_kernel, "first_sum", [kind((T_ROWS + M_ROWS, rows), bf16)] * 4, 4)(*a)
    c = [c[0]] + [send(value, step) for value, step in zip(c[1:], FAR[1:])]
    t, moments, logit_part = call(
        functools.partial(second_sum_kernel, width), "second_sum",
        [kind((T_ROWS, rows), bf16), kind((HEADS * PAD, P_SIZE), f32), kind((PAD, P_SIZE), f32)], 4,
    )(*c)
    t = [t] + [send(t, step, -1) for step in FAR[1:]]
    logit_part = logit_part + lax.ppermute(logit_part, "core", [(0, 1), (1, 0)])
    row = call(row_kernel, "row", kind((4 * T_ROWS + L_ROWS, rows), bf16), 6)(
        *t, far_logits(logit_part, 0), far_logits(logit_part, 1)
    )
    ts = [row] + [send(row, step, -1) for step in NEAR[1:]]
    pair = kind((2, part, rows), bf16)
    logits, grad_scores, *mine, away = call(
        functools.partial(backward_kernel, width, score_scale), "backward",
        [kind((1, PAD), f32), kind((REFS, everything), bf16)] + [pair] * 4 + [kind((DEPTH, part, rows), bf16)],
        16, 1,
        scratch=[
            pltpu.VMEM((ITERS, P_SIZE, rows), f32),
            pltpu.VMEM((ITERS * HEADS * BLOCKS, rows), f32),
            pltpu.VMEM((HEADS * BLOCKS, rows), f32),
            pltpu.VMEM((2 * REFS, part), bf16),
            pltpu.VMEM((2 * REFS, everything), bf16),
            pltpu.VMEM((part, everything), f32),
        ],
    )(*q, *ts, rs, rt, col, moments, raw, weights, plan, refs_part, labels)
    away = lax.ppermute(away, "core", [(0, 1), (1, 0)])
    o = call(cores_kernel, "cores", [pair] * 4, 5)(*mine, away)
    o = [o[0]] + [along_z(o[k], k) for k in (1, 2, 3)]
    u = call(chips_kernel, "chips", [kind((part, rows), bf16)] * 2, 4)(*o)
    u = [to_place(u[b], b) for b in range(2)]
    grad_features = call(last_kernel, "last", kind((part, rows), f32), 2)(*u)
    grad_references = call(references_kernel, "references", kind((HEADS, part, rows), f32), 2, flops=2 * REFS * part * everything)(
        grad_scores, cols
    )
    return (
        logits[:, :CLASSES],
        jnp.transpose(grad_features).reshape(batch, rows, part),
        jnp.transpose(grad_references, (0, 2, 1)),
    )


def solution(mesh):
    grid = Mesh(mesh.devices.reshape(DEPTH, 2, SIDE, SIDE), ("z", "core", "y", "x"))
    section, seq = ("z", "core"), ("y", "x")
    in_specs = (P(None, seq, None), P(section, None, None), P(section, seq, None), P(), P())
    out_specs = (P(), P(None, seq, section), P(section, None, seq))
    return jax.shard_map(local, mesh=grid, in_specs=in_specs, out_specs=out_specs, check_vma=False)
```

```python
import functools
import math

import jax
import jax.numpy as jnp
from jax import lax
from jax.experimental import pallas as pl
from jax.experimental.pallas import tpu as pltpu
from jax.sharding import Mesh, PartitionSpec as P

P_SIZE = 128
ITERS = 3
CLASSES = 10
PAD = 16
HEADS = 2
REFS = HEADS * P_SIZE

temper = 1.5
epsilon = 1e-06
loss_scale = 65536.0
f32 = jnp.float32
bf16 = jnp.bfloat16

SIDE = 4
DEPTH = 8
BLOCKS = SIDE * SIDE
CHIPS = ((0, 1, 7, 2), (0, 1, 7, 6))
T_ROWS = REFS + HEADS * PAD
M_ROWS = 2 * PAD
VMEM = pl.BlockSpec(memory_space=pltpu.VMEM)
SMEM = pl.BlockSpec(memory_space=pltpu.SMEM)
NT = (((1,), (1,)), ((), ()))
TN = (((0,), (0,)), ((), ()))


HBM = pl.BlockSpec(memory_space=pltpu.HBM)


def call(kernel, name, shapes, specs, scratch=(), flops=0):
    many = isinstance(shapes, list)
    return pl.pallas_call(
        kernel,
        out_shape=shapes,
        in_specs=[VMEM] * specs if isinstance(specs, int) else specs,
        out_specs=[VMEM] * len(shapes) if many else VMEM,
        scratch_shapes=list(scratch),
        compiler_params=pltpu.CompilerParams(vmem_limit_bytes=40 * 1024 * 1024),
        cost_estimate=pl.CostEstimate(flops=flops, bytes_accessed=1 << 20, transcendentals=0) if flops else None,
        name=name,
    )


def lanes(block, rows):
    return pl.ds(pl.multiple_of(block * rows, rows), rows)


def exchange(value):
    return lax.all_to_all(value, ("y", "x"), 0, 0)


def scores_kernel(scale, f_hbm, r_hbm, out_ref, part_ref, f_ref, r_ref, turned_ref, sems):
    half = out_ref.shape[1] - REFS
    part = 2 * half
    steps = r_ref.shape[0]
    rows = r_ref.shape[1]
    load = pltpu.make_async_copy(f_hbm, f_ref, sems.at[steps])
    load.start()
    loads = []
    for k in range(steps):
        loads.append(pltpu.make_async_copy(r_hbm.at[pl.ds(k * rows, rows)], r_ref.at[k], sems.at[k]))
        loads[k].start()
    load.wait()
    for j in range(BLOCKS // 2):
        where = slice(2 * part * j, 2 * part * (j + 1))
        turned_ref[where, :] = jnp.transpose(f_ref[:, where])
    core = lax.axis_index("core")
    for j in range(BLOCKS):
        out_ref[j, :half, :] = turned_ref[pl.ds(pl.multiple_of(part * j + half * core, half), half), :]
    place = lax.axis_index("y") * SIDE + lax.axis_index("x")
    for k in range(steps):
        loads[k].wait()
        scores = lax.dot_general(r_ref[k], f_ref[...], NT, preferred_element_type=f32)
        kernel = jnp.exp(scores * scale).astype(bf16)
        for j in range(BLOCKS):
            out_ref[j, half + k * rows : half + (k + 1) * rows, :] = kernel
        pair = r_ref[k, :, pl.ds(pl.multiple_of((place // 2) * (2 * part), 2 * part), 2 * part)]
        part_ref[k * rows : (k + 1) * rows, :] = jnp.where(lax.rem(place, 2) == 0, pair[:, :part], pair[:, part:])


def peel_kernel(in_ref, out_ref):
    half = out_ref.shape[1]
    for j in range(BLOCKS):
        out_ref[j] = in_ref[j, :half, :]


def diagonal():
    square = (P_SIZE, P_SIZE)
    return lax.broadcasted_iota(jnp.int32, square, 0) == lax.broadcasted_iota(jnp.int32, square, 1)


def to_row(column):
    return jnp.sum(jnp.where(diagonal(), column, 0.0), axis=0, keepdims=True)


def to_column(row):
    return jnp.sum(jnp.where(diagonal(), row, 0.0), axis=1, keepdims=True)


def sinkhorn_kernel(q_ref, len_ref, rs_ref, rt_ref, col_ref, plan_ref):
    length = len_ref[0]
    rows = q_ref.shape[2]
    low = q_ref.shape[1] - REFS
    mass = 1.0 / (jnp.zeros((1, rows), jnp.int32) + length).astype(f32)
    lane = lax.broadcasted_iota(jnp.int32, (1, rows), 1)
    masses = [jnp.where(s * rows + lane < length, mass, 0.0) for s in range(BLOCKS)]
    for t in range(ITERS):
        for h in range(HEADS):
            here = slice(h * P_SIZE, (h + 1) * P_SIZE)
            acc = jnp.zeros((P_SIZE, rows), f32)
            for s in range(BLOCKS):
                k = q_ref[s, low + h * P_SIZE : low + (h + 1) * P_SIZE, :].astype(f32)
                weighted = k if t == 0 else k * col_ref[t - 1, here, :]
                total = jnp.sum(weighted, axis=0, keepdims=True)
                scale = masses[s] / total
                place = (t * HEADS + h) * BLOCKS + s
                rt_ref[place : place + 1, :] = total
                rs_ref[place : place + 1, :] = scale
                acc = acc + k * scale
            col = 1.0 / (float(P_SIZE) * jnp.sum(acc, axis=1, keepdims=True))
            col_ref[t, here, :] = jnp.broadcast_to(col, (P_SIZE, rows))
    for h in range(HEADS):
        here = slice(h * P_SIZE, (h + 1) * P_SIZE)
        for s in range(BLOCKS):
            k = q_ref[s, low + h * P_SIZE : low + (h + 1) * P_SIZE, :].astype(f32)
            place = ((ITERS - 1) * HEADS + h) * BLOCKS + s
            plan = rs_ref[place : place + 1, :] * k * col_ref[ITERS - 1, here, :]
            plan_ref[here, s * rows : (s + 1) * rows] = plan.astype(bf16)


def forward_kernel(e_ref, other_ref, wt_ref, plan_ref, out_ref, raw_ref, fc_ref, ext_ref):
    core = lax.axis_index("core")
    half, rows = e_ref.shape[1:]
    for j in range(BLOCKS):
        here = slice(j * rows, (j + 1) * rows)
        fc_ref[pl.ds(pl.multiple_of(core * half, half), half), here] = e_ref[j]
        fc_ref[pl.ds(pl.multiple_of((1 - core) * half, half), half), here] = other_ref[j]
    raw = float(P_SIZE) * lax.dot_general(plan_ref[...], fc_ref[...], NT, preferred_element_type=f32)
    raw_ref[...] = raw
    ext_ref[:REFS, :] = raw.astype(bf16)
    ext_ref[REFS:, :] = wt_ref[...]
    for i in range(4):
        wide = jnp.dot(
            ext_ref[...], fc_ref[:, 4 * i * rows : 4 * (i + 1) * rows], preferred_element_type=f32
        ).astype(bf16)
        for k in range(4):
            out_ref[4 * i + k, :T_ROWS, :] = wide[:, k * rows : (k + 1) * rows]
    for h in range(HEADS):
        here = slice(h * P_SIZE, (h + 1) * P_SIZE)
        squares = jnp.sum(raw_ref[here, :] * raw_ref[here, :], axis=1, keepdims=True)
        products = lax.dot_general(
            wt_ref[h * PAD : (h + 1) * PAD, :], ext_ref[here, :], NT, preferred_element_type=f32
        )
        kind = lax.broadcasted_iota(jnp.int32, products.shape, 0)
        moments = jnp.where(kind == CLASSES, to_row(squares), products).astype(bf16)
        for j in range(BLOCKS):
            out_ref[j, T_ROWS + h * PAD : T_ROWS + (h + 1) * PAD, :] = moments


def add_blocks(ref, low, high):
    total = ref[0, low:high, :].astype(f32)
    for j in range(1, BLOCKS):
        total = total + ref[j, low:high, :].astype(f32)
    return total


def inverse_rms(moments, width):
    return lax.rsqrt(moments[CLASSES : CLASSES + 1, :] / width + epsilon)


def sum_kernel(width, in_ref, t_ref, m_ref, logit_ref):
    logits = jnp.zeros((PAD, 1), f32)
    for h in range(HEADS):
        moments = add_blocks(in_ref, T_ROWS + h * PAD, T_ROWS + (h + 1) * PAD)
        m_ref[h * PAD : (h + 1) * PAD, :] = moments
        part = jnp.sum(inverse_rms(moments, width) * moments, axis=1, keepdims=True)
        logits = logits + part / P_SIZE
    logit_ref[...] = jnp.broadcast_to(logits, logit_ref.shape)
    for low in range(0, T_ROWS, 96):
        t_ref[low : low + 96, :] = add_blocks(in_ref, low, low + 96).astype(bf16)


def row_kernel(t_ref, logit_ref, out_ref):
    logits = logit_ref[...]
    high = logits.astype(bf16)
    lane = lax.broadcasted_iota(jnp.int32, logits.shape, 1)
    both = jnp.where(lane < P_SIZE // 2, high.astype(f32), logits - high.astype(f32)).astype(bf16)
    for j in range(BLOCKS):
        out_ref[j, :T_ROWS, :] = t_ref[...]
        out_ref[j, T_ROWS:, :] = both


def sum_logits(ref):
    section = 2 * lax.axis_index("z") + lax.axis_index("core")
    total = jnp.zeros((PAD, P_SIZE), f32)
    for other in range(BLOCKS):
        total = total + ref[lax.rem(other + BLOCKS - section, BLOCKS), T_ROWS:, :].astype(f32)
    return jnp.broadcast_to(total[:, :1] + total[:, P_SIZE // 2 : P_SIZE // 2 + 1], total.shape)


def backward_kernel(
    width, score_scale,
    q_ref, t_ref, rs_ref, rt_ref, col_ref, m_ref, raw_ref, wt_ref, plan_ref, refs_ref, label_ref,
    logit_ref, gs_ref, p0, p1, p2, p3, other_ref, gt_ref, grs_ref, u_ref, left_ref, right_ref, wide_ref,
):
    rows = q_ref.shape[2]
    base = q_ref.shape[1] - REFS
    size = float(P_SIZE)
    logits = sum_logits(t_ref)
    square = lax.broadcasted_iota(jnp.int32, (PAD, PAD), 0) == lax.broadcasted_iota(jnp.int32, (PAD, PAD), 1)
    logit_ref[...] = jnp.sum(jnp.where(square, logits[:, :PAD], 0.0), axis=0, keepdims=True)
    kind = lax.broadcasted_iota(jnp.int32, logits.shape, 0)
    exps = jnp.where(kind < CLASSES, jnp.exp(logits), 0.0)
    probs = exps / jnp.sum(exps, axis=0, keepdims=True)
    grads = loss_scale * (probs - (kind == label_ref[0]).astype(f32))
    grads = jnp.where(kind < CLASSES, grads, 0.0)
    left_ref[:REFS, :] = refs_ref[...]
    right_ref[REFS:, :] = plan_ref[...]
    for h in range(HEADS):
        here = slice(h * P_SIZE, (h + 1) * P_SIZE)
        moments = m_ref[h * PAD : (h + 1) * PAD, :]
        inverse_row = inverse_rms(moments, width)
        dual_row = inverse_row * jnp.sum(grads * moments, axis=0, keepdims=True) / (size * width)
        inverse = to_column(inverse_row)
        pull = to_column(inverse_row * dual_row)
        normed = jnp.sum(grads[:, :1] * wt_ref[h * PAD : (h + 1) * PAD, :].astype(f32), axis=0, keepdims=True) / size
        grad_raw = (inverse * (normed - raw_ref[here, :] * pull)).astype(bf16)
        left_ref[REFS + h * P_SIZE : REFS + (h + 1) * P_SIZE, :] = (size * grad_raw.astype(f32)).astype(bf16)
        first = jnp.broadcast_to(size * inverse, (P_SIZE, rows))
        second = first * pull

        def load(s):
            return q_ref[s, base + h * P_SIZE : base + (h + 1) * P_SIZE, :].astype(f32)

        def grad_plan(s, u):
            return first * u - second * t_ref[s, here, :].astype(f32)

        def row(ref, t, s):
            place = (t * HEADS + h) * BLOCKS + s
            return ref[place : place + 1, :]

        def put(ref, t, s, value):
            place = (t * HEADS + h) * BLOCKS + s
            ref[place : place + 1, :] = value

        acc = jnp.zeros((P_SIZE, rows), f32)
        for s in range(BLOCKS):
            v = t_ref[s, REFS + h * PAD : REFS + (h + 1) * PAD, :].astype(f32)
            u = jnp.sum(grads * v, axis=0, keepdims=True) / size
            put(u_ref, 0, s, u)
            weighted = grad_plan(s, u) * load(s)
            put(grs_ref, ITERS - 1, s, jnp.sum(weighted * col_ref[ITERS - 1, here, :], axis=0, keepdims=True))
            acc = acc + weighted * row(rs_ref, ITERS - 1, s)
        for t in reversed(range(ITERS)):
            grad_col = jnp.sum(acc, axis=1, keepdims=True)
            gt_ref[t] = -size * col_ref[t, here, :] ** 2 * grad_col
            acc = jnp.zeros((P_SIZE, rows), f32)
            for s in range(BLOCKS):
                k = load(s)
                grad_row = jnp.sum(k * gt_ref[t], axis=0, keepdims=True)
                if t == ITERS - 1:
                    grad_row = grad_row + row(grs_ref, t, s)
                grad_rowsum = -grad_row * row(rs_ref, t, s) / row(rt_ref, t, s)
                put(grs_ref, t, s, grad_rowsum)
                if t > 0:
                    acc = acc + k * grad_rowsum
        for s in range(BLOCKS):
            total = row(rs_ref, ITERS - 1, s) * col_ref[ITERS - 1, here, :] * grad_plan(s, row(u_ref, 0, s))
            for t in range(ITERS):
                total = total + row(rs_ref, t, s) * gt_ref[t]
                if t > 0:
                    total = total + row(grs_ref, t, s) * col_ref[t - 1, here, :]
                else:
                    total = total + row(grs_ref, t, s)
            right_ref[here, s * rows : (s + 1) * rows] = (score_scale * total * load(s)).astype(bf16)
    gs_ref[...] = right_ref[:REFS, :]
    wide_ref[...] = lax.dot_general(left_ref[...], right_ref[...], TN, preferred_element_type=f32)
    core, z = lax.axis_index("core"), lax.axis_index("z")
    outs = (p0, p1, p2, p3)

    def take(step, which):
        return wide_ref[:, lanes(2 * lax.rem(z + step, DEPTH) + which, rows)].astype(bf16)

    for k in range(4):
        for b in range(2):
            step = jnp.where(core == 0, CHIPS[0][k], CHIPS[1][k]) + 4 * b
            outs[k][b] = take(step, core)
            step = jnp.where(core == 0, CHIPS[1][k], CHIPS[0][k]) + 4 * b
            other_ref[2 * k + b] = take(step, 1 - core)


def cores_kernel(p0, p1, p2, p3, other_ref, o0, o1, o2, o3):
    for k, (part, out) in enumerate(zip((p0, p1, p2, p3), (o0, o1, o2, o3))):
        for b in range(2):
            out[b] = (part[b].astype(f32) + other_ref[2 * k + b].astype(f32)).astype(bf16)


def chips_kernel(o0, o1, o2, o3, u0, u1):
    for b, out in enumerate((u0, u1)):
        total = o0[b].astype(f32) + o1[b].astype(f32) + o2[b].astype(f32) + o3[b].astype(f32)
        out[...] = total.astype(bf16)


def last_kernel(u0, u1, out_ref):
    out_ref[...] = u0[...].astype(f32) + u1[...].astype(f32)


def references_kernel(gs_ref, fc_ref, out_ref):
    for h in range(HEADS):
        heads = gs_ref[h * P_SIZE : (h + 1) * P_SIZE, :]
        out_ref[h] = lax.dot_general(fc_ref[...], heads, NT, preferred_element_type=f32)


def along_z(value, k):
    pairs = []
    for z in range(DEPTH):
        for core in range(2):
            pairs.append((2 * z + core, 2 * ((z + CHIPS[core][k]) % DEPTH) + core))
    return lax.ppermute(value, ("z", "core"), pairs)


def to_place(value, b):
    pairs = []
    for z in range(DEPTH):
        for core in range(2):
            for j in range(BLOCKS):
                block = 2 * ((z + 4 * b) % DEPTH) + core
                pairs.append(((2 * z + core) * BLOCKS + j, j * BLOCKS + block))
    return lax.ppermute(value, ("z", "core", "y", "x"), pairs)


def spread_logits(value):
    pairs = [((s + j) % BLOCKS * BLOCKS + j, s * BLOCKS + j) for s in range(BLOCKS) for j in range(BLOCKS)]
    return lax.ppermute(value, ("z", "core", "y", "x"), pairs)


def local(features, references, classifier, lengths, labels):
    batch, rows, width = features.shape
    part = width // BLOCKS
    everything = BLOCKS * rows
    score_scale = temper / math.sqrt(width)
    feats = features.reshape(rows, width)
    refs = references.reshape(REFS, width)
    kind = jax.ShapeDtypeStruct

    steps = 4
    half = part // 2
    mixed, refs_part = call(
        functools.partial(scores_kernel, score_scale), "scores",
        [kind((BLOCKS, half + REFS, rows), bf16), kind((REFS, part), bf16)], [HBM, HBM],
        scratch=[
            pltpu.VMEM((rows, width), bf16), pltpu.VMEM((steps, REFS // steps, width), bf16),
            pltpu.VMEM((width, rows), bf16), pltpu.SemaphoreType.DMA((steps + 1,)),
        ],
    )(feats, refs)
    mixed = exchange(mixed)
    e = call(peel_kernel, "peel", kind((BLOCKS, half, rows), bf16), 1)(mixed)
    other = lax.ppermute(e, "core", [(0, 1), (1, 0)])
    weights = jnp.pad(jnp.transpose(classifier, (0, 2, 1)), ((0, 0), (0, PAD - CLASSES), (0, 0)))
    weights = weights.reshape(HEADS * PAD, part)

    scales = kind((ITERS * HEADS * BLOCKS, rows), f32)
    rs, rt, col, plan = call(
        sinkhorn_kernel, "sinkhorn",
        [scales, scales, kind((ITERS, REFS, rows), f32), kind((REFS, everything), bf16)], [VMEM, SMEM],
    )(mixed, lengths)
    products, raw, cols = call(
        forward_kernel, "forward",
        [kind((BLOCKS, T_ROWS + M_ROWS, rows), bf16), kind((REFS, part), f32), kind((part, everything), bf16)], 4,
        scratch=[pltpu.VMEM((T_ROWS, part), bf16)],
    )(e, other, weights, plan)
    t, moments, logit_part = call(
        functools.partial(sum_kernel, width), "sum",
        [kind((T_ROWS, rows), bf16), kind((HEADS * PAD, P_SIZE), f32), kind((PAD, P_SIZE), f32)], 1,
    )(exchange(products))
    ts = exchange(
        call(row_kernel, "row", kind((BLOCKS, T_ROWS + PAD, rows), bf16), 2)(t, spread_logits(logit_part))
    )
    pair = kind((2, part, rows), bf16)
    logits, grad_scores, *mine, away = call(
        functools.partial(backward_kernel, width, score_scale), "backward",
        [kind((1, PAD), f32), kind((REFS, everything), bf16)] + [pair] * 4 + [kind((DEPTH, part, rows), bf16)],
        [VMEM] * 10 + [SMEM],
        scratch=[
            pltpu.VMEM((ITERS, P_SIZE, rows), f32),
            pltpu.VMEM((ITERS * HEADS * BLOCKS, rows), f32),
            pltpu.VMEM((HEADS * BLOCKS, rows), f32),
            pltpu.VMEM((2 * REFS, part), bf16),
            pltpu.VMEM((2 * REFS, everything), bf16),
            pltpu.VMEM((part, everything), f32),
        ],
    )(mixed, ts, rs, rt, col, moments, raw, weights, plan, refs_part, labels)
    away = lax.ppermute(away, "core", [(0, 1), (1, 0)])
    o = call(cores_kernel, "cores", [pair] * 4, 5)(*mine, away)
    o = [o[0]] + [along_z(o[k], k) for k in (1, 2, 3)]
    u = call(chips_kernel, "chips", [kind((part, rows), bf16)] * 2, 4)(*o)
    u = [to_place(u[b], b) for b in range(2)]
    grad_features = call(last_kernel, "last", kind((part, rows), f32), 2)(*u)
    grad_references = call(references_kernel, "references", kind((HEADS, part, rows), f32), 2, flops=2 * REFS * part * everything)(
        grad_scores, cols
    )
    return (
        logits[:, :CLASSES],
        jnp.transpose(grad_features).reshape(batch, rows, part),
        jnp.transpose(grad_references, (0, 2, 1)),
    )


def solution(mesh):
    grid = Mesh(mesh.devices.reshape(DEPTH, 2, SIDE, SIDE), ("z", "core", "y", "x"))
    section, seq = ("z", "core"), ("y", "x")
    in_specs = (P(None, seq, None), P(section, None, None), P(section, seq, None), P(), P())
    out_specs = (P(), P(None, seq, section), P(section, None, seq))
    return jax.shard_map(local, mesh=grid, in_specs=in_specs, out_specs=out_specs, check_vma=False)
```

```python
import functools
import math

import jax
import jax.numpy as jnp
from jax import lax
from jax.experimental import pallas as pl
from jax.experimental.pallas import tpu as pltpu
from jax.sharding import Mesh, PartitionSpec as P

P_SIZE = 128
ITERS = 3
CLASSES = 10
PAD = 16
HEADS = 2
REFS = HEADS * P_SIZE

temper = 1.5
epsilon = 1e-06
loss_scale = 65536.0
f32 = jnp.float32
bf16 = jnp.bfloat16

SIDE = 4
DEPTH = 8
BLOCKS = SIDE * SIDE
CHIPS = ((0, 1, 7, 2), (0, 1, 7, 6))
T_ROWS = REFS + HEADS * PAD
M_ROWS = 2 * PAD
VMEM = pl.BlockSpec(memory_space=pltpu.VMEM)
SMEM = pl.BlockSpec(memory_space=pltpu.SMEM)
NT = (((1,), (1,)), ((), ()))
TN = (((0,), (0,)), ((), ()))


def call(kernel, name, shapes, specs, scratch=(), flops=0, mib=8):
    many = isinstance(shapes, list)
    return pl.pallas_call(
        kernel,
        out_shape=shapes,
        in_specs=[VMEM] * specs if isinstance(specs, int) else specs,
        out_specs=[VMEM] * len(shapes) if many else VMEM,
        scratch_shapes=list(scratch),
        compiler_params=pltpu.CompilerParams(vmem_limit_bytes=mib * 1024 * 1024),
        cost_estimate=pl.CostEstimate(flops=flops, bytes_accessed=1 << 20, transcendentals=0) if flops else None,
        name=name,
    )


def lanes(block, rows):
    return pl.ds(pl.multiple_of(block * rows, rows), rows)


def exchange(value):
    return lax.all_to_all(value, ("y", "x"), 0, 0)


def split_kernel(f_ref, out_ref, turned_ref):
    half = out_ref.shape[1]
    part = 2 * half
    for j in range(BLOCKS // 2):
        where = slice(2 * part * j, 2 * part * (j + 1))
        turned_ref[where, :] = jnp.transpose(f_ref[:, where])
    core = lax.axis_index("core")
    for j in range(BLOCKS):
        out_ref[j] = turned_ref[pl.ds(pl.multiple_of(part * j + half * core, half), half), :]


def scores_kernel(scale, f_ref, r_ref, half_ref, out_ref):
    half = half_ref.shape[1]
    scores = lax.dot_general(r_ref[...], f_ref[...], NT, preferred_element_type=f32)
    kernel = jnp.exp(scores * scale).astype(bf16)
    for j in range(BLOCKS):
        out_ref[j, :half, :] = half_ref[j]
        out_ref[j, half:, :] = kernel


def peel_kernel(in_ref, out_ref):
    half = out_ref.shape[1]
    for j in range(BLOCKS):
        out_ref[j] = in_ref[j, :half, :]


def put_columns(mixed_ref, other_ref, out_ref):
    core = lax.axis_index("core")
    half, rows = other_ref.shape[1:]
    for j in range(BLOCKS):
        here = slice(j * rows, (j + 1) * rows)
        out_ref[pl.ds(pl.multiple_of(core * half, half), half), here] = mixed_ref[j, :half, :]
        out_ref[pl.ds(pl.multiple_of((1 - core) * half, half), half), here] = other_ref[j]


def diagonal():
    square = (P_SIZE, P_SIZE)
    return lax.broadcasted_iota(jnp.int32, square, 0) == lax.broadcasted_iota(jnp.int32, square, 1)


def to_row(column):
    return jnp.sum(jnp.where(diagonal(), column, 0.0), axis=0, keepdims=True)


def to_column(row):
    return jnp.sum(jnp.where(diagonal(), row, 0.0), axis=1, keepdims=True)


def sinkhorn_kernel(q_ref, len_ref, label_ref, rs_ref, rt_ref, col_ref, plan_ref):
    length = len_ref[0]
    rows = q_ref.shape[2]
    low = q_ref.shape[1] - REFS
    mass = 1.0 / (jnp.zeros((1, rows), jnp.int32) + length).astype(f32)
    lane = lax.broadcasted_iota(jnp.int32, (1, rows), 1)
    masses = [jnp.where(s * rows + lane < length, mass, 0.0) for s in range(BLOCKS)]
    for t in range(ITERS):
        for h in range(HEADS):
            here = slice(h * P_SIZE, (h + 1) * P_SIZE)
            acc = jnp.zeros((P_SIZE, rows), f32)
            for s in range(BLOCKS):
                k = q_ref[s, low + h * P_SIZE : low + (h + 1) * P_SIZE, :].astype(f32)
                weighted = k if t == 0 else k * col_ref[t - 1, here, :]
                total = jnp.sum(weighted, axis=0, keepdims=True)
                scale = masses[s] / total
                place = (t * HEADS + h) * BLOCKS + s
                rt_ref[place : place + 1, :] = total
                rs_ref[place : place + 1, :] = scale
                acc = acc + k * scale
            col = 1.0 / (float(P_SIZE) * jnp.sum(acc, axis=1, keepdims=True))
            col_ref[t, here, :] = jnp.broadcast_to(col, (P_SIZE, rows))
    for h in range(HEADS):
        here = slice(h * P_SIZE, (h + 1) * P_SIZE)
        for s in range(BLOCKS):
            k = q_ref[s, low + h * P_SIZE : low + (h + 1) * P_SIZE, :].astype(f32)
            place = ((ITERS - 1) * HEADS + h) * BLOCKS + s
            plan = rs_ref[place : place + 1, :] * k * col_ref[ITERS - 1, here, :]
            plan_ref[here, s * rows : (s + 1) * rows] = plan.astype(bf16)


def forward_kernel(mixed_ref, other_ref, wt_ref, plan_ref, out_ref, raw_ref, fc_ref, ext_ref):
    rows = other_ref.shape[2]
    put_columns(mixed_ref, other_ref, fc_ref)
    raw = float(P_SIZE) * lax.dot_general(plan_ref[...], fc_ref[...], NT, preferred_element_type=f32)
    raw_ref[...] = raw
    ext_ref[:REFS, :] = raw.astype(bf16)
    ext_ref[REFS:, :] = wt_ref[...]
    for i in range(4):
        wide = jnp.dot(
            ext_ref[...], fc_ref[:, 4 * i * rows : 4 * (i + 1) * rows], preferred_element_type=f32
        ).astype(bf16)
        for k in range(4):
            out_ref[4 * i + k, :T_ROWS, :] = wide[:, k * rows : (k + 1) * rows]
    for h in range(HEADS):
        here = slice(h * P_SIZE, (h + 1) * P_SIZE)
        squares = jnp.sum(raw_ref[here, :] * raw_ref[here, :], axis=1, keepdims=True)
        products = lax.dot_general(
            wt_ref[h * PAD : (h + 1) * PAD, :], ext_ref[here, :], NT, preferred_element_type=f32
        )
        kind = lax.broadcasted_iota(jnp.int32, products.shape, 0)
        moments = jnp.where(kind == CLASSES, to_row(squares), products).astype(bf16)
        for j in range(BLOCKS):
            out_ref[j, T_ROWS + h * PAD : T_ROWS + (h + 1) * PAD, :] = moments


def add_blocks(ref, low, high):
    total = ref[0, low:high, :].astype(f32)
    for j in range(1, BLOCKS):
        total = total + ref[j, low:high, :].astype(f32)
    return total


def inverse_rms(moments, width):
    return lax.rsqrt(moments[CLASSES : CLASSES + 1, :] / width + epsilon)


def sum_kernel(width, in_ref, t_ref, m_ref, logit_ref):
    logits = jnp.zeros((PAD, 1), f32)
    for h in range(HEADS):
        moments = add_blocks(in_ref, T_ROWS + h * PAD, T_ROWS + (h + 1) * PAD)
        m_ref[h * PAD : (h + 1) * PAD, :] = moments
        part = jnp.sum(inverse_rms(moments, width) * moments, axis=1, keepdims=True)
        logits = logits + part / P_SIZE
    logit_ref[...] = jnp.broadcast_to(logits, logit_ref.shape)
    for low in range(0, T_ROWS, 96):
        t_ref[low : low + 96, :] = add_blocks(in_ref, low, low + 96).astype(bf16)


def row_kernel(t_ref, logit_ref, out_ref):
    logits = logit_ref[...]
    high = logits.astype(bf16)
    lane = lax.broadcasted_iota(jnp.int32, logits.shape, 1)
    both = jnp.where(lane < P_SIZE // 2, high.astype(f32), logits - high.astype(f32)).astype(bf16)
    for j in range(BLOCKS):
        out_ref[j, :T_ROWS, :] = t_ref[...]
        out_ref[j, T_ROWS:, :] = both


def sum_logits(ref):
    section = 2 * lax.axis_index("z") + lax.axis_index("core")
    total = jnp.zeros((PAD, P_SIZE), f32)
    for other in range(BLOCKS):
        total = total + ref[lax.rem(other + BLOCKS - section, BLOCKS), T_ROWS:, :].astype(f32)
    return jnp.broadcast_to(total[:, :1] + total[:, P_SIZE // 2 : P_SIZE // 2 + 1], total.shape)


def scales_of(grads, moments, width):
    inverse = inverse_rms(moments, width)
    dual = inverse * jnp.sum(grads * moments, axis=0, keepdims=True) / (float(P_SIZE) * width)
    return to_column(inverse), to_column(inverse * dual)


def backward_kernel(
    width, score_scale,
    q_ref, t_ref, rs_ref, rt_ref, col_ref, m_ref, label_ref,
    logit_ref, grads_ref, gs_ref, gt_ref, grs_ref, u_ref,
):
    rows = q_ref.shape[2]
    base = q_ref.shape[1] - REFS
    size = float(P_SIZE)
    logits = sum_logits(t_ref)
    square = lax.broadcasted_iota(jnp.int32, (PAD, PAD), 0) == lax.broadcasted_iota(jnp.int32, (PAD, PAD), 1)
    logit_ref[...] = jnp.sum(jnp.where(square, logits[:, :PAD], 0.0), axis=0, keepdims=True)
    kind = lax.broadcasted_iota(jnp.int32, logits.shape, 0)
    exps = jnp.where(kind < CLASSES, jnp.exp(logits), 0.0)
    probs = exps / jnp.sum(exps, axis=0, keepdims=True)
    grads = loss_scale * (probs - (kind == label_ref[0]).astype(f32))
    grads = jnp.where(kind < CLASSES, grads, 0.0)
    grads_ref[...] = grads
    for h in range(HEADS):
        here = slice(h * P_SIZE, (h + 1) * P_SIZE)
        inverse, pull = scales_of(grads, m_ref[h * PAD : (h + 1) * PAD, :], width)
        first = jnp.broadcast_to(size * inverse, (P_SIZE, rows))
        second = first * pull

        def load(s):
            return q_ref[s, base + h * P_SIZE : base + (h + 1) * P_SIZE, :].astype(f32)

        def grad_plan(s, u):
            return first * u - second * t_ref[s, here, :].astype(f32)

        def row(ref, t, s):
            place = (t * HEADS + h) * BLOCKS + s
            return ref[place : place + 1, :]

        def put(ref, t, s, value):
            place = (t * HEADS + h) * BLOCKS + s
            ref[place : place + 1, :] = value

        acc = jnp.zeros((P_SIZE, rows), f32)
        for s in range(BLOCKS):
            v = t_ref[s, REFS + h * PAD : REFS + (h + 1) * PAD, :].astype(f32)
            u = jnp.sum(grads * v, axis=0, keepdims=True) / size
            put(u_ref, 0, s, u)
            weighted = grad_plan(s, u) * load(s)
            put(grs_ref, ITERS - 1, s, jnp.sum(weighted * col_ref[ITERS - 1, here, :], axis=0, keepdims=True))
            acc = acc + weighted * row(rs_ref, ITERS - 1, s)
        for t in reversed(range(ITERS)):
            grad_col = jnp.sum(acc, axis=1, keepdims=True)
            gt_ref[t] = -size * col_ref[t, here, :] ** 2 * grad_col
            acc = jnp.zeros((P_SIZE, rows), f32)
            for s in range(BLOCKS):
                k = load(s)
                grad_row = jnp.sum(k * gt_ref[t], axis=0, keepdims=True)
                if t == ITERS - 1:
                    grad_row = grad_row + row(grs_ref, t, s)
                grad_rowsum = -grad_row * row(rs_ref, t, s) / row(rt_ref, t, s)
                put(grs_ref, t, s, grad_rowsum)
                if t > 0:
                    acc = acc + k * grad_rowsum
        for s in range(BLOCKS):
            total = row(rs_ref, ITERS - 1, s) * col_ref[ITERS - 1, here, :] * grad_plan(s, row(u_ref, 0, s))
            for t in range(ITERS):
                total = total + row(rs_ref, t, s) * gt_ref[t]
                if t > 0:
                    total = total + row(grs_ref, t, s) * col_ref[t - 1, here, :]
                else:
                    total = total + row(grs_ref, t, s)
            gs_ref[here, s * rows : (s + 1) * rows] = (score_scale * total * load(s)).astype(bf16)


def parts_kernel(
    width, gs_ref, grads_ref, m_ref, wt_ref, raw_ref, plan_ref, refs_ref,
    p0, p1, p2, p3, other_ref, left_ref, right_ref, wide_ref,
):
    rows = other_ref.shape[2]
    part = raw_ref.shape[1]
    size = float(P_SIZE)
    grads = grads_ref[...]
    place = lax.axis_index("y") * SIDE + lax.axis_index("x")
    pair = refs_ref[:, pl.ds(pl.multiple_of((place // 2) * (2 * part), 2 * part), 2 * part)]
    left_ref[:REFS, :] = jnp.where(lax.rem(place, 2) == 0, pair[:, :part], pair[:, part:])
    for h in range(HEADS):
        here = slice(h * P_SIZE, (h + 1) * P_SIZE)
        inverse, pull = scales_of(grads, m_ref[h * PAD : (h + 1) * PAD, :], width)
        normed = jnp.sum(grads[:, :1] * wt_ref[h * PAD : (h + 1) * PAD, :].astype(f32), axis=0, keepdims=True) / size
        grad_raw = (inverse * (normed - raw_ref[here, :] * pull)).astype(bf16)
        left_ref[REFS + h * P_SIZE : REFS + (h + 1) * P_SIZE, :] = (size * grad_raw.astype(f32)).astype(bf16)
    right_ref[:REFS, :] = gs_ref[...]
    right_ref[REFS:, :] = plan_ref[...]
    wide_ref[...] = lax.dot_general(left_ref[...], right_ref[...], TN, preferred_element_type=f32)
    core, z = lax.axis_index("core"), lax.axis_index("z")
    outs = (p0, p1, p2, p3)

    def take(step, which):
        block = lax.bitwise_xor(2 * lax.rem(z + step, DEPTH) + which, place)
        return wide_ref[:, lanes(block, rows)].astype(bf16)

    for k in range(4):
        for b in range(2):
            step = jnp.where(core == 0, CHIPS[0][k], CHIPS[1][k]) + 4 * b
            outs[k][b] = take(step, core)
            step = jnp.where(core == 0, CHIPS[1][k], CHIPS[0][k]) + 4 * b
            other_ref[2 * k + b] = take(step, 1 - core)


def cores_kernel(p0, p1, p2, p3, other_ref, o0, o1, o2, o3):
    for k, (part, out) in enumerate(zip((p0, p1, p2, p3), (o0, o1, o2, o3))):
        for b in range(2):
            out[b] = (part[b].astype(f32) + other_ref[2 * k + b].astype(f32)).astype(bf16)


def chips_kernel(o0, o1, o2, o3, u0, u1):
    for b, out in enumerate((u0, u1)):
        total = o0[b].astype(f32) + o1[b].astype(f32) + o2[b].astype(f32) + o3[b].astype(f32)
        out[...] = total.astype(bf16)


def last_kernel(u0, u1, out_ref):
    out_ref[...] = u0[...].astype(f32) + u1[...].astype(f32)


def references_kernel(gs_ref, mixed_ref, other_ref, out_ref, fc_ref):
    put_columns(mixed_ref, other_ref, fc_ref)
    for h in range(HEADS):
        heads = gs_ref[h * P_SIZE : (h + 1) * P_SIZE, :]
        out_ref[h] = lax.dot_general(fc_ref[...], heads, NT, preferred_element_type=f32)


def along_z(value, k):
    pairs = []
    for z in range(DEPTH):
        for core in range(2):
            pairs.append((2 * z + core, 2 * ((z + CHIPS[core][k]) % DEPTH) + core))
    return lax.ppermute(value, ("z", "core"), pairs)


def to_place(value, b):
    pairs = []
    for z in range(DEPTH):
        for core in range(2):
            for j in range(BLOCKS):
                block = (2 * ((z + 4 * b) % DEPTH) + core) ^ j
                pairs.append(((2 * z + core) * BLOCKS + j, j * BLOCKS + block))
    return lax.ppermute(value, ("z", "core", "y", "x"), pairs)


def spread_logits(value):
    pairs = [((s + j) % BLOCKS * BLOCKS + j, s * BLOCKS + j) for s in range(BLOCKS) for j in range(BLOCKS)]
    return lax.ppermute(value, ("z", "core", "y", "x"), pairs)


def local(features, references, classifier, lengths, labels):
    batch, rows, width = features.shape
    part = width // BLOCKS
    everything = BLOCKS * rows
    score_scale = temper / math.sqrt(width)
    feats = features.reshape(rows, width)
    refs = references.reshape(REFS, width)
    kind = jax.ShapeDtypeStruct

    half = part // 2
    halves = kind((BLOCKS, half, rows), bf16)
    split = call(split_kernel, "split", halves, 1, scratch=[pltpu.VMEM((width, rows), bf16)])(feats)
    mixed = call(
        functools.partial(scores_kernel, score_scale), "scores", kind((BLOCKS, half + REFS, rows), bf16), 3
    )(feats, refs, split)
    mixed = exchange(mixed)
    other = lax.ppermute(call(peel_kernel, "peel", halves, 1)(mixed), "core", [(0, 1), (1, 0)])
    weights = jnp.pad(jnp.transpose(classifier, (0, 2, 1)), ((0, 0), (0, PAD - CLASSES), (0, 0)))
    weights = weights.reshape(HEADS * PAD, part)

    scales = kind((ITERS * HEADS * BLOCKS, rows), f32)
    rs, rt, col, plan = call(
        sinkhorn_kernel, "sinkhorn",
        [scales, scales, kind((ITERS, REFS, rows), f32), kind((REFS, everything), bf16)], [VMEM, SMEM, SMEM],
    )(mixed, lengths, labels)
    products, raw = call(
        forward_kernel, "forward",
        [kind((BLOCKS, T_ROWS + M_ROWS, rows), bf16), kind((REFS, part), f32)], 4,
        scratch=[pltpu.VMEM((part, everything), bf16), pltpu.VMEM((T_ROWS, part), bf16)],
    )(mixed, other, weights, plan)
    t, moments, logit_part = call(
        functools.partial(sum_kernel, width), "sum",
        [kind((T_ROWS, rows), bf16), kind((HEADS * PAD, P_SIZE), f32), kind((PAD, P_SIZE), f32)], 1,
    )(exchange(products))
    ts = exchange(
        call(row_kernel, "row", kind((BLOCKS, T_ROWS + PAD, rows), bf16), 2)(t, spread_logits(logit_part))
    )
    pair = kind((2, part, rows), bf16)
    logits, grads, grad_scores = call(
        functools.partial(backward_kernel, width, score_scale), "backward",
        [kind((1, PAD), f32), kind((PAD, P_SIZE), f32), kind((REFS, everything), bf16)],
        [VMEM] * 6 + [SMEM],
        scratch=[
            pltpu.VMEM((ITERS, P_SIZE, rows), f32),
            pltpu.VMEM((ITERS * HEADS * BLOCKS, rows), f32),
            pltpu.VMEM((HEADS * BLOCKS, rows), f32),
        ],
    )(mixed, ts, rs, rt, col, moments, labels)
    *mine, away = call(
        functools.partial(parts_kernel, width), "parts", [pair] * 4 + [kind((DEPTH, part, rows), bf16)], 7,
        scratch=[
            pltpu.VMEM((2 * REFS, part), bf16),
            pltpu.VMEM((2 * REFS, everything), bf16),
            pltpu.VMEM((part, everything), f32),
        ],
        mib=12,
    )(grad_scores, grads, moments, weights, raw, plan, refs)
    away = lax.ppermute(away, "core", [(0, 1), (1, 0)])
    o = call(cores_kernel, "cores", [pair] * 4, 5)(*mine, away)
    o = [o[0]] + [along_z(o[k], k) for k in (1, 2, 3)]
    u = call(chips_kernel, "chips", [kind((part, rows), bf16)] * 2, 4)(*o)
    u = [to_place(u[b], b) for b in range(2)]
    grad_features = call(last_kernel, "last", kind((part, rows), f32), 2)(*u)
    grad_references = call(
        references_kernel, "references", kind((HEADS, part, rows), f32), 3,
        scratch=[pltpu.VMEM((part, everything), bf16)], flops=2 * REFS * part * everything,
    )(grad_scores, mixed, other)
    return (
        logits[:, :CLASSES],
        jnp.transpose(grad_features).reshape(batch, rows, part),
        jnp.transpose(grad_references, (0, 2, 1)),
    )


def solution(mesh):
    grid = Mesh(mesh.devices.reshape(DEPTH, 2, SIDE, SIDE), ("z", "core", "y", "x"))
    section, seq = ("z", "core"), ("y", "x")
    in_specs = (P(None, seq, None), P(section, None, None), P(section, seq, None), P(), P())
    out_specs = (P(), P(None, seq, section), P(section, None, seq))
    return jax.shard_map(local, mesh=grid, in_specs=in_specs, out_specs=out_specs, check_vma=False)
```

```python
import functools
import math

import jax
import jax.numpy as jnp
from jax import lax
from jax.experimental import pallas as pl
from jax.experimental.pallas import tpu as pltpu
from jax.sharding import Mesh, PartitionSpec as P

P_SIZE = 128
ITERS = 3
CLASSES = 10
PAD = 16
HEADS = 2
REFS = HEADS * P_SIZE

temper = 1.5
epsilon = 1e-06
loss_scale = 65536.0
f32 = jnp.float32
bf16 = jnp.bfloat16

SIDE = 4
DEPTH = 8
BLOCKS = SIDE * SIDE
CHIPS = ((0, 1, 7, 2), (0, 1, 7, 6))
T_ROWS = REFS + HEADS * PAD
MOVE = 4
M_ROWS = PAD
VMEM = pl.BlockSpec(memory_space=pltpu.VMEM)
HBM = pl.BlockSpec(memory_space=pltpu.HBM)
SMEM = pl.BlockSpec(memory_space=pltpu.SMEM)
NT = (((1,), (1,)), ((), ()))
TN = (((0,), (0,)), ((), ()))


def call(kernel, name, shapes, specs, scratch=(), flops=0, mib=8):
    many = isinstance(shapes, list)
    return pl.pallas_call(
        kernel,
        out_shape=shapes,
        in_specs=[VMEM] * specs if isinstance(specs, int) else specs,
        out_specs=[VMEM] * len(shapes) if many else VMEM,
        scratch_shapes=list(scratch),
        compiler_params=pltpu.CompilerParams(vmem_limit_bytes=mib * 1024 * 1024),
        cost_estimate=pl.CostEstimate(flops=flops, bytes_accessed=1 << 20, transcendentals=0) if flops else None,
        name=name,
    )


def lanes(block, rows):
    return pl.ds(pl.multiple_of(block * rows, rows), rows)


def exchange(value):
    return lax.all_to_all(value, ("y", "x"), 0, 0)


def scores_kernel(scale, f_ref, r_hbm, out_ref, r_ref, turned_ref, sems):
    half = out_ref.shape[1] - REFS
    part = 2 * half
    steps, rows = r_ref.shape[:2]
    loads = []
    for k in range(steps):
        loads.append(pltpu.make_async_copy(r_hbm.at[pl.ds(k * rows, rows)], r_ref.at[k], sems.at[k]))
        loads[k].start()
    for j in range(BLOCKS // 2):
        where = slice(2 * part * j, 2 * part * (j + 1))
        turned_ref[where, :] = jnp.transpose(f_ref[:, where])
    core = lax.axis_index("core")
    for j in range(BLOCKS):
        out_ref[j, :half, :] = turned_ref[pl.ds(pl.multiple_of(part * j + half * core, half), half), :]
    for k in range(steps):
        loads[k].wait()
        scores = lax.dot_general(r_ref[k], f_ref[...], NT, preferred_element_type=f32)
        kernel = jnp.exp(scores * scale).astype(bf16)
        for j in range(BLOCKS):
            out_ref[j, half + k * rows : half + (k + 1) * rows, :] = kernel


def peel_kernel(in_ref, out_ref):
    half = out_ref.shape[1]
    for j in range(BLOCKS):
        out_ref[j] = in_ref[j, :half, :]


def put_columns(mixed_ref, other_ref, out_ref):
    core = lax.axis_index("core")
    half, rows = other_ref.shape[1:]
    for j in range(BLOCKS):
        here = slice(j * rows, (j + 1) * rows)
        out_ref[pl.ds(pl.multiple_of(core * half, half), half), here] = mixed_ref[j, :half, :]
        out_ref[pl.ds(pl.multiple_of((1 - core) * half, half), half), here] = other_ref[j]


def diagonal():
    square = (P_SIZE, P_SIZE)
    return lax.broadcasted_iota(jnp.int32, square, 0) == lax.broadcasted_iota(jnp.int32, square, 1)


def to_row(column):
    return jnp.sum(jnp.where(diagonal(), column, 0.0), axis=0, keepdims=True)


def to_column(row):
    return jnp.sum(jnp.where(diagonal(), row, 0.0), axis=1, keepdims=True)


def sinkhorn_kernel(q_ref, len_ref, label_ref, rs_ref, rt_ref, col_ref, plan_ref):
    length = len_ref[0]
    rows = q_ref.shape[2]
    low = q_ref.shape[1] - REFS
    mass = 1.0 / (jnp.zeros((1, rows), jnp.int32) + length).astype(f32)
    lane = lax.broadcasted_iota(jnp.int32, (1, rows), 1)
    masses = [jnp.where(s * rows + lane < length, mass, 0.0) for s in range(BLOCKS)]
    for t in range(ITERS):
        for h in range(HEADS):
            here = slice(h * P_SIZE, (h + 1) * P_SIZE)
            acc = jnp.zeros((P_SIZE, rows), f32)
            for s in range(BLOCKS):
                k = q_ref[s, low + h * P_SIZE : low + (h + 1) * P_SIZE, :].astype(f32)
                weighted = k if t == 0 else k * col_ref[t - 1, here, :]
                total = jnp.sum(weighted, axis=0, keepdims=True)
                scale = masses[s] / total
                place = (t * HEADS + h) * BLOCKS + s
                rt_ref[place : place + 1, :] = total
                rs_ref[place : place + 1, :] = scale
                acc = acc + k * scale
            col = 1.0 / (float(P_SIZE) * jnp.sum(acc, axis=1, keepdims=True))
            col_ref[t, here, :] = jnp.broadcast_to(col, (P_SIZE, rows))
    for h in range(HEADS):
        here = slice(h * P_SIZE, (h + 1) * P_SIZE)
        for s in range(BLOCKS):
            k = q_ref[s, low + h * P_SIZE : low + (h + 1) * P_SIZE, :].astype(f32)
            place = ((ITERS - 1) * HEADS + h) * BLOCKS + s
            plan = rs_ref[place : place + 1, :] * k * col_ref[ITERS - 1, here, :]
            plan_ref[here, s * rows : (s + 1) * rows] = plan.astype(bf16)


def forward_kernel(mixed_ref, other_ref, wt_ref, plan_ref, out_ref, raw_ref, fc_ref, ext_ref):
    rows = other_ref.shape[2]
    put_columns(mixed_ref, other_ref, fc_ref)
    raw = float(P_SIZE) * lax.dot_general(plan_ref[...], fc_ref[...], NT, preferred_element_type=f32)
    raw_ref[...] = raw
    ext_ref[:REFS, :] = raw.astype(bf16)
    ext_ref[REFS:, :] = wt_ref[...]
    tails, heads = [], []
    for h in range(HEADS):
        here = slice(h * P_SIZE, (h + 1) * P_SIZE)
        squares = jnp.sum(raw_ref[here, :] * raw_ref[here, :], axis=1, keepdims=True)
        products = lax.dot_general(
            wt_ref[h * PAD : (h + 1) * PAD, :], ext_ref[here, :], NT, preferred_element_type=f32
        )
        kind = lax.broadcasted_iota(jnp.int32, products.shape, 0)
        moments = jnp.where(kind == CLASSES, to_row(squares), products)
        heads.append(moments[:8])
        tails.append(pltpu.roll(moments, MOVE, 0))
    first = jnp.concatenate(heads, axis=0).astype(bf16)
    for i in range(4):
        wide = jnp.dot(
            ext_ref[...], fc_ref[:, 4 * i * rows : 4 * (i + 1) * rows], preferred_element_type=f32
        )
        for k in range(4):
            here = slice(k * rows, (k + 1) * rows)
            out_ref[4 * i + k, :REFS, :] = wide[:REFS, here].astype(bf16)
            for h in range(HEADS):
                low = REFS + h * PAD
                value = jnp.where(kind < CLASSES, wide[low : low + PAD, here], tails[h])
                out_ref[4 * i + k, low : low + PAD, :] = value.astype(bf16)
            out_ref[4 * i + k, T_ROWS:, :] = first


def add_blocks(ref, low, high):
    total = ref[0, low:high, :].astype(f32)
    for j in range(1, BLOCKS):
        total = total + ref[j, low:high, :].astype(f32)
    return total


def inverse_rms(moments, width):
    return lax.rsqrt(moments[CLASSES : CLASSES + 1, :] / width + epsilon)


def sixteen():
    square = (PAD, PAD)
    return lax.broadcasted_iota(jnp.int32, square, 0) == lax.broadcasted_iota(jnp.int32, square, 1)


def sum_kernel(width, in_ref, t_ref, m_ref, logit_ref):
    logits = jnp.zeros((PAD, 1), f32)
    first = add_blocks(in_ref, T_ROWS, T_ROWS + M_ROWS)
    for h in range(HEADS):
        low = REFS + h * PAD
        block = add_blocks(in_ref, low, low + PAD)
        t_ref[low : low + PAD, :] = block.astype(bf16)
        kind = lax.broadcasted_iota(jnp.int32, block.shape, 0)
        head = first if h == 0 else pltpu.roll(first, 8, 0)
        moments = jnp.where(kind < 8, head, jnp.where(kind <= CLASSES, pltpu.roll(block, PAD - MOVE, 0), 0.0))
        m_ref[h * PAD : (h + 1) * PAD, :] = moments
        part = jnp.sum(inverse_rms(moments, width) * moments, axis=1, keepdims=True)
        logits = logits + part / P_SIZE
    row = jnp.sum(jnp.where(sixteen(), logits, 0.0), axis=0, keepdims=True)
    logit_ref[...] = jnp.broadcast_to(row, logit_ref.shape)
    for low in range(0, REFS, 64):
        t_ref[low : low + 64, :] = add_blocks(in_ref, low, low + 64).astype(bf16)


def row_kernel(t_ref, logit_ref, out_ref):
    logits = logit_ref[...]
    high = logits.astype(bf16).astype(f32)
    low = REFS + PAD
    kind = lax.broadcasted_iota(jnp.int32, logits.shape, 0)
    block = t_ref[REFS:low, :PAD].astype(f32)
    block = jnp.where(kind == CLASSES, high, jnp.where(kind == CLASSES + 1, logits - high, block)).astype(bf16)
    for j in range(BLOCKS):
        out_ref[j] = t_ref[...]
        out_ref[j, REFS:low, :PAD] = block


def sum_logits(ref):
    section = 2 * lax.axis_index("z") + lax.axis_index("core")
    total = jnp.zeros((PAD, PAD), f32)
    for other in range(BLOCKS):
        total = total + ref[lax.rem(other + BLOCKS - section, BLOCKS), REFS : REFS + PAD, :PAD].astype(f32)
    return total[CLASSES : CLASSES + 1] + total[CLASSES + 1 : CLASSES + 2]


def scales_of(grads, moments, width):
    inverse = inverse_rms(moments, width)
    dual = inverse * jnp.sum(grads * moments, axis=0, keepdims=True) / (float(P_SIZE) * width)
    return to_column(inverse), to_column(inverse * dual)


def backward_kernel(
    width, score_scale,
    q_ref, t_ref, rs_ref, rt_ref, col_ref, m_ref, label_ref,
    logit_ref, grads_ref, gs_ref, gt_ref, grs_ref, u_ref,
):
    rows = q_ref.shape[2]
    base = q_ref.shape[1] - REFS
    size = float(P_SIZE)
    logits = sum_logits(t_ref)
    logit_ref[...] = logits
    logits = jnp.sum(jnp.where(sixteen(), logits, 0.0), axis=1, keepdims=True)
    logits = jnp.broadcast_to(logits, (PAD, P_SIZE))
    kind = lax.broadcasted_iota(jnp.int32, logits.shape, 0)
    exps = jnp.where(kind < CLASSES, jnp.exp(logits), 0.0)
    probs = exps / jnp.sum(exps, axis=0, keepdims=True)
    grads = loss_scale * (probs - (kind == label_ref[0]).astype(f32))
    grads = jnp.where(kind < CLASSES, grads, 0.0)
    grads_ref[...] = grads
    for h in range(HEADS):
        here = slice(h * P_SIZE, (h + 1) * P_SIZE)
        inverse, pull = scales_of(grads, m_ref[h * PAD : (h + 1) * PAD, :], width)
        first = jnp.broadcast_to(size * inverse, (P_SIZE, rows))
        second = first * pull

        def load(s):
            return q_ref[s, base + h * P_SIZE : base + (h + 1) * P_SIZE, :].astype(f32)

        def grad_plan(s, u):
            return first * u - second * t_ref[s, here, :].astype(f32)

        def row(ref, t, s):
            place = (t * HEADS + h) * BLOCKS + s
            return ref[place : place + 1, :]

        def put(ref, t, s, value):
            place = (t * HEADS + h) * BLOCKS + s
            ref[place : place + 1, :] = value

        acc = jnp.zeros((P_SIZE, rows), f32)
        for s in range(BLOCKS):
            v = t_ref[s, REFS + h * PAD : REFS + (h + 1) * PAD, :].astype(f32)
            u = jnp.sum(grads * v, axis=0, keepdims=True) / size
            put(u_ref, 0, s, u)
            weighted = grad_plan(s, u) * load(s)
            put(grs_ref, ITERS - 1, s, jnp.sum(weighted * col_ref[ITERS - 1, here, :], axis=0, keepdims=True))
            acc = acc + weighted * row(rs_ref, ITERS - 1, s)
        for t in reversed(range(ITERS)):
            grad_col = jnp.sum(acc, axis=1, keepdims=True)
            gt_ref[t] = -size * col_ref[t, here, :] ** 2 * grad_col
            acc = jnp.zeros((P_SIZE, rows), f32)
            for s in range(BLOCKS):
                k = load(s)
                grad_row = jnp.sum(k * gt_ref[t], axis=0, keepdims=True)
                if t == ITERS - 1:
                    grad_row = grad_row + row(grs_ref, t, s)
                grad_rowsum = -grad_row * row(rs_ref, t, s) / row(rt_ref, t, s)
                put(grs_ref, t, s, grad_rowsum)
                if t > 0:
                    acc = acc + k * grad_rowsum
        for s in range(BLOCKS):
            total = row(rs_ref, ITERS - 1, s) * col_ref[ITERS - 1, here, :] * grad_plan(s, row(u_ref, 0, s))
            for t in range(ITERS):
                total = total + row(rs_ref, t, s) * gt_ref[t]
                if t > 0:
                    total = total + row(grs_ref, t, s) * col_ref[t - 1, here, :]
                else:
                    total = total + row(grs_ref, t, s)
            gs_ref[here, s * rows : (s + 1) * rows] = (score_scale * total * load(s)).astype(bf16)


def parts_kernel(
    width, gs_ref, grads_ref, m_ref, wt_ref, raw_ref, plan_ref, refs_ref,
    p0, p1, p2, p3, other_ref, left_ref, right_ref, wide_ref,
):
    rows = other_ref.shape[2]
    part = raw_ref.shape[1]
    size = float(P_SIZE)
    grads = grads_ref[...]
    place = lax.axis_index("y") * SIDE + lax.axis_index("x")
    pair = refs_ref[:, pl.ds(pl.multiple_of((place // 2) * (2 * part), 2 * part), 2 * part)]
    left_ref[:REFS, :] = jnp.where(lax.rem(place, 2) == 0, pair[:, :part], pair[:, part:])
    for h in range(HEADS):
        here = slice(h * P_SIZE, (h + 1) * P_SIZE)
        inverse, pull = scales_of(grads, m_ref[h * PAD : (h + 1) * PAD, :], width)
        normed = jnp.sum(grads[:, :1] * wt_ref[h * PAD : (h + 1) * PAD, :].astype(f32), axis=0, keepdims=True) / size
        grad_raw = (inverse * (normed - raw_ref[here, :] * pull)).astype(bf16)
        left_ref[REFS + h * P_SIZE : REFS + (h + 1) * P_SIZE, :] = (size * grad_raw.astype(f32)).astype(bf16)
    right_ref[:REFS, :] = gs_ref[...]
    right_ref[REFS:, :] = plan_ref[...]
    wide_ref[...] = lax.dot_general(left_ref[...], right_ref[...], TN, preferred_element_type=f32)
    core, z = lax.axis_index("core"), lax.axis_index("z")
    outs = (p0, p1, p2, p3)

    def take(step, which):
        block = lax.bitwise_xor(2 * lax.rem(z + step, DEPTH) + which, place)
        return wide_ref[:, lanes(block, rows)].astype(bf16)

    for k in range(4):
        for b in range(2):
            step = jnp.where(core == 0, CHIPS[0][k], CHIPS[1][k]) + 4 * b
            outs[k][b] = take(step, core)
            step = jnp.where(core == 0, CHIPS[1][k], CHIPS[0][k]) + 4 * b
            other_ref[2 * k + b] = take(step, 1 - core)


def cores_kernel(p0, p1, p2, p3, other_ref, o0, o1, o2, o3):
    for k, (part, out) in enumerate(zip((p0, p1, p2, p3), (o0, o1, o2, o3))):
        for b in range(2):
            out[b] = (part[b].astype(f32) + other_ref[2 * k + b].astype(f32)).astype(bf16)


def chips_kernel(o0, o1, o2, o3, u0, u1):
    for b, out in enumerate((u0, u1)):
        total = o0[b].astype(f32) + o1[b].astype(f32) + o2[b].astype(f32) + o3[b].astype(f32)
        out[...] = total.astype(bf16)


def last_kernel(u0, u1, out_ref):
    out_ref[...] = u0[...].astype(f32) + u1[...].astype(f32)


def references_kernel(gs_ref, mixed_ref, other_ref, out_ref, fc_ref):
    put_columns(mixed_ref, other_ref, fc_ref)
    for h in range(HEADS):
        heads = gs_ref[h * P_SIZE : (h + 1) * P_SIZE, :]
        out_ref[h] = lax.dot_general(fc_ref[...], heads, NT, preferred_element_type=f32)


def along_z(value, k):
    pairs = []
    for z in range(DEPTH):
        for core in range(2):
            pairs.append((2 * z + core, 2 * ((z + CHIPS[core][k]) % DEPTH) + core))
    return lax.ppermute(value, ("z", "core"), pairs)


def to_place(value, b):
    pairs = []
    for z in range(DEPTH):
        for core in range(2):
            for j in range(BLOCKS):
                block = (2 * ((z + 4 * b) % DEPTH) + core) ^ j
                pairs.append(((2 * z + core) * BLOCKS + j, j * BLOCKS + block))
    return lax.ppermute(value, ("z", "core", "y", "x"), pairs)


def spread_logits(value):
    pairs = [((s + j) % BLOCKS * BLOCKS + j, s * BLOCKS + j) for s in range(BLOCKS) for j in range(BLOCKS)]
    return lax.ppermute(value, ("z", "core", "y", "x"), pairs)


def local(features, references, classifier, lengths, labels):
    batch, rows, width = features.shape
    part = width // BLOCKS
    everything = BLOCKS * rows
    score_scale = temper / math.sqrt(width)
    feats = features.reshape(rows, width)
    refs = references.reshape(REFS, width)
    kind = jax.ShapeDtypeStruct

    half = part // 2
    halves = kind((BLOCKS, half, rows), bf16)
    steps = 4
    mixed = call(
        functools.partial(scores_kernel, score_scale), "scores", kind((BLOCKS, half + REFS, rows), bf16), [VMEM, HBM],
        scratch=[
            pltpu.VMEM((steps, REFS // steps, width), bf16), pltpu.VMEM((width, rows), bf16),
            pltpu.SemaphoreType.DMA((steps,)),
        ],
        mib=60,
    )(feats, refs)
    mixed = exchange(mixed)
    other = lax.ppermute(call(peel_kernel, "peel", halves, 1)(mixed), "core", [(0, 1), (1, 0)])
    weights = jnp.pad(jnp.transpose(classifier, (0, 2, 1)), ((0, 0), (0, PAD - CLASSES), (0, 0)))
    weights = weights.reshape(HEADS * PAD, part)

    scales = kind((ITERS * HEADS * BLOCKS, rows), f32)
    rs, rt, col, plan = call(
        sinkhorn_kernel, "sinkhorn",
        [scales, scales, kind((ITERS, REFS, rows), f32), kind((REFS, everything), bf16)], [VMEM, SMEM, SMEM],
    )(mixed, lengths, labels)
    products, raw = call(
        forward_kernel, "forward",
        [kind((BLOCKS, T_ROWS + M_ROWS, rows), bf16), kind((REFS, part), f32)], 4,
        scratch=[pltpu.VMEM((part, everything), bf16), pltpu.VMEM((T_ROWS, part), bf16)],
    )(mixed, other, weights, plan)
    t, moments, logit_part = call(
        functools.partial(sum_kernel, width), "sum",
        [kind((T_ROWS, rows), bf16), kind((HEADS * PAD, P_SIZE), f32), kind((PAD, PAD), f32)], 1,
    )(exchange(products))
    ts = exchange(
        call(row_kernel, "row", kind((BLOCKS, T_ROWS, rows), bf16), 2)(t, spread_logits(logit_part))
    )
    pair = kind((2, part, rows), bf16)
    logits, grads, grad_scores = call(
        functools.partial(backward_kernel, width, score_scale), "backward",
        [kind((1, PAD), f32), kind((PAD, P_SIZE), f32), kind((REFS, everything), bf16)],
        [VMEM] * 6 + [SMEM],
        scratch=[
            pltpu.VMEM((ITERS, P_SIZE, rows), f32),
            pltpu.VMEM((ITERS * HEADS * BLOCKS, rows), f32),
            pltpu.VMEM((HEADS * BLOCKS, rows), f32),
        ],
    )(mixed, ts, rs, rt, col, moments, labels)
    *mine, away = call(
        functools.partial(parts_kernel, width), "parts", [pair] * 4 + [kind((DEPTH, part, rows), bf16)], 7,
        scratch=[
            pltpu.VMEM((2 * REFS, part), bf16),
            pltpu.VMEM((2 * REFS, everything), bf16),
            pltpu.VMEM((part, everything), f32),
        ],
        mib=12,
    )(grad_scores, grads, moments, weights, raw, plan, refs)
    away = lax.ppermute(away, "core", [(0, 1), (1, 0)])
    o = call(cores_kernel, "cores", [pair] * 4, 5)(*mine, away)
    o = [o[0]] + [along_z(o[k], k) for k in (1, 2, 3)]
    u = call(chips_kernel, "chips", [kind((part, rows), bf16)] * 2, 4)(*o)
    u = [to_place(u[b], b) for b in range(2)]
    grad_features = call(last_kernel, "last", kind((part, rows), f32), 2)(*u)
    grad_references = call(
        references_kernel, "references", kind((HEADS, part, rows), f32), 3,
        scratch=[pltpu.VMEM((part, everything), bf16)], flops=2 * REFS * part * everything,
    )(grad_scores, mixed, other)
    return (
        logits[:, :CLASSES],
        jnp.transpose(grad_features).reshape(batch, rows, part),
        jnp.transpose(grad_references, (0, 2, 1)),
    )


def solution(mesh):
    grid = Mesh(mesh.devices.reshape(DEPTH, 2, SIDE, SIDE), ("z", "core", "y", "x"))
    section, seq = ("z", "core"), ("y", "x")
    in_specs = (P(None, seq, None), P(section, None, None), P(section, seq, None), P(), P())
    out_specs = (P(), P(None, seq, section), P(section, None, seq))
    return jax.shard_map(local, mesh=grid, in_specs=in_specs, out_specs=out_specs, check_vma=False)
```

```python
import functools
import math

import jax
import jax.numpy as jnp
from jax import lax
from jax.experimental import pallas as pl
from jax.experimental.pallas import tpu as pltpu
from jax.sharding import Mesh, PartitionSpec as P

P_SIZE = 128
ITERS = 3
CLASSES = 10
PAD = 16
HEADS = 2
REFS = HEADS * P_SIZE

temper = 1.5
epsilon = 1e-06
loss_scale = 65536.0
f32 = jnp.float32
bf16 = jnp.bfloat16

SIDE = 4
DEPTH = 8
BLOCKS = SIDE * SIDE
CHIPS = ((0, 1, 7, 2), (0, 1, 7, 6))
T_ROWS = REFS + HEADS * PAD
MOVE = 4
M_ROWS = PAD
VMEM = pl.BlockSpec(memory_space=pltpu.VMEM)
SMEM = pl.BlockSpec(memory_space=pltpu.SMEM)
NT = (((1,), (1,)), ((), ()))
TN = (((0,), (0,)), ((), ()))


def call(kernel, name, shapes, specs, scratch=(), flops=0, mib=8):
    many = isinstance(shapes, list)
    return pl.pallas_call(
        kernel,
        out_shape=shapes,
        in_specs=[VMEM] * specs if isinstance(specs, int) else specs,
        out_specs=[VMEM] * len(shapes) if many else VMEM,
        scratch_shapes=list(scratch),
        compiler_params=pltpu.CompilerParams(vmem_limit_bytes=mib * 1024 * 1024),
        cost_estimate=pl.CostEstimate(flops=flops, bytes_accessed=1 << 20, transcendentals=0) if flops else None,
        name=name,
    )


def lanes(block, rows):
    return pl.ds(pl.multiple_of(block * rows, rows), rows)


def exchange(value):
    return lax.all_to_all(value, ("x", "y"), 0, 0)


def at(j):
    return j % SIDE * SIDE + j // SIDE


def split_kernel(f_ref, out_ref, turned_ref):
    half = out_ref.shape[1]
    part = 2 * half
    for j in range(BLOCKS // 2):
        where = slice(2 * part * j, 2 * part * (j + 1))
        turned_ref[where, :] = jnp.transpose(f_ref[:, where])
    core = lax.axis_index("core")
    for j in range(BLOCKS):
        out_ref[at(j)] = turned_ref[pl.ds(pl.multiple_of(part * j + half * core, half), half), :]


def scores_kernel(scale, f_ref, r_ref, half_ref, out_ref):
    half = half_ref.shape[1]
    scores = lax.dot_general(r_ref[...], f_ref[...], NT, preferred_element_type=f32)
    kernel = jnp.exp(scores * scale).astype(bf16)
    for j in range(BLOCKS):
        out_ref[j, :half, :] = half_ref[j]
        out_ref[j, half:, :] = kernel


def peel_kernel(in_ref, out_ref):
    half = out_ref.shape[1]
    for j in range(BLOCKS):
        out_ref[j] = in_ref[j, :half, :]


def put_columns(mixed_ref, other_ref, out_ref):
    core = lax.axis_index("core")
    half, rows = other_ref.shape[1:]
    for j in range(BLOCKS):
        here = slice(j * rows, (j + 1) * rows)
        out_ref[pl.ds(pl.multiple_of(core * half, half), half), here] = mixed_ref[at(j), :half, :]
        out_ref[pl.ds(pl.multiple_of((1 - core) * half, half), half), here] = other_ref[at(j)]


def diagonal():
    square = (P_SIZE, P_SIZE)
    return lax.broadcasted_iota(jnp.int32, square, 0) == lax.broadcasted_iota(jnp.int32, square, 1)


def to_row(column):
    return jnp.sum(jnp.where(diagonal(), column, 0.0), axis=0, keepdims=True)


def to_column(row):
    return jnp.sum(jnp.where(diagonal(), row, 0.0), axis=1, keepdims=True)


def sinkhorn_kernel(q_ref, len_ref, label_ref, rs_ref, rt_ref, col_ref, plan_ref):
    length = len_ref[0]
    rows = q_ref.shape[2]
    low = q_ref.shape[1] - REFS
    mass = 1.0 / (jnp.zeros((1, rows), jnp.int32) + length).astype(f32)
    lane = lax.broadcasted_iota(jnp.int32, (1, rows), 1)
    masses = [jnp.where(s * rows + lane < length, mass, 0.0) for s in range(BLOCKS)]
    for t in range(ITERS):
        for h in range(HEADS):
            here = slice(h * P_SIZE, (h + 1) * P_SIZE)
            acc = jnp.zeros((P_SIZE, rows), f32)
            for s in range(BLOCKS):
                k = q_ref[at(s), low + h * P_SIZE : low + (h + 1) * P_SIZE, :].astype(f32)
                weighted = k if t == 0 else k * col_ref[t - 1, here, :]
                total = jnp.sum(weighted, axis=0, keepdims=True)
                scale = masses[s] / total
                place = (t * HEADS + h) * BLOCKS + s
                rt_ref[place : place + 1, :] = total
                rs_ref[place : place + 1, :] = scale
                acc = acc + k * scale
            col = 1.0 / (float(P_SIZE) * jnp.sum(acc, axis=1, keepdims=True))
            col_ref[t, here, :] = jnp.broadcast_to(col, (P_SIZE, rows))
    for h in range(HEADS):
        here = slice(h * P_SIZE, (h + 1) * P_SIZE)
        for s in range(BLOCKS):
            k = q_ref[at(s), low + h * P_SIZE : low + (h + 1) * P_SIZE, :].astype(f32)
            place = ((ITERS - 1) * HEADS + h) * BLOCKS + s
            plan = rs_ref[place : place + 1, :] * k * col_ref[ITERS - 1, here, :]
            plan_ref[here, s * rows : (s + 1) * rows] = plan.astype(bf16)


def forward_kernel(mixed_ref, other_ref, wt_ref, plan_ref, out_ref, raw_ref, fc_ref, ext_ref):
    rows = other_ref.shape[2]
    put_columns(mixed_ref, other_ref, fc_ref)
    raw = float(P_SIZE) * lax.dot_general(plan_ref[...], fc_ref[...], NT, preferred_element_type=f32)
    raw_ref[...] = raw
    ext_ref[:REFS, :] = raw.astype(bf16)
    ext_ref[REFS:, :] = wt_ref[...]
    tails, heads = [], []
    for h in range(HEADS):
        here = slice(h * P_SIZE, (h + 1) * P_SIZE)
        squares = jnp.sum(raw_ref[here, :] * raw_ref[here, :], axis=1, keepdims=True)
        products = lax.dot_general(
            wt_ref[h * PAD : (h + 1) * PAD, :], ext_ref[here, :], NT, preferred_element_type=f32
        )
        kind = lax.broadcasted_iota(jnp.int32, products.shape, 0)
        moments = jnp.where(kind == CLASSES, to_row(squares), products)
        heads.append(moments[:8])
        tails.append(pltpu.roll(moments, MOVE, 0))
    first = jnp.concatenate(heads, axis=0).astype(bf16)
    for i in range(4):
        wide = jnp.dot(
            ext_ref[...], fc_ref[:, 4 * i * rows : 4 * (i + 1) * rows], preferred_element_type=f32
        )
        for k in range(4):
            here = slice(k * rows, (k + 1) * rows)
            out_ref[at(4 * i + k), :REFS, :] = wide[:REFS, here].astype(bf16)
            for h in range(HEADS):
                low = REFS + h * PAD
                value = jnp.where(kind < CLASSES, wide[low : low + PAD, here], tails[h])
                out_ref[at(4 * i + k), low : low + PAD, :] = value.astype(bf16)
            out_ref[at(4 * i + k), T_ROWS:, :] = first


def add_blocks(ref, low, high):
    total = ref[0, low:high, :].astype(f32)
    for j in range(1, BLOCKS):
        total = total + ref[j, low:high, :].astype(f32)
    return total


def inverse_rms(moments, width):
    return lax.rsqrt(moments[CLASSES : CLASSES + 1, :] / width + epsilon)


def sixteen():
    square = (PAD, PAD)
    return lax.broadcasted_iota(jnp.int32, square, 0) == lax.broadcasted_iota(jnp.int32, square, 1)


def sum_kernel(width, in_ref, t_ref, m_ref, logit_ref):
    logits = jnp.zeros((PAD, 1), f32)
    first = add_blocks(in_ref, T_ROWS, T_ROWS + M_ROWS)
    for h in range(HEADS):
        low = REFS + h * PAD
        block = add_blocks(in_ref, low, low + PAD)
        t_ref[low : low + PAD, :] = block.astype(bf16)
        kind = lax.broadcasted_iota(jnp.int32, block.shape, 0)
        head = first if h == 0 else pltpu.roll(first, 8, 0)
        moments = jnp.where(kind < 8, head, jnp.where(kind <= CLASSES, pltpu.roll(block, PAD - MOVE, 0), 0.0))
        m_ref[h * PAD : (h + 1) * PAD, :] = moments
        part = jnp.sum(inverse_rms(moments, width) * moments, axis=1, keepdims=True)
        logits = logits + part / P_SIZE
    row = jnp.sum(jnp.where(sixteen(), logits, 0.0), axis=0, keepdims=True)
    logit_ref[...] = jnp.broadcast_to(row, logit_ref.shape)
    for low in range(0, REFS, 64):
        t_ref[low : low + 64, :] = add_blocks(in_ref, low, low + 64).astype(bf16)


def row_kernel(t_ref, logit_ref, out_ref):
    logits = logit_ref[...]
    high = logits.astype(bf16).astype(f32)
    low = REFS + PAD
    kind = lax.broadcasted_iota(jnp.int32, logits.shape, 0)
    block = t_ref[REFS:low, :PAD].astype(f32)
    block = jnp.where(kind == CLASSES, high, jnp.where(kind == CLASSES + 1, logits - high, block)).astype(bf16)
    for j in range(BLOCKS):
        out_ref[j] = t_ref[...]
        out_ref[j, REFS:low, :PAD] = block


def sum_logits(ref):
    section = 2 * lax.axis_index("z") + lax.axis_index("core")
    total = jnp.zeros((PAD, PAD), f32)
    for other in range(BLOCKS):
        total = total + ref[at(lax.rem(other + BLOCKS - section, BLOCKS)), REFS : REFS + PAD, :PAD].astype(f32)
    return total[CLASSES : CLASSES + 1] + total[CLASSES + 1 : CLASSES + 2]


def scales_of(grads, moments, width):
    inverse = inverse_rms(moments, width)
    dual = inverse * jnp.sum(grads * moments, axis=0, keepdims=True) / (float(P_SIZE) * width)
    return to_column(inverse), to_column(inverse * dual)


def backward_kernel(
    width, score_scale,
    q_ref, t_ref, rs_ref, rt_ref, col_ref, m_ref, label_ref,
    logit_ref, grads_ref, gs_ref, gt_ref, grs_ref, u_ref,
):
    rows = q_ref.shape[2]
    base = q_ref.shape[1] - REFS
    size = float(P_SIZE)
    logits = sum_logits(t_ref)
    logit_ref[...] = logits
    logits = jnp.sum(jnp.where(sixteen(), logits, 0.0), axis=1, keepdims=True)
    logits = jnp.broadcast_to(logits, (PAD, P_SIZE))
    kind = lax.broadcasted_iota(jnp.int32, logits.shape, 0)
    exps = jnp.where(kind < CLASSES, jnp.exp(logits), 0.0)
    probs = exps / jnp.sum(exps, axis=0, keepdims=True)
    grads = loss_scale * (probs - (kind == label_ref[0]).astype(f32))
    grads = jnp.where(kind < CLASSES, grads, 0.0)
    grads_ref[...] = grads
    for h in range(HEADS):
        here = slice(h * P_SIZE, (h + 1) * P_SIZE)
        inverse, pull = scales_of(grads, m_ref[h * PAD : (h + 1) * PAD, :], width)
        first = jnp.broadcast_to(size * inverse, (P_SIZE, rows))
        second = first * pull

        def load(s):
            return q_ref[at(s), base + h * P_SIZE : base + (h + 1) * P_SIZE, :].astype(f32)

        def grad_plan(s, u):
            return first * u - second * t_ref[at(s), here, :].astype(f32)

        def row(ref, t, s):
            place = (t * HEADS + h) * BLOCKS + s
            return ref[place : place + 1, :]

        def put(ref, t, s, value):
            place = (t * HEADS + h) * BLOCKS + s
            ref[place : place + 1, :] = value

        acc = jnp.zeros((P_SIZE, rows), f32)
        for s in range(BLOCKS):
            v = t_ref[at(s), REFS + h * PAD : REFS + (h + 1) * PAD, :].astype(f32)
            u = jnp.sum(grads * v, axis=0, keepdims=True) / size
            put(u_ref, 0, s, u)
            weighted = grad_plan(s, u) * load(s)
            put(grs_ref, ITERS - 1, s, jnp.sum(weighted * col_ref[ITERS - 1, here, :], axis=0, keepdims=True))
            acc = acc + weighted * row(rs_ref, ITERS - 1, s)
        for t in reversed(range(ITERS)):
            grad_col = jnp.sum(acc, axis=1, keepdims=True)
            gt_ref[t] = -size * col_ref[t, here, :] ** 2 * grad_col
            acc = jnp.zeros((P_SIZE, rows), f32)
            for s in range(BLOCKS):
                k = load(s)
                grad_row = jnp.sum(k * gt_ref[t], axis=0, keepdims=True)
                if t == ITERS - 1:
                    grad_row = grad_row + row(grs_ref, t, s)
                grad_rowsum = -grad_row * row(rs_ref, t, s) / row(rt_ref, t, s)
                put(grs_ref, t, s, grad_rowsum)
                if t > 0:
                    acc = acc + k * grad_rowsum
        for s in range(BLOCKS):
            total = row(rs_ref, ITERS - 1, s) * col_ref[ITERS - 1, here, :] * grad_plan(s, row(u_ref, 0, s))
            for t in range(ITERS):
                total = total + row(rs_ref, t, s) * gt_ref[t]
                if t > 0:
                    total = total + row(grs_ref, t, s) * col_ref[t - 1, here, :]
                else:
                    total = total + row(grs_ref, t, s)
            gs_ref[here, s * rows : (s + 1) * rows] = (score_scale * total * load(s)).astype(bf16)


def parts_kernel(
    width, gs_ref, grads_ref, m_ref, wt_ref, raw_ref, plan_ref, refs_ref,
    p0, p1, p2, p3, other_ref, left_ref, right_ref, wide_ref,
):
    rows = other_ref.shape[2]
    part = raw_ref.shape[1]
    size = float(P_SIZE)
    grads = grads_ref[...]
    place = lax.axis_index("y") * SIDE + lax.axis_index("x")
    pair = refs_ref[:, pl.ds(pl.multiple_of((place // 2) * (2 * part), 2 * part), 2 * part)]
    left_ref[:REFS, :] = jnp.where(lax.rem(place, 2) == 0, pair[:, :part], pair[:, part:])
    for h in range(HEADS):
        here = slice(h * P_SIZE, (h + 1) * P_SIZE)
        inverse, pull = scales_of(grads, m_ref[h * PAD : (h + 1) * PAD, :], width)
        normed = jnp.sum(grads[:, :1] * wt_ref[h * PAD : (h + 1) * PAD, :].astype(f32), axis=0, keepdims=True) / size
        grad_raw = (inverse * (normed - raw_ref[here, :] * pull)).astype(bf16)
        left_ref[REFS + h * P_SIZE : REFS + (h + 1) * P_SIZE, :] = (size * grad_raw.astype(f32)).astype(bf16)
    right_ref[:REFS, :] = gs_ref[...]
    right_ref[REFS:, :] = plan_ref[...]
    wide_ref[...] = lax.dot_general(left_ref[...], right_ref[...], TN, preferred_element_type=f32)
    core, z = lax.axis_index("core"), lax.axis_index("z")
    outs = (p0, p1, p2, p3)

    def take(step, which):
        block = lax.bitwise_xor(2 * lax.rem(z + step, DEPTH) + which, place)
        return wide_ref[:, lanes(block, rows)].astype(bf16)

    for k in range(4):
        for b in range(2):
            step = jnp.where(core == 0, CHIPS[0][k], CHIPS[1][k]) + 4 * b
            outs[k][b] = take(step, core)
            step = jnp.where(core == 0, CHIPS[1][k], CHIPS[0][k]) + 4 * b
            other_ref[2 * k + b] = take(step, 1 - core)


def cores_kernel(p0, p1, p2, p3, other_ref, o0, o1, o2, o3):
    for k, (part, out) in enumerate(zip((p0, p1, p2, p3), (o0, o1, o2, o3))):
        for b in range(2):
            out[b] = (part[b].astype(f32) + other_ref[2 * k + b].astype(f32)).astype(bf16)


def chips_kernel(o0, o1, o2, o3, u0, u1):
    for b, out in enumerate((u0, u1)):
        total = o0[b].astype(f32) + o1[b].astype(f32) + o2[b].astype(f32) + o3[b].astype(f32)
        out[...] = total.astype(bf16)


def last_kernel(u0, u1, out_ref):
    out_ref[...] = u0[...].astype(f32) + u1[...].astype(f32)


def references_kernel(gs_ref, mixed_ref, other_ref, out_ref, fc_ref):
    put_columns(mixed_ref, other_ref, fc_ref)
    for h in range(HEADS):
        heads = gs_ref[h * P_SIZE : (h + 1) * P_SIZE, :]
        out_ref[h] = lax.dot_general(fc_ref[...], heads, NT, preferred_element_type=f32)


def along_z(value, k):
    pairs = []
    for z in range(DEPTH):
        for core in range(2):
            pairs.append((2 * z + core, 2 * ((z + CHIPS[core][k]) % DEPTH) + core))
    return lax.ppermute(value, ("z", "core"), pairs)


def to_place(value, b):
    pairs = []
    for z in range(DEPTH):
        for core in range(2):
            for j in range(BLOCKS):
                block = (2 * ((z + 4 * b) % DEPTH) + core) ^ j
                pairs.append(((2 * z + core) * BLOCKS + j, j * BLOCKS + block))
    return lax.ppermute(value, ("z", "core", "y", "x"), pairs)


def spread_logits(value):
    pairs = [((s + j) % BLOCKS * BLOCKS + j, s * BLOCKS + j) for s in range(BLOCKS) for j in range(BLOCKS)]
    return lax.ppermute(value, ("z", "core", "y", "x"), pairs)


def local(features, references, classifier, lengths, labels):
    batch, rows, width = features.shape
    part = width // BLOCKS
    everything = BLOCKS * rows
    score_scale = temper / math.sqrt(width)
    feats = features.reshape(rows, width)
    refs = references.reshape(REFS, width)
    kind = jax.ShapeDtypeStruct

    half = part // 2
    halves = kind((BLOCKS, half, rows), bf16)
    split = call(split_kernel, "split", halves, 1, scratch=[pltpu.VMEM((width, rows), bf16)])(feats)
    mixed = call(
        functools.partial(scores_kernel, score_scale), "scores", kind((BLOCKS, half + REFS, rows), bf16), 3
    )(feats, refs, split)
    mixed = exchange(mixed)
    other = lax.ppermute(call(peel_kernel, "peel", halves, 1)(mixed), "core", [(0, 1), (1, 0)])
    weights = jnp.pad(jnp.transpose(classifier, (0, 2, 1)), ((0, 0), (0, PAD - CLASSES), (0, 0)))
    weights = weights.reshape(HEADS * PAD, part)

    scales = kind((ITERS * HEADS * BLOCKS, rows), f32)
    rs, rt, col, plan = call(
        sinkhorn_kernel, "sinkhorn",
        [scales, scales, kind((ITERS, REFS, rows), f32), kind((REFS, everything), bf16)], [VMEM, SMEM, SMEM],
    )(mixed, lengths, labels)
    products, raw = call(
        forward_kernel, "forward",
        [kind((BLOCKS, T_ROWS + M_ROWS, rows), bf16), kind((REFS, part), f32)], 4,
        scratch=[pltpu.VMEM((part, everything), bf16), pltpu.VMEM((T_ROWS, part), bf16)],
    )(mixed, other, weights, plan)
    t, moments, logit_part = call(
        functools.partial(sum_kernel, width), "sum",
        [kind((T_ROWS, rows), bf16), kind((HEADS * PAD, P_SIZE), f32), kind((PAD, PAD), f32)], 1,
    )(exchange(products))
    ts = exchange(
        call(row_kernel, "row", kind((BLOCKS, T_ROWS, rows), bf16), 2)(t, spread_logits(logit_part))
    )
    pair = kind((2, part, rows), bf16)
    logits, grads, grad_scores = call(
        functools.partial(backward_kernel, width, score_scale), "backward",
        [kind((1, PAD), f32), kind((PAD, P_SIZE), f32), kind((REFS, everything), bf16)],
        [VMEM] * 6 + [SMEM],
        scratch=[
            pltpu.VMEM((ITERS, P_SIZE, rows), f32),
            pltpu.VMEM((ITERS * HEADS * BLOCKS, rows), f32),
            pltpu.VMEM((HEADS * BLOCKS, rows), f32),
        ],
    )(mixed, ts, rs, rt, col, moments, labels)
    *mine, away = call(
        functools.partial(parts_kernel, width), "parts", [pair] * 4 + [kind((DEPTH, part, rows), bf16)], 7,
        scratch=[
            pltpu.VMEM((2 * REFS, part), bf16),
            pltpu.VMEM((2 * REFS, everything), bf16),
            pltpu.VMEM((part, everything), f32),
        ],
        mib=12,
    )(grad_scores, grads, moments, weights, raw, plan, refs)
    away = lax.ppermute(away, "core", [(0, 1), (1, 0)])
    o = call(cores_kernel, "cores", [pair] * 4, 5)(*mine, away)
    o = [o[0]] + [along_z(o[k], k) for k in (1, 2, 3)]
    u = call(chips_kernel, "chips", [kind((part, rows), bf16)] * 2, 4)(*o)
    u = [to_place(u[b], b) for b in range(2)]
    grad_features = call(last_kernel, "last", kind((part, rows), f32), 2)(*u)
    grad_references = call(
        references_kernel, "references", kind((HEADS, part, rows), f32), 3,
        scratch=[pltpu.VMEM((part, everything), bf16)], flops=2 * REFS * part * everything,
    )(grad_scores, mixed, other)
    return (
        logits[:, :CLASSES],
        jnp.transpose(grad_features).reshape(batch, rows, part),
        jnp.transpose(grad_references, (0, 2, 1)),
    )


def solution(mesh):
    grid = Mesh(mesh.devices.reshape(DEPTH, 2, SIDE, SIDE), ("z", "core", "y", "x"))
    section, seq = ("z", "core"), ("y", "x")
    in_specs = (P(None, seq, None), P(section, None, None), P(section, seq, None), P(), P())
    out_specs = (P(), P(None, seq, section), P(section, None, seq))
    return jax.shard_map(local, mesh=grid, in_specs=in_specs, out_specs=out_specs, check_vma=False)
```

```python
import functools
import math

import jax
import jax.numpy as jnp
from jax import lax
from jax.experimental import pallas as pl
from jax.experimental.pallas import tpu as pltpu
from jax.sharding import Mesh, PartitionSpec as P

P_SIZE = 128
ITERS = 3
CLASSES = 10
PAD = 16
HEADS = 2
REFS = HEADS * P_SIZE

temper = 1.5
epsilon = 1e-06
loss_scale = 65536.0
f32 = jnp.float32
bf16 = jnp.bfloat16

SIDE = 4
DEPTH = 8
BLOCKS = SIDE * SIDE
CHIPS = ((0, 1, 7, 2), (0, 1, 7, 6))
T_ROWS = REFS + HEADS * PAD
MOVE = 4
M_ROWS = PAD
VMEM = pl.BlockSpec(memory_space=pltpu.VMEM)
SMEM = pl.BlockSpec(memory_space=pltpu.SMEM)
NT = (((1,), (1,)), ((), ()))
TN = (((0,), (0,)), ((), ()))


def call(kernel, name, shapes, specs, scratch=(), flops=0, mib=8):
    many = isinstance(shapes, list)
    return pl.pallas_call(
        kernel,
        out_shape=shapes,
        in_specs=[VMEM] * specs if isinstance(specs, int) else specs,
        out_specs=[VMEM] * len(shapes) if many else VMEM,
        scratch_shapes=list(scratch),
        compiler_params=pltpu.CompilerParams(vmem_limit_bytes=mib * 1024 * 1024),
        cost_estimate=pl.CostEstimate(flops=flops, bytes_accessed=1 << 20, transcendentals=0) if flops else None,
        name=name,
    )


def lanes(block, rows):
    return pl.ds(pl.multiple_of(block * rows, rows), rows)


def exchange(value):
    return lax.all_to_all(value, ("x", "y"), 0, 0)


def at(j):
    return j % SIDE * SIDE + j // SIDE


def split_kernel(f_ref, len_ref, label_ref, out_ref, turned_ref):
    half = out_ref.shape[1]
    part = 2 * half
    for j in range(BLOCKS // 2):
        where = slice(2 * part * j, 2 * part * (j + 1))
        turned_ref[where, :] = jnp.transpose(f_ref[:, where])
    core = lax.axis_index("core")
    for j in range(BLOCKS):
        out_ref[at(j)] = turned_ref[pl.ds(pl.multiple_of(part * j + half * core, half), half), :]


def scores_kernel(scale, f_ref, r_ref, half_ref, out_ref):
    half = half_ref.shape[1]
    scores = lax.dot_general(r_ref[...], f_ref[...], NT, preferred_element_type=f32)
    kernel = jnp.exp(scores * scale).astype(bf16)
    for j in range(BLOCKS):
        out_ref[j, :half, :] = half_ref[j]
        out_ref[j, half:, :] = kernel


def peel_kernel(in_ref, out_ref):
    half = out_ref.shape[1]
    for j in range(BLOCKS):
        out_ref[j] = in_ref[j, :half, :]


def put_columns(mixed_ref, other_ref, out_ref):
    core = lax.axis_index("core")
    half, rows = other_ref.shape[1:]
    for j in range(BLOCKS):
        here = slice(j * rows, (j + 1) * rows)
        out_ref[pl.ds(pl.multiple_of(core * half, half), half), here] = mixed_ref[at(j), :half, :]
        out_ref[pl.ds(pl.multiple_of((1 - core) * half, half), half), here] = other_ref[at(j)]


def diagonal():
    square = (P_SIZE, P_SIZE)
    return lax.broadcasted_iota(jnp.int32, square, 0) == lax.broadcasted_iota(jnp.int32, square, 1)


def to_row(column):
    return jnp.sum(jnp.where(diagonal(), column, 0.0), axis=0, keepdims=True)


def to_column(row):
    return jnp.sum(jnp.where(diagonal(), row, 0.0), axis=1, keepdims=True)


def sinkhorn_kernel(q_ref, len_ref, label_ref, rs_ref, rt_ref, col_ref, plan_ref):
    length = len_ref[0]
    rows = q_ref.shape[2]
    low = q_ref.shape[1] - REFS
    mass = 1.0 / (jnp.zeros((1, rows), jnp.int32) + length).astype(f32)
    lane = lax.broadcasted_iota(jnp.int32, (1, rows), 1)
    masses = [jnp.where(s * rows + lane < length, mass, 0.0) for s in range(BLOCKS)]
    for t in range(ITERS):
        for h in range(HEADS):
            here = slice(h * P_SIZE, (h + 1) * P_SIZE)
            acc = jnp.zeros((P_SIZE, rows), f32)
            for s in range(BLOCKS):
                k = q_ref[at(s), low + h * P_SIZE : low + (h + 1) * P_SIZE, :].astype(f32)
                weighted = k if t == 0 else k * col_ref[t - 1, here, :]
                total = jnp.sum(weighted, axis=0, keepdims=True)
                scale = masses[s] / total
                place = (t * HEADS + h) * BLOCKS + s
                rt_ref[place : place + 1, :] = total
                rs_ref[place : place + 1, :] = scale
                acc = acc + k * scale
            col = 1.0 / (float(P_SIZE) * jnp.sum(acc, axis=1, keepdims=True))
            col_ref[t, here, :] = jnp.broadcast_to(col, (P_SIZE, rows))
    for h in range(HEADS):
        here = slice(h * P_SIZE, (h + 1) * P_SIZE)
        for s in range(BLOCKS):
            k = q_ref[at(s), low + h * P_SIZE : low + (h + 1) * P_SIZE, :].astype(f32)
            place = ((ITERS - 1) * HEADS + h) * BLOCKS + s
            plan = rs_ref[place : place + 1, :] * k * col_ref[ITERS - 1, here, :]
            plan_ref[here, s * rows : (s + 1) * rows] = plan.astype(bf16)


def forward_kernel(mixed_ref, other_ref, wt_ref, plan_ref, out_ref, raw_ref, fc_ref, ext_ref):
    rows = other_ref.shape[2]
    put_columns(mixed_ref, other_ref, fc_ref)
    raw = float(P_SIZE) * lax.dot_general(plan_ref[...], fc_ref[...], NT, preferred_element_type=f32)
    raw_ref[...] = raw
    ext_ref[:REFS, :] = raw.astype(bf16)
    ext_ref[REFS:, :] = wt_ref[...]
    tails, heads = [], []
    for h in range(HEADS):
        here = slice(h * P_SIZE, (h + 1) * P_SIZE)
        squares = jnp.sum(raw_ref[here, :] * raw_ref[here, :], axis=1, keepdims=True)
        products = lax.dot_general(
            wt_ref[h * PAD : (h + 1) * PAD, :], ext_ref[here, :], NT, preferred_element_type=f32
        )
        kind = lax.broadcasted_iota(jnp.int32, products.shape, 0)
        moments = jnp.where(kind == CLASSES, to_row(squares), products)
        heads.append(moments[:8])
        tails.append(pltpu.roll(moments, MOVE, 0))
    first = jnp.concatenate(heads, axis=0).astype(bf16)
    for i in range(4):
        wide = jnp.dot(
            ext_ref[...], fc_ref[:, 4 * i * rows : 4 * (i + 1) * rows], preferred_element_type=f32
        )
        for k in range(4):
            here = slice(k * rows, (k + 1) * rows)
            out_ref[at(4 * i + k), :REFS, :] = wide[:REFS, here].astype(bf16)
            for h in range(HEADS):
                low = REFS + h * PAD
                value = jnp.where(kind < CLASSES, wide[low : low + PAD, here], tails[h])
                out_ref[at(4 * i + k), low : low + PAD, :] = value.astype(bf16)
            out_ref[at(4 * i + k), T_ROWS:, :] = first


def add_blocks(ref, low, high):
    total = ref[0, low:high, :].astype(f32)
    for j in range(1, BLOCKS):
        total = total + ref[j, low:high, :].astype(f32)
    return total


def inverse_rms(moments, width):
    return lax.rsqrt(moments[CLASSES : CLASSES + 1, :] / width + epsilon)


def sixteen():
    square = (PAD, PAD)
    return lax.broadcasted_iota(jnp.int32, square, 0) == lax.broadcasted_iota(jnp.int32, square, 1)


def sum_kernel(width, in_ref, t_ref, m_ref, logit_ref):
    logits = jnp.zeros((PAD, 1), f32)
    first = add_blocks(in_ref, T_ROWS, T_ROWS + M_ROWS)
    for h in range(HEADS):
        low = REFS + h * PAD
        block = add_blocks(in_ref, low, low + PAD)
        t_ref[low : low + PAD, :] = block.astype(bf16)
        kind = lax.broadcasted_iota(jnp.int32, block.shape, 0)
        head = first if h == 0 else pltpu.roll(first, 8, 0)
        moments = jnp.where(kind < 8, head, jnp.where(kind <= CLASSES, pltpu.roll(block, PAD - MOVE, 0), 0.0))
        m_ref[h * PAD : (h + 1) * PAD, :] = moments
        part = jnp.sum(inverse_rms(moments, width) * moments, axis=1, keepdims=True)
        logits = logits + part / P_SIZE
    row = jnp.sum(jnp.where(sixteen(), logits, 0.0), axis=0, keepdims=True)
    logit_ref[...] = jnp.broadcast_to(row, logit_ref.shape)
    for low in range(0, REFS, 64):
        t_ref[low : low + 64, :] = add_blocks(in_ref, low, low + 64).astype(bf16)


def row_kernel(t_ref, logit_ref, out_ref):
    logits = logit_ref[...]
    high = logits.astype(bf16).astype(f32)
    low = REFS + PAD
    kind = lax.broadcasted_iota(jnp.int32, logits.shape, 0)
    block = t_ref[REFS:low, :PAD].astype(f32)
    block = jnp.where(kind == CLASSES, high, jnp.where(kind == CLASSES + 1, logits - high, block)).astype(bf16)
    for j in range(BLOCKS):
        out_ref[j] = t_ref[...]
        out_ref[j, REFS:low, :PAD] = block


def sum_logits(ref):
    section = 2 * lax.axis_index("z") + lax.axis_index("core")
    total = jnp.zeros((PAD, PAD), f32)
    for other in range(BLOCKS):
        total = total + ref[at(lax.rem(other + BLOCKS - section, BLOCKS)), REFS : REFS + PAD, :PAD].astype(f32)
    return total[CLASSES : CLASSES + 1] + total[CLASSES + 1 : CLASSES + 2]


def scales_of(grads, moments, width):
    inverse = inverse_rms(moments, width)
    dual = inverse * jnp.sum(grads * moments, axis=0, keepdims=True) / (float(P_SIZE) * width)
    return to_column(inverse), to_column(inverse * dual)


def backward_kernel(
    width, score_scale,
    q_ref, t_ref, rs_ref, rt_ref, col_ref, m_ref, label_ref,
    logit_ref, grads_ref, gs_ref, gt_ref, grs_ref, u_ref,
):
    rows = q_ref.shape[2]
    base = q_ref.shape[1] - REFS
    size = float(P_SIZE)
    logits = sum_logits(t_ref)
    logit_ref[...] = logits
    logits = jnp.sum(jnp.where(sixteen(), logits, 0.0), axis=1, keepdims=True)
    logits = jnp.broadcast_to(logits, (PAD, P_SIZE))
    kind = lax.broadcasted_iota(jnp.int32, logits.shape, 0)
    exps = jnp.where(kind < CLASSES, jnp.exp(logits), 0.0)
    probs = exps / jnp.sum(exps, axis=0, keepdims=True)
    grads = loss_scale * (probs - (kind == label_ref[0]).astype(f32))
    grads = jnp.where(kind < CLASSES, grads, 0.0)
    grads_ref[...] = grads
    for h in range(HEADS):
        here = slice(h * P_SIZE, (h + 1) * P_SIZE)
        inverse, pull = scales_of(grads, m_ref[h * PAD : (h + 1) * PAD, :], width)
        first = jnp.broadcast_to(size * inverse, (P_SIZE, rows))
        second = first * pull

        def load(s):
            return q_ref[at(s), base + h * P_SIZE : base + (h + 1) * P_SIZE, :].astype(f32)

        def grad_plan(s, u):
            return first * u - second * t_ref[at(s), here, :].astype(f32)

        def row(ref, t, s):
            place = (t * HEADS + h) * BLOCKS + s
            return ref[place : place + 1, :]

        def put(ref, t, s, value):
            place = (t * HEADS + h) * BLOCKS + s
            ref[place : place + 1, :] = value

        acc = jnp.zeros((P_SIZE, rows), f32)
        for s in range(BLOCKS):
            v = t_ref[at(s), REFS + h * PAD : REFS + (h + 1) * PAD, :].astype(f32)
            u = jnp.sum(grads * v, axis=0, keepdims=True) / size
            put(u_ref, 0, s, u)
            weighted = grad_plan(s, u) * load(s)
            put(grs_ref, ITERS - 1, s, jnp.sum(weighted * col_ref[ITERS - 1, here, :], axis=0, keepdims=True))
            acc = acc + weighted * row(rs_ref, ITERS - 1, s)
        for t in reversed(range(ITERS)):
            grad_col = jnp.sum(acc, axis=1, keepdims=True)
            gt_ref[t] = -size * col_ref[t, here, :] ** 2 * grad_col
            acc = jnp.zeros((P_SIZE, rows), f32)
            for s in range(BLOCKS):
                k = load(s)
                grad_row = jnp.sum(k * gt_ref[t], axis=0, keepdims=True)
                if t == ITERS - 1:
                    grad_row = grad_row + row(grs_ref, t, s)
                grad_rowsum = -grad_row * row(rs_ref, t, s) / row(rt_ref, t, s)
                put(grs_ref, t, s, grad_rowsum)
                if t > 0:
                    acc = acc + k * grad_rowsum
        gain = score_scale * col_ref[ITERS - 1, here, :] * first
        loss = score_scale * col_ref[ITERS - 1, here, :] * second
        for t in range(ITERS):
            gt_ref[t] = score_scale * gt_ref[t]
        for s in range(BLOCKS):
            inner = gain * row(u_ref, 0, s) - loss * t_ref[at(s), here, :].astype(f32) + gt_ref[ITERS - 1]
            total = row(rs_ref, ITERS - 1, s) * inner
            for t in range(ITERS - 1):
                total = total + row(rs_ref, t, s) * gt_ref[t]
                total = total + (score_scale * row(grs_ref, t + 1, s)) * col_ref[t, here, :]
            total = total + score_scale * row(grs_ref, 0, s)
            value = (total * load(s)).astype(bf16)
            gs_ref[here, s * rows : (s + 1) * rows] = value


def parts_kernel(
    width, gs_ref, grads_ref, m_ref, wt_ref, raw_ref, plan_ref, refs_ref,
    p0, p1, p2, p3, other_ref, left_ref, right_ref, wide_ref,
):
    rows = other_ref.shape[2]
    part = raw_ref.shape[1]
    size = float(P_SIZE)
    grads = grads_ref[...]
    place = lax.axis_index("y") * SIDE + lax.axis_index("x")
    pair = refs_ref[:, pl.ds(pl.multiple_of((place // 2) * (2 * part), 2 * part), 2 * part)]
    left_ref[:REFS, :] = jnp.where(lax.rem(place, 2) == 0, pair[:, :part], pair[:, part:])
    for h in range(HEADS):
        here = slice(h * P_SIZE, (h + 1) * P_SIZE)
        inverse, pull = scales_of(grads, m_ref[h * PAD : (h + 1) * PAD, :], width)
        normed = jnp.sum(grads[:, :1] * wt_ref[h * PAD : (h + 1) * PAD, :].astype(f32), axis=0, keepdims=True) / size
        grad_raw = (inverse * (normed - raw_ref[here, :] * pull)).astype(bf16)
        left_ref[REFS + h * P_SIZE : REFS + (h + 1) * P_SIZE, :] = (size * grad_raw.astype(f32)).astype(bf16)
    right_ref[:REFS, :] = gs_ref[...]
    right_ref[REFS:, :] = plan_ref[...]
    wide_ref[...] = lax.dot_general(left_ref[...], right_ref[...], TN, preferred_element_type=f32)
    core, z = lax.axis_index("core"), lax.axis_index("z")
    outs = (p0, p1, p2, p3)

    def take(step, which):
        block = lax.bitwise_xor(2 * lax.rem(z + step, DEPTH) + which, place)
        return wide_ref[:, lanes(block, rows)].astype(bf16)

    for k in range(4):
        for b in range(2):
            step = jnp.where(core == 0, CHIPS[0][k], CHIPS[1][k]) + 4 * b
            outs[k][b] = take(step, core)
            step = jnp.where(core == 0, CHIPS[1][k], CHIPS[0][k]) + 4 * b
            other_ref[2 * k + b] = take(step, 1 - core)


def cores_kernel(p0, p1, p2, p3, other_ref, o0, o1, o2, o3):
    for k, (part, out) in enumerate(zip((p0, p1, p2, p3), (o0, o1, o2, o3))):
        for b in range(2):
            out[b] = (part[b].astype(f32) + other_ref[2 * k + b].astype(f32)).astype(bf16)


def chips_kernel(o0, o1, o2, o3, u0, u1):
    for b, out in enumerate((u0, u1)):
        total = o0[b].astype(f32) + o1[b].astype(f32) + o2[b].astype(f32) + o3[b].astype(f32)
        out[...] = total.astype(bf16)


def last_kernel(u0, u1, out_ref):
    out_ref[...] = u0[...].astype(f32) + u1[...].astype(f32)


def references_kernel(gs_ref, mixed_ref, other_ref, out_ref, fc_ref):
    put_columns(mixed_ref, other_ref, fc_ref)
    for h in range(HEADS):
        heads = gs_ref[h * P_SIZE : (h + 1) * P_SIZE, :]
        out_ref[h] = lax.dot_general(fc_ref[...], heads, NT, preferred_element_type=f32)


def along_z(value, k):
    pairs = []
    for z in range(DEPTH):
        for core in range(2):
            pairs.append((2 * z + core, 2 * ((z + CHIPS[core][k]) % DEPTH) + core))
    return lax.ppermute(value, ("z", "core"), pairs)


def to_place(value, b):
    pairs = []
    for z in range(DEPTH):
        for core in range(2):
            for j in range(BLOCKS):
                block = (2 * ((z + 4 * b) % DEPTH) + core) ^ j
                pairs.append(((2 * z + core) * BLOCKS + j, j * BLOCKS + block))
    return lax.ppermute(value, ("z", "core", "y", "x"), pairs)


def spread_logits(value):
    pairs = [((s + j) % BLOCKS * BLOCKS + j, s * BLOCKS + j) for s in range(BLOCKS) for j in range(BLOCKS)]
    return lax.ppermute(value, ("z", "core", "y", "x"), pairs)


def local(features, references, classifier, lengths, labels):
    batch, rows, width = features.shape
    part = width // BLOCKS
    everything = BLOCKS * rows
    score_scale = temper / math.sqrt(width)
    feats = features.reshape(rows, width)
    refs = references.reshape(REFS, width)
    kind = jax.ShapeDtypeStruct

    half = part // 2
    halves = kind((BLOCKS, half, rows), bf16)
    split = call(
        split_kernel, "split", halves, [VMEM, SMEM, SMEM], scratch=[pltpu.VMEM((width, rows), bf16)], flops=3 * 10**9
    )(feats, lengths, labels)
    mixed = call(
        functools.partial(scores_kernel, score_scale), "scores", kind((BLOCKS, half + REFS, rows), bf16), 3
    )(feats, refs, split)
    weights = jnp.pad(jnp.transpose(classifier, (0, 2, 1)), ((0, 0), (0, PAD - CLASSES), (0, 0)))
    weights = weights.reshape(HEADS * PAD, part)

    mixed, weights = lax.optimization_barrier((mixed, weights))
    mixed = exchange(mixed)
    other = lax.ppermute(call(peel_kernel, "peel", halves, 1)(mixed), "core", [(0, 1), (1, 0)])
    scales = kind((ITERS * HEADS * BLOCKS, rows), f32)
    rs, rt, col, plan = call(
        sinkhorn_kernel, "sinkhorn",
        [scales, scales, kind((ITERS, REFS, rows), f32), kind((REFS, everything), bf16)], [VMEM, SMEM, SMEM],
    )(mixed, lengths, labels)
    products, raw = call(
        forward_kernel, "forward",
        [kind((BLOCKS, T_ROWS + M_ROWS, rows), bf16), kind((REFS, part), f32)], 4,
        scratch=[pltpu.VMEM((part, everything), bf16), pltpu.VMEM((T_ROWS, part), bf16)],
    )(mixed, other, weights, plan)
    t, moments, logit_part = call(
        functools.partial(sum_kernel, width), "sum",
        [kind((T_ROWS, rows), bf16), kind((HEADS * PAD, P_SIZE), f32), kind((PAD, PAD), f32)], 1,
    )(exchange(products))
    ts = exchange(
        call(row_kernel, "row", kind((BLOCKS, T_ROWS, rows), bf16), 2)(t, spread_logits(logit_part))
    )
    pair = kind((2, part, rows), bf16)
    logits, grads, grad_scores = call(
        functools.partial(backward_kernel, width, score_scale), "backward",
        [kind((1, PAD), f32), kind((PAD, P_SIZE), f32), kind((REFS, everything), bf16)],
        [VMEM] * 6 + [SMEM],
        scratch=[
            pltpu.VMEM((ITERS, P_SIZE, rows), f32),
            pltpu.VMEM((ITERS * HEADS * BLOCKS, rows), f32),
            pltpu.VMEM((HEADS * BLOCKS, rows), f32),
        ],
    )(mixed, ts, rs, rt, col, moments, labels)
    *mine, away = call(
        functools.partial(parts_kernel, width), "parts", [pair] * 4 + [kind((DEPTH, part, rows), bf16)], 7,
        scratch=[
            pltpu.VMEM((2 * REFS, part), bf16),
            pltpu.VMEM((2 * REFS, everything), bf16),
            pltpu.VMEM((part, everything), f32),
        ],
        mib=12,
    )(grad_scores, grads, moments, weights, raw, plan, refs)
    away = lax.ppermute(away, "core", [(0, 1), (1, 0)])
    o = call(cores_kernel, "cores", [pair] * 4, 5)(*mine, away)
    o = [o[0]] + [along_z(o[k], k) for k in (1, 2, 3)]
    u = call(chips_kernel, "chips", [kind((part, rows), bf16)] * 2, 4)(*o)
    u = [to_place(u[b], b) for b in range(2)]
    grad_features = call(last_kernel, "last", kind((part, rows), f32), 2)(*u)
    grad_references = call(
        references_kernel, "references", kind((HEADS, part, rows), f32), 3,
        scratch=[pltpu.VMEM((part, everything), bf16)], flops=2 * REFS * part * everything,
    )(grad_scores, mixed, other)
    return (
        logits[:, :CLASSES],
        jnp.transpose(grad_features).reshape(batch, rows, part),
        jnp.transpose(grad_references, (0, 2, 1)),
    )


def solution(mesh):
    grid = Mesh(mesh.devices.reshape(DEPTH, 2, SIDE, SIDE), ("z", "core", "y", "x"))
    section, seq = ("z", "core"), ("y", "x")
    in_specs = (P(None, seq, None), P(section, None, None), P(section, seq, None), P(), P())
    out_specs = (P(), P(None, seq, section), P(section, None, seq))
    return jax.shard_map(local, mesh=grid, in_specs=in_specs, out_specs=out_specs, check_vma=False)
```

```python
import functools
import math

import jax
import jax.numpy as jnp
from jax import lax
from jax.experimental import pallas as pl
from jax.experimental.pallas import tpu as pltpu
from jax.sharding import Mesh, PartitionSpec as P

P_SIZE = 128
ITERS = 3
CLASSES = 10
PAD = 16
HEADS = 2
REFS = HEADS * P_SIZE

temper = 1.5
epsilon = 1e-06
loss_scale = 65536.0
f32 = jnp.float32
bf16 = jnp.bfloat16

SIDE = 4
DEPTH = 8
BLOCKS = SIDE * SIDE
CHIPS = ((0, 1, 7, 2), (0, 1, 7, 6))
T_ROWS = REFS + HEADS * PAD
MOVE = 4
M_ROWS = PAD
VMEM = pl.BlockSpec(memory_space=pltpu.VMEM)
SMEM = pl.BlockSpec(memory_space=pltpu.SMEM)
NT = (((1,), (1,)), ((), ()))
TN = (((0,), (0,)), ((), ()))


def call(kernel, name, shapes, specs, scratch=(), flops=0, mib=8):
    many = isinstance(shapes, list)
    return pl.pallas_call(
        kernel,
        out_shape=shapes,
        in_specs=[VMEM] * specs if isinstance(specs, int) else specs,
        out_specs=[VMEM] * len(shapes) if many else VMEM,
        scratch_shapes=list(scratch),
        compiler_params=pltpu.CompilerParams(vmem_limit_bytes=mib * 1024 * 1024),
        cost_estimate=pl.CostEstimate(flops=flops, bytes_accessed=1 << 20, transcendentals=0) if flops else None,
        name=name,
    )


def lanes(block, rows):
    return pl.ds(pl.multiple_of(block * rows, rows), rows)


def exchange(value):
    return lax.all_to_all(value, ("x", "y"), 0, 0)


def at(j):
    return j % SIDE * SIDE + j // SIDE


def split_kernel(f_ref, out_ref, turned_ref):
    half = out_ref.shape[1]
    part = 2 * half
    for j in range(BLOCKS // 2):
        where = slice(2 * part * j, 2 * part * (j + 1))
        turned_ref[where, :] = jnp.transpose(f_ref[:, where])
    core = lax.axis_index("core")
    for j in range(BLOCKS):
        out_ref[at(j)] = turned_ref[pl.ds(pl.multiple_of(part * j + half * core, half), half), :]


def scores_kernel(scale, f_ref, r_ref, half_ref, out_ref):
    half = half_ref.shape[1]
    scores = lax.dot_general(r_ref[...], f_ref[...], NT, preferred_element_type=f32)
    kernel = jnp.exp(scores * scale).astype(bf16)
    for j in range(BLOCKS):
        out_ref[j, :half, :] = half_ref[j]
        out_ref[j, half:, :] = kernel


def peel_kernel(in_ref, out_ref):
    half = out_ref.shape[1]
    for j in range(BLOCKS):
        out_ref[j] = in_ref[j, :half, :]


def put_columns(mixed_ref, other_ref, out_ref):
    core = lax.axis_index("core")
    half, rows = other_ref.shape[1:]
    for j in range(BLOCKS):
        here = slice(j * rows, (j + 1) * rows)
        out_ref[pl.ds(pl.multiple_of(core * half, half), half), here] = mixed_ref[at(j), :half, :]
        out_ref[pl.ds(pl.multiple_of((1 - core) * half, half), half), here] = other_ref[at(j)]


def diagonal():
    square = (P_SIZE, P_SIZE)
    return lax.broadcasted_iota(jnp.int32, square, 0) == lax.broadcasted_iota(jnp.int32, square, 1)


def to_row(column):
    return jnp.sum(jnp.where(diagonal(), column, 0.0), axis=0, keepdims=True)


def to_column(row):
    return jnp.sum(jnp.where(diagonal(), row, 0.0), axis=1, keepdims=True)


def sinkhorn_kernel(q_ref, len_ref, label_ref, rs_ref, rt_ref, col_ref, plan_ref):
    length = len_ref[0]
    rows = q_ref.shape[2]
    low = q_ref.shape[1] - REFS
    mass = 1.0 / (jnp.zeros((1, rows), jnp.int32) + length).astype(f32)
    lane = lax.broadcasted_iota(jnp.int32, (1, rows), 1)
    masses = [jnp.where(s * rows + lane < length, mass, 0.0) for s in range(BLOCKS)]
    for t in range(ITERS):
        for h in range(HEADS):
            here = slice(h * P_SIZE, (h + 1) * P_SIZE)
            acc = jnp.zeros((P_SIZE, rows), f32)
            for s in range(BLOCKS):
                k = q_ref[at(s), low + h * P_SIZE : low + (h + 1) * P_SIZE, :].astype(f32)
                weighted = k if t == 0 else k * col_ref[t - 1, here, :]
                total = jnp.sum(weighted, axis=0, keepdims=True)
                scale = masses[s] / total
                place = (t * HEADS + h) * BLOCKS + s
                rt_ref[place : place + 1, :] = total
                rs_ref[place : place + 1, :] = scale
                acc = acc + k * scale
            col = 1.0 / (float(P_SIZE) * jnp.sum(acc, axis=1, keepdims=True))
            col_ref[t, here, :] = jnp.broadcast_to(col, (P_SIZE, rows))
    for h in range(HEADS):
        here = slice(h * P_SIZE, (h + 1) * P_SIZE)
        for s in range(BLOCKS):
            k = q_ref[at(s), low + h * P_SIZE : low + (h + 1) * P_SIZE, :].astype(f32)
            place = ((ITERS - 1) * HEADS + h) * BLOCKS + s
            plan = rs_ref[place : place + 1, :] * k * col_ref[ITERS - 1, here, :]
            plan_ref[here, s * rows : (s + 1) * rows] = plan.astype(bf16)


def forward_kernel(mixed_ref, other_ref, wt_ref, plan_ref, out_ref, raw_ref, fc_ref, ext_ref):
    rows = other_ref.shape[2]
    put_columns(mixed_ref, other_ref, fc_ref)
    raw = float(P_SIZE) * lax.dot_general(plan_ref[...], fc_ref[...], NT, preferred_element_type=f32)
    raw_ref[...] = raw
    ext_ref[:REFS, :] = raw.astype(bf16)
    ext_ref[REFS:, :] = wt_ref[...]
    tails, heads = [], []
    for h in range(HEADS):
        here = slice(h * P_SIZE, (h + 1) * P_SIZE)
        squares = jnp.sum(raw_ref[here, :] * raw_ref[here, :], axis=1, keepdims=True)
        products = lax.dot_general(
            wt_ref[h * PAD : (h + 1) * PAD, :], ext_ref[here, :], NT, preferred_element_type=f32
        )
        kind = lax.broadcasted_iota(jnp.int32, products.shape, 0)
        moments = jnp.where(kind == CLASSES, to_row(squares), products)
        heads.append(moments[:8])
        tails.append(pltpu.roll(moments, MOVE, 0))
    first = jnp.concatenate(heads, axis=0).astype(bf16)
    for i in range(4):
        wide = jnp.dot(
            ext_ref[...], fc_ref[:, 4 * i * rows : 4 * (i + 1) * rows], preferred_element_type=f32
        )
        for k in range(4):
            here = slice(k * rows, (k + 1) * rows)
            out_ref[at(4 * i + k), :REFS, :] = wide[:REFS, here].astype(bf16)
            for h in range(HEADS):
                low = REFS + h * PAD
                value = jnp.where(kind < CLASSES, wide[low : low + PAD, here], tails[h])
                out_ref[at(4 * i + k), low : low + PAD, :] = value.astype(bf16)
            out_ref[at(4 * i + k), T_ROWS:, :] = first


def add_blocks(ref, low, high):
    total = ref[0, low:high, :].astype(f32)
    for j in range(1, BLOCKS):
        total = total + ref[j, low:high, :].astype(f32)
    return total


def inverse_rms(moments, width):
    return lax.rsqrt(moments[CLASSES : CLASSES + 1, :] / width + epsilon)


def sixteen():
    square = (PAD, PAD)
    return lax.broadcasted_iota(jnp.int32, square, 0) == lax.broadcasted_iota(jnp.int32, square, 1)


def sum_kernel(width, in_ref, t_ref, m_ref, logit_ref):
    logits = jnp.zeros((PAD, 1), f32)
    first = add_blocks(in_ref, T_ROWS, T_ROWS + M_ROWS)
    for h in range(HEADS):
        low = REFS + h * PAD
        block = add_blocks(in_ref, low, low + PAD)
        t_ref[low : low + PAD, :] = block.astype(bf16)
        kind = lax.broadcasted_iota(jnp.int32, block.shape, 0)
        head = first if h == 0 else pltpu.roll(first, 8, 0)
        moments = jnp.where(kind < 8, head, jnp.where(kind <= CLASSES, pltpu.roll(block, PAD - MOVE, 0), 0.0))
        m_ref[h * PAD : (h + 1) * PAD, :] = moments
        part = jnp.sum(inverse_rms(moments, width) * moments, axis=1, keepdims=True)
        logits = logits + part / P_SIZE
    row = jnp.sum(jnp.where(sixteen(), logits, 0.0), axis=0, keepdims=True)
    logit_ref[...] = jnp.broadcast_to(row, logit_ref.shape)
    for low in range(0, REFS, 64):
        t_ref[low : low + 64, :] = add_blocks(in_ref, low, low + 64).astype(bf16)


def row_kernel(t_ref, logit_ref, out_ref):
    logits = logit_ref[...]
    high = logits.astype(bf16).astype(f32)
    low = REFS + PAD
    kind = lax.broadcasted_iota(jnp.int32, logits.shape, 0)
    block = t_ref[REFS:low, :PAD].astype(f32)
    block = jnp.where(kind == CLASSES, high, jnp.where(kind == CLASSES + 1, logits - high, block)).astype(bf16)
    for j in range(BLOCKS):
        out_ref[j] = t_ref[...]
        out_ref[j, REFS:low, :PAD] = block


def sum_logits(ref):
    section = 2 * lax.axis_index("z") + lax.axis_index("core")
    total = jnp.zeros((PAD, PAD), f32)
    for other in range(BLOCKS):
        total = total + ref[at(lax.rem(other + BLOCKS - section, BLOCKS)), REFS : REFS + PAD, :PAD].astype(f32)
    return total[CLASSES : CLASSES + 1] + total[CLASSES + 1 : CLASSES + 2]


def scales_of(grads, moments, width):
    inverse = inverse_rms(moments, width)
    dual = inverse * jnp.sum(grads * moments, axis=0, keepdims=True) / (float(P_SIZE) * width)
    return to_column(inverse), to_column(inverse * dual)


def backward_kernel(
    width, score_scale,
    q_ref, t_ref, rs_ref, rt_ref, col_ref, m_ref, label_ref,
    logit_ref, grads_ref, gs_ref, gt_ref, grs_ref, u_ref,
):
    rows = q_ref.shape[2]
    base = q_ref.shape[1] - REFS
    size = float(P_SIZE)
    logits = sum_logits(t_ref)
    logit_ref[...] = logits
    logits = jnp.sum(jnp.where(sixteen(), logits, 0.0), axis=1, keepdims=True)
    logits = jnp.broadcast_to(logits, (PAD, P_SIZE))
    kind = lax.broadcasted_iota(jnp.int32, logits.shape, 0)
    exps = jnp.where(kind < CLASSES, jnp.exp(logits), 0.0)
    probs = exps / jnp.sum(exps, axis=0, keepdims=True)
    grads = loss_scale * (probs - (kind == label_ref[0]).astype(f32))
    grads = jnp.where(kind < CLASSES, grads, 0.0)
    grads_ref[...] = grads
    for h in range(HEADS):
        here = slice(h * P_SIZE, (h + 1) * P_SIZE)
        inverse, pull = scales_of(grads, m_ref[h * PAD : (h + 1) * PAD, :], width)
        first = jnp.broadcast_to(size * inverse, (P_SIZE, rows))
        second = first * pull

        def load(s):
            return q_ref[at(s), base + h * P_SIZE : base + (h + 1) * P_SIZE, :].astype(f32)

        def grad_plan(s, u):
            return first * u - second * t_ref[at(s), here, :].astype(f32)

        def row(ref, t, s):
            place = (t * HEADS + h) * BLOCKS + s
            return ref[place : place + 1, :]

        def put(ref, t, s, value):
            place = (t * HEADS + h) * BLOCKS + s
            ref[place : place + 1, :] = value

        acc = jnp.zeros((P_SIZE, rows), f32)
        for s in range(BLOCKS):
            v = t_ref[at(s), REFS + h * PAD : REFS + (h + 1) * PAD, :].astype(f32)
            u = jnp.sum(grads * v, axis=0, keepdims=True) / size
            put(u_ref, 0, s, u)
            weighted = grad_plan(s, u) * load(s)
            put(grs_ref, ITERS - 1, s, jnp.sum(weighted * col_ref[ITERS - 1, here, :], axis=0, keepdims=True))
            acc = acc + weighted * row(rs_ref, ITERS - 1, s)
        for t in reversed(range(ITERS)):
            grad_col = jnp.sum(acc, axis=1, keepdims=True)
            gt_ref[t] = -size * col_ref[t, here, :] ** 2 * grad_col
            acc = jnp.zeros((P_SIZE, rows), f32)
            for s in range(BLOCKS):
                k = load(s)
                grad_row = jnp.sum(k * gt_ref[t], axis=0, keepdims=True)
                if t == ITERS - 1:
                    grad_row = grad_row + row(grs_ref, t, s)
                grad_rowsum = -grad_row * row(rs_ref, t, s) / row(rt_ref, t, s)
                put(grs_ref, t, s, grad_rowsum)
                if t > 0:
                    acc = acc + k * grad_rowsum
        gain = score_scale * col_ref[ITERS - 1, here, :] * first
        loss = score_scale * col_ref[ITERS - 1, here, :] * second
        for t in range(ITERS):
            gt_ref[t] = score_scale * gt_ref[t]
        for s in range(BLOCKS):
            inner = gain * row(u_ref, 0, s) - loss * t_ref[at(s), here, :].astype(f32) + gt_ref[ITERS - 1]
            total = row(rs_ref, ITERS - 1, s) * inner
            for t in range(ITERS - 1):
                total = total + row(rs_ref, t, s) * gt_ref[t]
                total = total + (score_scale * row(grs_ref, t + 1, s)) * col_ref[t, here, :]
            total = total + score_scale * row(grs_ref, 0, s)
            value = (total * load(s)).astype(bf16)
            gs_ref[here, s * rows : (s + 1) * rows] = value


def parts_kernel(
    width, gs_ref, grads_ref, m_ref, wt_ref, raw_ref, plan_ref, refs_ref,
    p0, p1, p2, p3, other_ref, left_ref, right_ref, wide_ref,
):
    rows = other_ref.shape[2]
    part = raw_ref.shape[1]
    size = float(P_SIZE)
    grads = grads_ref[...]
    place = lax.axis_index("y") * SIDE + lax.axis_index("x")
    pair = refs_ref[:, pl.ds(pl.multiple_of((place // 2) * (2 * part), 2 * part), 2 * part)]
    left_ref[:REFS, :] = jnp.where(lax.rem(place, 2) == 0, pair[:, :part], pair[:, part:])
    for h in range(HEADS):
        here = slice(h * P_SIZE, (h + 1) * P_SIZE)
        inverse, pull = scales_of(grads, m_ref[h * PAD : (h + 1) * PAD, :], width)
        normed = jnp.sum(grads[:, :1] * wt_ref[h * PAD : (h + 1) * PAD, :].astype(f32), axis=0, keepdims=True) / size
        grad_raw = (inverse * (normed - raw_ref[here, :] * pull)).astype(bf16)
        left_ref[REFS + h * P_SIZE : REFS + (h + 1) * P_SIZE, :] = (size * grad_raw.astype(f32)).astype(bf16)
    right_ref[:REFS, :] = gs_ref[...]
    right_ref[REFS:, :] = plan_ref[...]
    wide_ref[...] = lax.dot_general(left_ref[...], right_ref[...], TN, preferred_element_type=f32)
    core, z = lax.axis_index("core"), lax.axis_index("z")
    outs = (p0, p1, p2, p3)

    def take(step, which):
        block = lax.bitwise_xor(2 * lax.rem(z + step, DEPTH) + which, place)
        return wide_ref[:, lanes(block, rows)].astype(bf16)

    for k in range(4):
        for b in range(2):
            step = jnp.where(core == 0, CHIPS[0][k], CHIPS[1][k]) + 4 * b
            outs[k][b] = take(step, core)
            step = jnp.where(core == 0, CHIPS[1][k], CHIPS[0][k]) + 4 * b
            other_ref[2 * k + b] = take(step, 1 - core)


def cores_kernel(p0, p1, p2, p3, other_ref, o0, o1, o2, o3):
    for k, (part, out) in enumerate(zip((p0, p1, p2, p3), (o0, o1, o2, o3))):
        for b in range(2):
            out[b] = (part[b].astype(f32) + other_ref[2 * k + b].astype(f32)).astype(bf16)


def chips_kernel(o0, o1, o2, o3, u0, u1):
    for b, out in enumerate((u0, u1)):
        total = o0[b].astype(f32) + o1[b].astype(f32) + o2[b].astype(f32) + o3[b].astype(f32)
        out[...] = total.astype(bf16)


def last_kernel(u0, u1, out_ref):
    out_ref[...] = u0[...].astype(f32) + u1[...].astype(f32)


def references_kernel(gs_ref, mixed_ref, other_ref, out_ref, fc_ref):
    put_columns(mixed_ref, other_ref, fc_ref)
    for h in range(HEADS):
        heads = gs_ref[h * P_SIZE : (h + 1) * P_SIZE, :]
        out_ref[h] = lax.dot_general(fc_ref[...], heads, NT, preferred_element_type=f32)


def along_z(value, k):
    pairs = []
    for z in range(DEPTH):
        for core in range(2):
            pairs.append((2 * z + core, 2 * ((z + CHIPS[core][k]) % DEPTH) + core))
    return lax.ppermute(value, ("z", "core"), pairs)


def to_place(value, b):
    pairs = []
    for z in range(DEPTH):
        for core in range(2):
            for j in range(BLOCKS):
                block = (2 * ((z + 4 * b) % DEPTH) + core) ^ j
                pairs.append(((2 * z + core) * BLOCKS + j, j * BLOCKS + block))
    return lax.ppermute(value, ("z", "core", "y", "x"), pairs)


def spread_logits(value):
    pairs = [((s + j) % BLOCKS * BLOCKS + j, s * BLOCKS + j) for s in range(BLOCKS) for j in range(BLOCKS)]
    return lax.ppermute(value, ("z", "core", "y", "x"), pairs)


def local(features, references, classifier, lengths, labels):
    batch, rows, width = features.shape
    part = width // BLOCKS
    everything = BLOCKS * rows
    score_scale = temper / math.sqrt(width)
    feats = features.reshape(rows, width)
    refs = references.reshape(REFS, width)
    kind = jax.ShapeDtypeStruct

    half = part // 2
    halves = kind((BLOCKS, half, rows), bf16)
    split = call(split_kernel, "split", halves, 1, scratch=[pltpu.VMEM((width, rows), bf16)], flops=3 * 10**9)(feats)
    mixed = call(
        functools.partial(scores_kernel, score_scale), "scores", kind((BLOCKS, half + REFS, rows), bf16), 3
    )(feats, refs, split)
    mixed = exchange(mixed)
    other = lax.ppermute(call(peel_kernel, "peel", halves, 1)(mixed), "core", [(0, 1), (1, 0)])
    weights = jnp.pad(jnp.transpose(classifier, (0, 2, 1)), ((0, 0), (0, PAD - CLASSES), (0, 0)))
    weights = weights.reshape(HEADS * PAD, part)


    scales = kind((ITERS * HEADS * BLOCKS, rows), f32)
    rs, rt, col, plan = call(
        sinkhorn_kernel, "sinkhorn",
        [scales, scales, kind((ITERS, REFS, rows), f32), kind((REFS, everything), bf16)], [VMEM, SMEM, SMEM],
    )(mixed, lengths, labels)
    products, raw = call(
        forward_kernel, "forward",
        [kind((BLOCKS, T_ROWS + M_ROWS, rows), bf16), kind((REFS, part), f32)], 4,
        scratch=[pltpu.VMEM((part, everything), bf16), pltpu.VMEM((T_ROWS, part), bf16)],
    )(mixed, other, weights, plan)
    t, moments, logit_part = call(
        functools.partial(sum_kernel, width), "sum",
        [kind((T_ROWS, rows), bf16), kind((HEADS * PAD, P_SIZE), f32), kind((PAD, PAD), f32)], 1,
    )(exchange(products))
    ts = exchange(
        call(row_kernel, "row", kind((BLOCKS, T_ROWS, rows), bf16), 2)(t, spread_logits(logit_part))
    )
    pair = kind((2, part, rows), bf16)
    logits, grads, grad_scores = call(
        functools.partial(backward_kernel, width, score_scale), "backward",
        [kind((1, PAD), f32), kind((PAD, P_SIZE), f32), kind((REFS, everything), bf16)],
        [VMEM] * 6 + [SMEM],
        scratch=[
            pltpu.VMEM((ITERS, P_SIZE, rows), f32),
            pltpu.VMEM((ITERS * HEADS * BLOCKS, rows), f32),
            pltpu.VMEM((HEADS * BLOCKS, rows), f32),
        ],
    )(mixed, ts, rs, rt, col, moments, labels)
    *mine, away = call(
        functools.partial(parts_kernel, width), "parts", [pair] * 4 + [kind((DEPTH, part, rows), bf16)], 7,
        scratch=[
            pltpu.VMEM((2 * REFS, part), bf16),
            pltpu.VMEM((2 * REFS, everything), bf16),
            pltpu.VMEM((part, everything), f32),
        ],
        mib=12,
    )(grad_scores, grads, moments, weights, raw, plan, refs)
    away = lax.ppermute(away, "core", [(0, 1), (1, 0)])
    o = call(cores_kernel, "cores", [pair] * 4, 5)(*mine, away)
    o = [o[0]] + [along_z(o[k], k) for k in (1, 2, 3)]
    u = call(chips_kernel, "chips", [kind((part, rows), bf16)] * 2, 4)(*o)
    u = [to_place(u[b], b) for b in range(2)]
    grad_features = call(last_kernel, "last", kind((part, rows), f32), 2)(*u)
    grad_references = call(
        references_kernel, "references", kind((HEADS, part, rows), f32), 3,
        scratch=[pltpu.VMEM((part, everything), bf16)], flops=2 * REFS * part * everything,
    )(grad_scores, mixed, other)
    return (
        logits[:, :CLASSES],
        jnp.transpose(grad_features).reshape(batch, rows, part),
        jnp.transpose(grad_references, (0, 2, 1)),
    )


def solution(mesh):
    grid = Mesh(mesh.devices.reshape(DEPTH, 2, SIDE, SIDE), ("z", "core", "y", "x"))
    section, seq = ("z", "core"), ("y", "x")
    in_specs = (P(None, seq, None), P(section, None, None), P(section, seq, None), P(), P())
    out_specs = (P(), P(None, seq, section), P(section, None, seq))
    return jax.shard_map(local, mesh=grid, in_specs=in_specs, out_specs=out_specs, check_vma=False)
```

```python
import functools
import math

import jax
import jax.numpy as jnp
from jax import lax
from jax.experimental import pallas as pl
from jax.experimental.pallas import tpu as pltpu
from jax.sharding import Mesh, PartitionSpec as P

P_SIZE = 128
ITERS = 3
CLASSES = 10
PAD = 16
HEADS = 2
REFS = HEADS * P_SIZE

temper = 1.5
epsilon = 1e-06
loss_scale = 65536.0
f32 = jnp.float32
bf16 = jnp.bfloat16

SIDE = 4
DEPTH = 8
BLOCKS = SIDE * SIDE
CHIPS = ((0, 1, 7, 2), (0, 1, 7, 6))
T_ROWS = REFS + HEADS * PAD
MOVE = 4
M_ROWS = PAD
VMEM = pl.BlockSpec(memory_space=pltpu.VMEM)
SMEM = pl.BlockSpec(memory_space=pltpu.SMEM)
NT = (((1,), (1,)), ((), ()))
TN = (((0,), (0,)), ((), ()))


def call(kernel, name, shapes, specs, scratch=(), flops=0, mib=8):
    many = isinstance(shapes, list)
    return pl.pallas_call(
        kernel,
        out_shape=shapes,
        in_specs=[VMEM] * specs if isinstance(specs, int) else specs,
        out_specs=[VMEM] * len(shapes) if many else VMEM,
        scratch_shapes=list(scratch),
        compiler_params=pltpu.CompilerParams(vmem_limit_bytes=mib * 1024 * 1024),
        cost_estimate=pl.CostEstimate(flops=flops, bytes_accessed=1 << 20, transcendentals=0) if flops else None,
        name=name,
    )


def lanes(block, rows):
    return pl.ds(pl.multiple_of(block * rows, rows), rows)


def exchange(value):
    return lax.all_to_all(value, ("x", "y"), 0, 0)


def at(j):
    return j % SIDE * SIDE + j // SIDE


def split_kernel(f_ref, out_ref, turned_ref):
    half = out_ref.shape[1]
    part = 2 * half
    for j in range(BLOCKS // 2):
        where = slice(2 * part * j, 2 * part * (j + 1))
        turned_ref[where, :] = jnp.transpose(f_ref[:, where])
    core = lax.axis_index("core")
    for j in range(BLOCKS):
        out_ref[at(j)] = turned_ref[pl.ds(pl.multiple_of(part * j + half * core, half), half), :]


def scores_kernel(scale, f_ref, r_ref, half_ref, out_ref):
    half = half_ref.shape[1]
    scores = lax.dot_general(r_ref[...], f_ref[...], NT, preferred_element_type=f32)
    kernel = jnp.exp(scores * scale).astype(bf16)
    for j in range(BLOCKS):
        out_ref[j, :half, :] = half_ref[j]
        out_ref[j, half:, :] = kernel


def peel_kernel(in_ref, out_ref):
    half = out_ref.shape[1]
    for j in range(BLOCKS):
        out_ref[j] = in_ref[j, :half, :]


def put_columns(mixed_ref, other_ref, out_ref):
    core = lax.axis_index("core")
    half, rows = other_ref.shape[1:]
    for j in range(BLOCKS):
        here = slice(j * rows, (j + 1) * rows)
        out_ref[pl.ds(pl.multiple_of(core * half, half), half), here] = mixed_ref[at(j), :half, :]
        out_ref[pl.ds(pl.multiple_of((1 - core) * half, half), half), here] = other_ref[at(j)]


def diagonal():
    square = (P_SIZE, P_SIZE)
    return lax.broadcasted_iota(jnp.int32, square, 0) == lax.broadcasted_iota(jnp.int32, square, 1)


def to_row(column):
    return jnp.sum(jnp.where(diagonal(), column, 0.0), axis=0, keepdims=True)


def to_column(row):
    return jnp.sum(jnp.where(diagonal(), row, 0.0), axis=1, keepdims=True)


def sinkhorn_kernel(q_ref, len_ref, label_ref, rs_ref, rt_ref, col_ref, plan_ref):
    length = len_ref[0]
    rows = q_ref.shape[2]
    low = q_ref.shape[1] - REFS
    mass = 1.0 / (jnp.zeros((1, rows), jnp.int32) + length).astype(f32)
    lane = lax.broadcasted_iota(jnp.int32, (1, rows), 1)
    masses = [jnp.where(s * rows + lane < length, mass, 0.0) for s in range(BLOCKS)]
    for t in range(ITERS):
        for h in range(HEADS):
            here = slice(h * P_SIZE, (h + 1) * P_SIZE)
            acc = jnp.zeros((P_SIZE, rows), f32)
            for s in range(BLOCKS):
                k = q_ref[at(s), low + h * P_SIZE : low + (h + 1) * P_SIZE, :].astype(f32)
                weighted = k if t == 0 else k * col_ref[t - 1, here, :]
                total = jnp.sum(weighted, axis=0, keepdims=True)
                scale = masses[s] / total
                place = (t * HEADS + h) * BLOCKS + s
                rt_ref[place : place + 1, :] = total
                rs_ref[place : place + 1, :] = scale
                acc = acc + k * scale
            col = 1.0 / (float(P_SIZE) * jnp.sum(acc, axis=1, keepdims=True))
            col_ref[t, here, :] = jnp.broadcast_to(col, (P_SIZE, rows))
    for h in range(HEADS):
        here = slice(h * P_SIZE, (h + 1) * P_SIZE)
        for s in range(BLOCKS):
            k = q_ref[at(s), low + h * P_SIZE : low + (h + 1) * P_SIZE, :].astype(f32)
            place = ((ITERS - 1) * HEADS + h) * BLOCKS + s
            plan = rs_ref[place : place + 1, :] * k * col_ref[ITERS - 1, here, :]
            plan_ref[here, s * rows : (s + 1) * rows] = plan.astype(bf16)


def forward_kernel(mixed_ref, other_ref, wt_ref, plan_ref, out_ref, raw_ref, fc_ref, ext_ref):
    rows = other_ref.shape[2]
    put_columns(mixed_ref, other_ref, fc_ref)
    raw = float(P_SIZE) * lax.dot_general(plan_ref[...], fc_ref[...], NT, preferred_element_type=f32)
    raw_ref[...] = raw
    ext_ref[:REFS, :] = raw.astype(bf16)
    ext_ref[REFS:, :] = wt_ref[...]
    tails, heads = [], []
    for h in range(HEADS):
        here = slice(h * P_SIZE, (h + 1) * P_SIZE)
        squares = jnp.sum(raw_ref[here, :] * raw_ref[here, :], axis=1, keepdims=True)
        products = lax.dot_general(
            wt_ref[h * PAD : (h + 1) * PAD, :], ext_ref[here, :], NT, preferred_element_type=f32
        )
        kind = lax.broadcasted_iota(jnp.int32, products.shape, 0)
        moments = jnp.where(kind == CLASSES, to_row(squares), products)
        heads.append(moments[:8])
        tails.append(pltpu.roll(moments, MOVE, 0))
    first = jnp.concatenate(heads, axis=0).astype(bf16)
    for i in range(4):
        wide = jnp.dot(
            ext_ref[...], fc_ref[:, 4 * i * rows : 4 * (i + 1) * rows], preferred_element_type=f32
        )
        for k in range(4):
            here = slice(k * rows, (k + 1) * rows)
            out_ref[at(4 * i + k), :REFS, :] = wide[:REFS, here].astype(bf16)
            for h in range(HEADS):
                low = REFS + h * PAD
                value = jnp.where(kind < CLASSES, wide[low : low + PAD, here], tails[h])
                out_ref[at(4 * i + k), low : low + PAD, :] = value.astype(bf16)
            out_ref[at(4 * i + k), T_ROWS:, :] = first


def add_blocks(ref, low, high):
    total = ref[0, low:high, :].astype(f32)
    for j in range(1, BLOCKS):
        total = total + ref[j, low:high, :].astype(f32)
    return total


def inverse_rms(moments, width):
    return lax.rsqrt(moments[CLASSES : CLASSES + 1, :] / width + epsilon)


def sixteen():
    square = (PAD, PAD)
    return lax.broadcasted_iota(jnp.int32, square, 0) == lax.broadcasted_iota(jnp.int32, square, 1)


def sum_kernel(width, in_ref, t_ref, m_ref, logit_ref):
    logits = jnp.zeros((PAD, 1), f32)
    first = add_blocks(in_ref, T_ROWS, T_ROWS + M_ROWS)
    for h in range(HEADS):
        low = REFS + h * PAD
        block = add_blocks(in_ref, low, low + PAD)
        t_ref[low : low + PAD, :] = block.astype(bf16)
        kind = lax.broadcasted_iota(jnp.int32, block.shape, 0)
        head = first if h == 0 else pltpu.roll(first, 8, 0)
        moments = jnp.where(kind < 8, head, jnp.where(kind <= CLASSES, pltpu.roll(block, PAD - MOVE, 0), 0.0))
        m_ref[h * PAD : (h + 1) * PAD, :] = moments
        part = jnp.sum(inverse_rms(moments, width) * moments, axis=1, keepdims=True)
        logits = logits + part / P_SIZE
    row = jnp.sum(jnp.where(sixteen(), logits, 0.0), axis=0, keepdims=True)
    logit_ref[...] = jnp.broadcast_to(row, logit_ref.shape)
    for low in range(0, REFS, 64):
        t_ref[low : low + 64, :] = add_blocks(in_ref, low, low + 64).astype(bf16)


def row_kernel(t_ref, logit_ref, out_ref):
    logits = logit_ref[...]
    high = logits.astype(bf16).astype(f32)
    low = REFS + PAD
    kind = lax.broadcasted_iota(jnp.int32, logits.shape, 0)
    block = t_ref[REFS:low, :PAD].astype(f32)
    block = jnp.where(kind == CLASSES, high, jnp.where(kind == CLASSES + 1, logits - high, block)).astype(bf16)
    for j in range(BLOCKS):
        out_ref[j] = t_ref[...]
        out_ref[j, REFS:low, :PAD] = block


def sum_logits(ref):
    section = 2 * lax.axis_index("z") + lax.axis_index("core")
    total = jnp.zeros((PAD, PAD), f32)
    for other in range(BLOCKS):
        total = total + ref[at(lax.rem(other + BLOCKS - section, BLOCKS)), REFS : REFS + PAD, :PAD].astype(f32)
    return total[CLASSES : CLASSES + 1] + total[CLASSES + 1 : CLASSES + 2]


def scales_of(grads, moments, width):
    inverse = inverse_rms(moments, width)
    dual = inverse * jnp.sum(grads * moments, axis=0, keepdims=True) / (float(P_SIZE) * width)
    return to_column(inverse), to_column(inverse * dual)


def backward_kernel(
    width, score_scale,
    q_ref, t_ref, rs_ref, rt_ref, col_ref, m_ref, label_ref,
    logit_ref, grads_ref, gs_ref, gt_ref, grs_ref, u_ref,
):
    rows = q_ref.shape[2]
    base = q_ref.shape[1] - REFS
    size = float(P_SIZE)
    logits = sum_logits(t_ref)
    logit_ref[...] = logits
    logits = jnp.sum(jnp.where(sixteen(), logits, 0.0), axis=1, keepdims=True)
    logits = jnp.broadcast_to(logits, (PAD, P_SIZE))
    kind = lax.broadcasted_iota(jnp.int32, logits.shape, 0)
    exps = jnp.where(kind < CLASSES, jnp.exp(logits), 0.0)
    probs = exps / jnp.sum(exps, axis=0, keepdims=True)
    grads = loss_scale * (probs - (kind == label_ref[0]).astype(f32))
    grads = jnp.where(kind < CLASSES, grads, 0.0)
    grads_ref[...] = grads
    for h in range(HEADS):
        here = slice(h * P_SIZE, (h + 1) * P_SIZE)
        inverse, pull = scales_of(grads, m_ref[h * PAD : (h + 1) * PAD, :], width)
        first = jnp.broadcast_to(size * inverse, (P_SIZE, rows))
        second = first * pull

        def load(s):
            return q_ref[at(s), base + h * P_SIZE : base + (h + 1) * P_SIZE, :].astype(f32)

        def grad_plan(s, u):
            return first * u - second * t_ref[at(s), here, :].astype(f32)

        def row(ref, t, s):
            place = (t * HEADS + h) * BLOCKS + s
            return ref[place : place + 1, :]

        def put(ref, t, s, value):
            place = (t * HEADS + h) * BLOCKS + s
            ref[place : place + 1, :] = value

        acc = jnp.zeros((P_SIZE, rows), f32)
        for s in range(BLOCKS):
            v = t_ref[at(s), REFS + h * PAD : REFS + (h + 1) * PAD, :].astype(f32)
            u = jnp.sum(grads * v, axis=0, keepdims=True) / size
            put(u_ref, 0, s, u)
            weighted = grad_plan(s, u) * load(s)
            put(grs_ref, ITERS - 1, s, jnp.sum(weighted * col_ref[ITERS - 1, here, :], axis=0, keepdims=True))
            acc = acc + weighted * row(rs_ref, ITERS - 1, s)
        for t in reversed(range(ITERS)):
            grad_col = jnp.sum(acc, axis=1, keepdims=True)
            gt_ref[t] = -size * col_ref[t, here, :] ** 2 * grad_col
            acc = jnp.zeros((P_SIZE, rows), f32)
            for s in range(BLOCKS):
                k = load(s)
                grad_row = jnp.sum(k * gt_ref[t], axis=0, keepdims=True)
                if t == ITERS - 1:
                    grad_row = grad_row + row(grs_ref, t, s)
                grad_rowsum = -grad_row * row(rs_ref, t, s) / row(rt_ref, t, s)
                put(grs_ref, t, s, grad_rowsum)
                if t > 0:
                    acc = acc + k * grad_rowsum
        gain = score_scale * col_ref[ITERS - 1, here, :] * first
        loss = score_scale * col_ref[ITERS - 1, here, :] * second
        for t in range(ITERS):
            gt_ref[t] = score_scale * gt_ref[t]
        for s in range(BLOCKS):
            inner = gain * row(u_ref, 0, s) - loss * t_ref[at(s), here, :].astype(f32) + gt_ref[ITERS - 1]
            total = row(rs_ref, ITERS - 1, s) * inner
            for t in range(ITERS - 1):
                total = total + row(rs_ref, t, s) * gt_ref[t]
                total = total + (score_scale * row(grs_ref, t + 1, s)) * col_ref[t, here, :]
            total = total + score_scale * row(grs_ref, 0, s)
            value = (total * load(s)).astype(bf16)
            gs_ref[here, s * rows : (s + 1) * rows] = value


def put_products(core, gs_ref, plan_ref, left_ref, right_ref, wide_ref):
    z = lax.axis_index("z")
    place = lax.axis_index("y") * SIDE + lax.axis_index("x")
    rows = right_ref.shape[1] // DEPTH
    for k in range(4):
        for b in range(2):
            step = jnp.where(core == 0, CHIPS[0][k], CHIPS[1][k]) + 4 * b
            block = lax.bitwise_xor(2 * lax.rem(z + step, DEPTH) + core, place)
            here = slice((2 * k + b) * rows, (2 * k + b + 1) * rows)
            right_ref[:REFS, here] = gs_ref[:, lanes(block, rows)]
            right_ref[REFS:, here] = plan_ref[:, lanes(block, rows)]
    wide_ref[...] = lax.dot_general(left_ref[...], right_ref[...], TN, preferred_element_type=f32).astype(bf16)


def away_kernel(width, gs_ref, grads_ref, m_ref, wt_ref, raw_ref, plan_ref, refs_ref, other_ref, left_ref, right_ref, wide_ref):
    rows = other_ref.shape[2]
    part = raw_ref.shape[1]
    size = float(P_SIZE)
    grads = grads_ref[...]
    place = lax.axis_index("y") * SIDE + lax.axis_index("x")
    pair = refs_ref[:, pl.ds(pl.multiple_of((place // 2) * (2 * part), 2 * part), 2 * part)]
    left_ref[:REFS, :] = jnp.where(lax.rem(place, 2) == 0, pair[:, :part], pair[:, part:])
    for h in range(HEADS):
        here = slice(h * P_SIZE, (h + 1) * P_SIZE)
        inverse, pull = scales_of(grads, m_ref[h * PAD : (h + 1) * PAD, :], width)
        normed = jnp.sum(grads[:, :1] * wt_ref[h * PAD : (h + 1) * PAD, :].astype(f32), axis=0, keepdims=True) / size
        grad_raw = (inverse * (normed - raw_ref[here, :] * pull)).astype(bf16)
        left_ref[REFS + h * P_SIZE : REFS + (h + 1) * P_SIZE, :] = (size * grad_raw.astype(f32)).astype(bf16)
    put_products(1 - lax.axis_index("core"), gs_ref, plan_ref, left_ref, right_ref, wide_ref)
    for k in range(DEPTH):
        other_ref[k] = wide_ref[:, k * rows : (k + 1) * rows]


def mine_kernel(gs_ref, plan_ref, left_ref, p0, p1, p2, p3, right_ref, wide_ref):
    rows = p0.shape[2]
    put_products(lax.axis_index("core"), gs_ref, plan_ref, left_ref, right_ref, wide_ref)
    for k, out in enumerate((p0, p1, p2, p3)):
        for b in range(2):
            out[b] = wide_ref[:, (2 * k + b) * rows : (2 * k + b + 1) * rows]


def cores_kernel(p0, p1, p2, p3, other_ref, o0, o1, o2, o3):
    for k, (part, out) in enumerate(zip((p0, p1, p2, p3), (o0, o1, o2, o3))):
        for b in range(2):
            out[b] = (part[b].astype(f32) + other_ref[2 * k + b].astype(f32)).astype(bf16)


def chips_kernel(o0, o1, o2, o3, u0, u1):
    for b, out in enumerate((u0, u1)):
        total = o0[b].astype(f32) + o1[b].astype(f32) + o2[b].astype(f32) + o3[b].astype(f32)
        out[...] = total.astype(bf16)


def last_kernel(u0, u1, out_ref):
    out_ref[...] = u0[...].astype(f32) + u1[...].astype(f32)


def references_kernel(gs_ref, mixed_ref, other_ref, out_ref, fc_ref):
    put_columns(mixed_ref, other_ref, fc_ref)
    for h in range(HEADS):
        heads = gs_ref[h * P_SIZE : (h + 1) * P_SIZE, :]
        out_ref[h] = lax.dot_general(fc_ref[...], heads, NT, preferred_element_type=f32)


def along_z(value, k):
    pairs = []
    for z in range(DEPTH):
        for core in range(2):
            pairs.append((2 * z + core, 2 * ((z + CHIPS[core][k]) % DEPTH) + core))
    return lax.ppermute(value, ("z", "core"), pairs)


def to_place(value, b):
    pairs = []
    for z in range(DEPTH):
        for core in range(2):
            for j in range(BLOCKS):
                block = (2 * ((z + 4 * b) % DEPTH) + core) ^ j
                pairs.append(((2 * z + core) * BLOCKS + j, j * BLOCKS + block))
    return lax.ppermute(value, ("z", "core", "y", "x"), pairs)


def spread_logits(value):
    pairs = [((s + j) % BLOCKS * BLOCKS + j, s * BLOCKS + j) for s in range(BLOCKS) for j in range(BLOCKS)]
    return lax.ppermute(value, ("z", "core", "y", "x"), pairs)


def local(features, references, classifier, lengths, labels):
    batch, rows, width = features.shape
    part = width // BLOCKS
    everything = BLOCKS * rows
    score_scale = temper / math.sqrt(width)
    feats = features.reshape(rows, width)
    refs = references.reshape(REFS, width)
    kind = jax.ShapeDtypeStruct

    half = part // 2
    halves = kind((BLOCKS, half, rows), bf16)
    split = call(split_kernel, "split", halves, 1, scratch=[pltpu.VMEM((width, rows), bf16)], flops=3 * 10**9)(feats)
    mixed = call(
        functools.partial(scores_kernel, score_scale), "scores", kind((BLOCKS, half + REFS, rows), bf16), 3
    )(feats, refs, split)
    mixed = exchange(mixed)
    other = lax.ppermute(call(peel_kernel, "peel", halves, 1)(mixed), "core", [(0, 1), (1, 0)])
    weights = jnp.pad(jnp.transpose(classifier, (0, 2, 1)), ((0, 0), (0, PAD - CLASSES), (0, 0)))
    weights = weights.reshape(HEADS * PAD, part)


    scales = kind((ITERS * HEADS * BLOCKS, rows), f32)
    rs, rt, col, plan = call(
        sinkhorn_kernel, "sinkhorn",
        [scales, scales, kind((ITERS, REFS, rows), f32), kind((REFS, everything), bf16)], [VMEM, SMEM, SMEM],
    )(mixed, lengths, labels)
    products, raw = call(
        forward_kernel, "forward",
        [kind((BLOCKS, T_ROWS + M_ROWS, rows), bf16), kind((REFS, part), f32)], 4,
        scratch=[pltpu.VMEM((part, everything), bf16), pltpu.VMEM((T_ROWS, part), bf16)],
    )(mixed, other, weights, plan)
    t, moments, logit_part = call(
        functools.partial(sum_kernel, width), "sum",
        [kind((T_ROWS, rows), bf16), kind((HEADS * PAD, P_SIZE), f32), kind((PAD, PAD), f32)], 1,
    )(exchange(products))
    ts = exchange(
        call(row_kernel, "row", kind((BLOCKS, T_ROWS, rows), bf16), 2)(t, spread_logits(logit_part))
    )
    pair = kind((2, part, rows), bf16)
    logits, grads, grad_scores = call(
        functools.partial(backward_kernel, width, score_scale), "backward",
        [kind((1, PAD), f32), kind((PAD, P_SIZE), f32), kind((REFS, everything), bf16)],
        [VMEM] * 6 + [SMEM],
        scratch=[
            pltpu.VMEM((ITERS, P_SIZE, rows), f32),
            pltpu.VMEM((ITERS * HEADS * BLOCKS, rows), f32),
            pltpu.VMEM((HEADS * BLOCKS, rows), f32),
        ],
    )(mixed, ts, rs, rt, col, moments, labels)
    products_scratch = [pltpu.VMEM((2 * REFS, DEPTH * rows), bf16), pltpu.VMEM((part, DEPTH * rows), bf16)]
    away, left = call(
        functools.partial(away_kernel, width), "away", [kind((DEPTH, part, rows), bf16), kind((2 * REFS, part), bf16)], 7,
        scratch=products_scratch,
    )(grad_scores, grads, moments, weights, raw, plan, refs)
    away = lax.ppermute(away, "core", [(0, 1), (1, 0)])
    mine = call(mine_kernel, "mine", [pair] * 4, 3, scratch=products_scratch, flops=10**9)(grad_scores, plan, left)
    o = call(cores_kernel, "cores", [pair] * 4, 5)(*mine, away)
    o = [o[0]] + [along_z(o[k], k) for k in (1, 2, 3)]
    u = call(chips_kernel, "chips", [kind((part, rows), bf16)] * 2, 4)(*o)
    u = [to_place(u[b], b) for b in range(2)]
    grad_features = call(last_kernel, "last", kind((part, rows), f32), 2)(*u)
    grad_references = call(
        references_kernel, "references", kind((HEADS, part, rows), f32), 3,
        scratch=[pltpu.VMEM((part, everything), bf16)], flops=2 * REFS * part * everything,
    )(grad_scores, mixed, other)
    return (
        logits[:, :CLASSES],
        jnp.transpose(grad_features).reshape(batch, rows, part),
        jnp.transpose(grad_references, (0, 2, 1)),
    )


def solution(mesh):
    grid = Mesh(mesh.devices.reshape(DEPTH, 2, SIDE, SIDE), ("z", "core", "y", "x"))
    section, seq = ("z", "core"), ("y", "x")
    in_specs = (P(None, seq, None), P(section, None, None), P(section, seq, None), P(), P())
    out_specs = (P(), P(None, seq, section), P(section, None, seq))
    return jax.shard_map(local, mesh=grid, in_specs=in_specs, out_specs=out_specs, check_vma=False)
```
